512 devices in a mesh: fsdp: 32 (over x, y, core), tensor: 16 (over z).
Axes of the slice: x: 4, y: 4, z: 16, core: 2. Of those that a mesh axis runs over, the one named last changes fastest.
Arguments:
- momentum: bfloat16 [10, 2, 4096, 1536], P(None, None, 'fsdp', 'tensor'), may hold values from -6 to 6
- gradient: bfloat16 [10, 2, 4096, 1536], P(None, None, 'fsdp', 'tensor'), may hold values from -4.2 to 4.2
- right_in: bfloat16 [10, 2, 1536, 128], P(None, None, 'tensor'), may hold values from -6 to 6
- owners: int32 [10], replicated, may hold values from 0 to 15, as said below
Outputs:
- state_out: bfloat16 [32, 2, 4096, 1536], P('tensor', None, 'fsdp')
- left_out: float32 [32, 2, 4096, 128], P('tensor', None, 'fsdp')
- right_out: float32 [10, 2, 1536, 128], P(None, None, 'tensor')
The draws below stay inside these ranges and needn't reach their ends.
Inputs may be any that keep to these rules, and one draw needn't show every extreme that they name: `owners`: each entry is a tensor index. No tensor index takes more than 2 experts, and some index takes exactly 2.
All inputs are finite; a program needn't handle non-finite values.
Results may differ from the reference program's by a relative error of at most 0.0072.
Values may be sent and summed in bfloat16 or wider, within the bound.
No kernel may reach another device: no remote copies, remote signals or barrier semaphores. Data moves between devices by JAX's collectives and lax.ppermute only.
A program may use at most 64 MiB of HBM per device.

```python
import math
import jax
import jax.numpy as jnp
from jax import lax

D = 4096
HID = 1536
RANK = 128
KINDS = 2
CAP = 2
EXPERTS = 10
SLOTS = 32


def draw_owners(key, part):
    key = jax.random.fold_in(key, 5)
    first, second, third = jax.random.split(key, 3)
    groups = SLOTS // CAP
    order = jax.random.permutation(first, SLOTS)
    rank_of = order // CAP
    upper_end = jax.random.randint(second, (), 0, 2)
    full_rank = upper_end * (groups - 1)
    other_rank = groups - 1 - full_rank
    level = jnp.where(rank_of == full_rank, 0, jnp.where(order == other_rank * CAP, 1, 2))
    score = level * SLOTS + jnp.arange(SLOTS)
    picked = order[jnp.argsort(score, stable=True)][:EXPERTS]
    chosen = (picked // CAP).astype(jnp.int32)
    return jax.random.permutation(third, chosen).astype(jnp.int32)


def mixed_field(left_part, right_part, noise_part, scale, limit):
    inner = left_part.shape[-1]
    product = jnp.einsum('ekdl,eklh->ekdh', left_part, right_part, precision=lax.Precision.HIGHEST)
    product = product / math.sqrt(inner)
    value = math.sqrt(0.85) * product + math.sqrt(0.15) * noise_part
    value = jnp.clip(value, -limit, limit) * scale
    return value.astype(jnp.bfloat16)


def draw_momentum(key, part):
    key = jax.random.fold_in(key, 11)
    first, second, third = jax.random.split(key, 3)
    inner = max(RANK // 4, 1)
    left_part = jax.random.normal(first, (EXPERTS, KINDS, D, inner), jnp.float32)
    right_part = jax.random.normal(second, (EXPERTS, KINDS, inner, HID), jnp.float32)
    noise_part = jax.random.normal(third, (EXPERTS, KINDS, D, HID), jnp.float32)
    return mixed_field(left_part, right_part, noise_part, 1.0, 6.0)


def draw_gradient(key, part):
    key = jax.random.fold_in(key, 17)
    first, second, third = jax.random.split(key, 3)
    inner = max(RANK // 4, 1)
    left_part = jax.random.normal(first, (EXPERTS, KINDS, D, inner), jnp.float32)
    right_part = jax.random.normal(second, (EXPERTS, KINDS, inner, HID), jnp.float32)
    noise_part = jax.random.normal(third, (EXPERTS, KINDS, D, HID), jnp.float32)
    return mixed_field(left_part, right_part, noise_part, 0.7, 6.0)


def level_of(rng, dims, pieces, smallest, high):
    gain = 1.0
    for dim, parts in pieces:
        steps = jax.random.uniform(jax.random.fold_in(jax.random.fold_in(rng, 6), dim), (parts,), jnp.float32, smallest / len(pieces), high / len(pieces))
        gain = gain * jnp.repeat(jnp.exp(steps), dims[dim] // parts).reshape((-1,) + (1,) * (len(dims) - 1 - dim))
    return gain


def normal_values(rng, shape, deviation, most, cuts=(), kind=jnp.bfloat16):
    entries = deviation * jax.random.normal(rng, shape, jnp.float32)
    if cuts:
        entries = entries * level_of(rng, shape, cuts, -0.22, 0.18)
    return jnp.clip(entries, -most, most).astype(kind)


def setup_inputs(seed: int = 0) -> dict:
    seeds = jax.random.split(jax.random.key(seed), 5)
    return {
        "momentum": draw_momentum(jax.random.fold_in(seeds[4], 71), 0),
        "gradient": draw_gradient(jax.random.fold_in(seeds[4], 71), 0),
        "right_in": normal_values(seeds[2], (EXPERTS, KINDS, HID, RANK), 1.0, 6.0, ((2, 16),)),
        "owners": draw_owners(jax.random.fold_in(seeds[4], 71), 0),
    }


ridge_term = 0.001
feedback = 0.1
epsilon = 1e-06

def orthonormal(panel, gram_total):
    eye_matrix = jnp.eye(gram_total.shape[-1], dtype=jnp.float32)
    lower_factor = jnp.linalg.cholesky(gram_total + ridge_term * eye_matrix)
    solved = jax.scipy.linalg.solve_triangular(lower_factor, jnp.swapaxes(panel, -1, -2), lower=True)
    return jnp.swapaxes(solved, -1, -2)

def reference(momentum, gradient, right_in, owners):
    highest = lax.Precision.HIGHEST
    summed = (momentum.astype(jnp.float32) + gradient.astype(jnp.float32)).astype(jnp.bfloat16)
    summed_wide = summed.astype(jnp.float32)
    panel = jnp.einsum('emrk,emkq->emrq', summed_wide, right_in.astype(jnp.float32), precision=highest)
    gram_total = jnp.einsum('emrq,emrs->emqs', panel, panel, precision=highest)
    ortho = orthonormal(panel, gram_total)
    ortho_low = ortho.astype(jnp.bfloat16).astype(jnp.float32)
    factor = jnp.einsum('emrk,emrq->emkq', summed_wide, ortho_low, precision=highest)
    mean_square = lax.optimization_barrier(jnp.mean(factor * factor, axis=2))
    right_out = factor * lax.rsqrt(mean_square + epsilon)[:, :, None, :]
    corrected = summed_wide - feedback * jnp.einsum('emrq,emkq->emrk', ortho, factor, precision=highest)
    fresh = corrected.astype(jnp.bfloat16)
    index_line = jnp.arange(EXPERTS, dtype=jnp.int32)
    same_owner = owners[:, None] == owners[None, :]
    earlier = index_line[None, :] < index_line[:, None]
    position = lax.optimization_barrier(jnp.sum((same_owner & earlier).astype(jnp.int32), axis=1)).astype(jnp.int32)
    slot = (owners * CAP + position).astype(jnp.int32)
    state_out = jnp.zeros((SLOTS, KINDS, D, HID), jnp.bfloat16).at[slot].set(fresh)
    left_out = jnp.zeros((SLOTS, KINDS, D, RANK), jnp.float32).at[slot].set(ortho * math.sqrt(D))
    return (state_out, left_out, right_out)
```

```python
import functools
import math

import jax
import jax.numpy as jnp
from jax import lax
from jax.experimental import pallas as pl
from jax.experimental.pallas import tpu as pltpu
from jax.sharding import Mesh
from jax.sharding import PartitionSpec as P

D = 4096
HID = 1536
CAP = 2
EXPERTS = 10
GROUPS = 16
BLOCK = 96
RANK = 128

ridge_term = 0.001
feedback = 0.1
epsilon = 1e-06

F32 = jnp.float32
BF16 = jnp.bfloat16
HIGHEST = lax.Precision.HIGHEST
XY = ("x", "y")
FSDP = ("x", "y", "c")
SWAP = [(0, 1), (1, 0)]
VMEM = pl.BlockSpec(memory_space=pltpu.VMEM)
SMEM = pl.BlockSpec(memory_space=pltpu.SMEM)


def call(body, outs, scratch=(), flops=0, specs=None, n_in=0):
    return pl.pallas_call(
        body,
        out_shape=outs,
        in_specs=specs if specs is not None else [VMEM] * n_in,
        out_specs=jax.tree.map(lambda _: VMEM, outs),
        scratch_shapes=list(scratch),
        compiler_params=pltpu.CompilerParams(vmem_limit_bytes=48 * 1024 * 1024),
        cost_estimate=pl.CostEstimate(flops=flops, bytes_accessed=4_000_000, transcendentals=0),
    )


def dot(a, b, contract=((1,), (0,)), precision=None):
    return lax.dot_general(
        a, b, (contract, ((), ())), precision=precision, preferred_element_type=F32
    )


def iota(shape, dim):
    return lax.broadcasted_iota(jnp.int32, shape, dim)


def fill_table(own, table, count):
    for g in range(GROUPS):
        count[g] = 0
    for s in range(GROUPS * CAP):
        table[s] = EXPERTS
    for e in range(EXPERTS):
        g = own[e]
        p = count[g]
        count[g] = p + 1
        table[g * CAP + p] = e


def tile_row(position):
    t = position & 7
    return jnp.where(t >= 3, t - 3 + BLOCK, t)


def slice_right(own, place, right, out, table, count, held):
    fill_table(own, table, count)
    f = place[0] * 8 + place[1] * 2 + place[2]
    t = iota((8, 192), 0)
    pick = ((iota((8, 192), 1) == tile_row(t) + 3 * f) & (t < 6)).astype(BF16)
    for e in range(EXPERTS):
        held[e] = dot(pick, right[e].reshape(192, RANK))
    held[EXPERTS] = jnp.zeros((8, RANK), F32)

    def group(g, _):
        pair = jnp.concatenate([held[table[g * CAP]], held[table[g * CAP + 1]]], axis=0)
        out[g] = pair.astype(BF16)
        return 0

    lax.fori_loop(0, GROUPS, group, 0)


def place_state(own, momentum, gradient, out, table, count):
    fill_table(own, table, count)

    def slot(s, _):
        e = table[s]

        @pl.when(e < EXPERTS)
        def _():
            total = momentum[e].astype(F32) + gradient[e].astype(F32)
            out[s] = total.astype(BF16).reshape(192, 128)

        @pl.when(e >= EXPERTS)
        def _():
            out[s] = jnp.zeros((192, 128), BF16)

        return 0

    lax.fori_loop(0, GROUPS * CAP, slot, 0)


def offset(i):
    return jnp.where(i == 1, 3, jnp.where(i == 2, 1, jnp.where(i == 3, 2, 0)))


def unpermute_matrix(place, core):
    col = iota((384, 256), 1)
    chip = col >> 4
    x = (place[0] + offset(chip & 3)) & 3
    y = (place[1] + offset(chip >> 2)) & 3
    f = x * 8 + y * 2 + core
    target = ((col >> 3) & 1) * 192 + tile_row(col) + 3 * f
    return ((iota((384, 256), 0) == target) & ((col & 7) < 6)).astype(BF16)


def join_right(place, near, far, out, matrix):
    c = place[2]
    matrix[:, :256] = unpermute_matrix(place, c)
    matrix[:, 256:] = unpermute_matrix(place, 1 - c)

    def block(z, _):
        a = near[:, z].reshape(256, RANK)
        b = far[:, z].reshape(256, RANK)
        both = jnp.concatenate([a, b], axis=0)
        out[z] = dot(matrix[...], both).astype(BF16)
        return 0

    lax.fori_loop(0, GROUPS, block, 0)


def split3(value):
    high = value.astype(BF16)
    rest = value - high.astype(F32)
    middle = rest.astype(BF16)
    low = (rest - middle.astype(F32)).astype(BF16)
    return high, middle, low


def permute_matrix(place, kind):
    row = iota((256, BLOCK), 0)
    f = ((row >> 3) & 15) * 2 + ((row >> 7) ^ place[2])
    t = row & 7
    j = t - 3 * kind
    return ((iota((256, BLOCK), 1) == 3 * f + j) & (j >= 0) & (j < 3)).astype(BF16)


def panels(state, right, panel, gram):
    for i in range(2 * CAP):
        rows = pl.ds(i * BLOCK, BLOCK)

        def block(z, total):
            return total + dot(state[z, rows, :], right[z, rows, :], ((0,), (0,)))

        value = lax.fori_loop(0, GROUPS, block, jnp.zeros((128, RANK), F32), unroll=4)
        panel[i] = value
        gram[i] = dot(value, value, ((0,), (0,)), HIGHEST)


def weigh(place, state, panel, keep, send):
    order = [permute_matrix(place, k) for k in range(2)]
    for s in range(CAP):
        parts = [split3(panel[2 * s + k]) for k in range(2)]
        stacked = [jnp.concatenate([parts[0][i], parts[1][i]], axis=0) for i in range(3)]

        def block(z, _):
            moved = [
                dot(order[k], state[z, pl.ds((2 * s + k) * BLOCK, BLOCK), :]).astype(BF16)
                for k in range(2)
            ]
            wide = jnp.concatenate(moved, axis=1)
            value = dot(wide, stacked[0]) + (dot(wide, stacked[1]) + dot(wide, stacked[2]))
            rows = pl.ds(s * 8, 8)
            keep[:, z, rows, :] = value[:128].reshape(16, 8, RANK)
            send[:, z, rows, :] = value[128:].reshape(16, 8, RANK)
            return 0

        lax.fori_loop(0, GROUPS, block, 0)


def invert(gram, out, work, *, count, size):
    n = RANK
    eye = (iota((n, n), 0) == iota((n, n), 1)).astype(F32)
    for m in range(count):
        work[m, :, :n] = gram[m] + ridge_term * eye
        work[m, :, n:] = eye
    row = iota((size, 2 * n), 0)
    lane = iota((size, n), 1)
    for k in range(0, n, size):
        blocks = [work[m, k : k + size, :] for m in range(count)]
        for i in range(size):
            for m in range(count):
                b = blocks[m]
                scale = lax.rsqrt(b[i : i + 1, k + i : k + i + 1])
                line = b[i : i + 1, :] * scale
                column = jnp.where(row > i, b[:, k + i : k + i + 1] * scale, 0.0)
                blocks[m] = jnp.where(row == i, line, b - column * line)
        for m in range(count):
            b = blocks[m]
            out[m, k : k + size, :] = b[:, n:]
            if k + size < n:
                left = jnp.where(lane >= k + size, b[:, :n], 0.0)
                change = dot(left, b, ((0,), (0,)), HIGHEST)
                work[m, k + size :, :] -= change[k + size :, :]


def scale_factor(parts, inverse, out):
    total = parts[0]
    for i in range(1, 16):
        total = total + parts[i]
    rows = GROUPS * 8
    t = iota((rows, RANK), 0) & 7
    tiles = []
    for s in range(CAP):
        w = total[:, s * 8 : (s + 1) * 8, :].reshape(rows, RANK)
        both = [dot(w, inverse[2 * s + k], ((1,), (1,)), HIGHEST) for k in range(2)]
        value = jnp.where(t < 3, both[0], both[1])
        square = value * value
        sums = [
            jnp.sum(jnp.where((t >= 3 * k) & (t < 3 * k + 3), square, 0.0), axis=0, keepdims=True)
            for k in range(2)
        ]
        value = jnp.where(t == 6, sums[0], jnp.where(t == 7, sums[1], value))
        tiles.append(value.reshape(GROUPS, 8, RANK))
    out[...] = jnp.concatenate(tiles, axis=1).astype(BF16)


def orthonormal(panel, inverse, left, low):
    for i in range(2 * CAP):
        ortho = dot(panel[i], inverse[i], ((1,), (1,)), HIGHEST)
        left[i] = ortho * math.sqrt(D)
        low[i] = (ortho * (-feedback)).astype(BF16)


def select(own, tiles, out, table, count, held, packed):
    fill_table(own, table, count)
    for g in range(GROUPS):
        value = tiles[g].astype(F32)
        for s in range(CAP):
            held[table[g * CAP + s]] = value[s * 8 : (s + 1) * 8]
    for e in range(0, EXPERTS, 2):
        packed[e * 8 : e * 8 + 16, :] = jnp.concatenate([held[e], held[e + 1]], axis=0).astype(BF16)
    value = packed[...]
    for i in range(16):
        out[i] = value


def finish_right(place, near, far, out):
    col = iota((392, 256), 1)
    row = iota((392, 256), 0)
    t = col & 7
    s = (col >> 3) & 1
    matrices = []
    for core in (place[2], 1 - place[2]):
        f = (col >> 4) * 2 + core
        target = jnp.where(t < 6, s * 192 + tile_row(col) + 3 * f, 384 + s * 2 + (t - 6))
        matrices.append((row == target).astype(BF16))
    both = jnp.concatenate(matrices, axis=1)
    for g in range(EXPERTS // 2):
        rows = slice(g * 16, (g + 1) * 16)
        data = jnp.concatenate(
            [near[:, rows, :].reshape(256, RANK), far[:, rows, :].reshape(256, RANK)], axis=0
        )
        value = dot(both, data)
        for s in range(2):
            for k in range(2):
                i = 2 * s + k
                scale = lax.rsqrt(value[384 + i : 385 + i, :] * (1.0 / HID) + epsilon)
                out[2 * g + s, k] = value[i * BLOCK : (i + 1) * BLOCK, :] * scale


def finish_state(place, state, near, far, low, out, matrix, wide):
    c = place[2]
    matrix[:, :256] = unpermute_matrix(place, c)
    matrix[:, 256:] = unpermute_matrix(place, 1 - c)

    def block(z, _):
        both = jnp.concatenate(
            [near[:, z].reshape(256, RANK), far[:, z].reshape(256, RANK)], axis=0
        )
        value = dot(matrix[...], both).astype(BF16)
        rows = pl.ds(pl.multiple_of(z * BLOCK, BLOCK), BLOCK)
        for i in range(2 * CAP):
            wide[i, rows, :128] = state[z, i * BLOCK : (i + 1) * BLOCK, :]
            wide[i, rows, 128:] = value[i * BLOCK : (i + 1) * BLOCK, :]
        return 0

    lax.fori_loop(0, GROUPS, block, 0)
    eye = (iota((128, 128), 0) == iota((128, 128), 1)).astype(BF16)
    for i in range(2 * CAP):
        lhs = jnp.concatenate([eye, low[i]], axis=1)
        out[i] = dot(lhs, wide[i], ((1,), (1,))).astype(BF16)


def gather_slices(x):
    ring = lambda shift: [(i, (i + shift) % 4) for i in range(4)]
    for axis in ("x", "y"):
        x = jnp.stack([x] + [lax.ppermute(x, axis, ring(d)) for d in (1, 3, 2)])
    x = x.reshape((16,) + x.shape[2:])
    return x, lax.ppermute(x, "c", SWAP)


def exchange(x, axis):
    return lax.all_to_all(x, axis, split_axis=0, concat_axis=0, tiled=True)


def shards(momentum, gradient, right_in, owners):
    sds = jax.ShapeDtypeStruct
    place = jnp.stack([lax.axis_index("x"), lax.axis_index("y"), lax.axis_index("c")]).astype(
        jnp.int32
    )
    tables = [pltpu.SMEM((GROUPS * CAP,), jnp.int32), pltpu.SMEM((GROUPS,), jnp.int32)]
    n = 2 * CAP
    slices = call(
        slice_right,
        sds((16, 16, RANK), BF16),
        tables + [pltpu.VMEM((EXPERTS + 1, 8, RANK), F32)],
        specs=[SMEM, SMEM, VMEM],
    )(owners, place, right_in)
    slices = exchange(slices, "z")
    sent = call(
        place_state, sds((32, 192, 128), BF16), tables, specs=[SMEM, VMEM, VMEM]
    )(owners, jnp.swapaxes(momentum, 2, 3), jnp.swapaxes(gradient, 2, 3))
    sent, slices = lax.optimization_barrier((sent, slices))
    state = exchange(sent.reshape(16, 384, 128), "z")
    near, far = gather_slices(slices)
    matrix = pltpu.VMEM((384, 512), BF16)
    right = call(
        join_right, sds((16, 384, RANK), BF16), [matrix], flops=800_000_000, specs=[SMEM, VMEM, VMEM]
    )(place, near, far)
    panel, gram = call(
        panels, (sds((n, 128, RANK), F32), sds((n, RANK, RANK), F32)), n_in=2, flops=500_000_000
    )(state, right)
    gram = exchange(gram.reshape(32, 4 * n, RANK), FSDP)
    gram = jnp.broadcast_to(jnp.sum(gram, axis=0)[None], gram.shape)
    gram = exchange(gram, FSDP).reshape(n, RANK, RANK)
    half = sds((16, 16, 16, RANK), F32)
    keep, send = call(weigh, (half, half), specs=[SMEM, VMEM, VMEM], flops=2_000_000_000)(
        place, state, panel
    )
    parts = keep + lax.ppermute(send, "c", SWAP)
    parts = exchange(parts.reshape(16, 256, RANK), XY).reshape(16, 16, 16, RANK)
    inverse = call(
        functools.partial(invert, count=n, size=8),
        sds((n, RANK, RANK), F32),
        [pltpu.VMEM((n, RANK, 2 * RANK), F32)],
        n_in=1,
        flops=8_000_000_000,
    )(gram)
    tiles = call(scale_factor, sds((16, 16, RANK), BF16), n_in=2, flops=100_000_000)(parts, inverse)
    left, low = call(
        orthonormal,
        (sds((n, 128, RANK), F32), sds((n, 128, RANK), BF16)),
        n_in=2,
        flops=100_000_000,
    )(panel, inverse)
    back = exchange(tiles, "z")
    near, far = gather_slices(tiles)
    chosen = call(
        select,
        sds((16, 80, RANK), BF16),
        tables + [pltpu.VMEM((EXPERTS + 1, 8, RANK), F32), pltpu.VMEM((80, RANK), BF16)],
        specs=[SMEM, VMEM],
    )(owners, back)
    chosen = exchange(chosen, XY)
    other = lax.ppermute(chosen, "c", SWAP)
    right_out = call(
        finish_right, sds((EXPERTS, 2, BLOCK, RANK), F32), specs=[SMEM, VMEM, VMEM], flops=300_000_000
    )(place, chosen, other)
    state_out = call(
        finish_state,
        sds((n, 128, HID), BF16),
        [matrix, pltpu.VMEM((n, HID, 256), BF16)],
        specs=[SMEM, VMEM, VMEM, VMEM, VMEM],
        flops=1_200_000_000,
    )(place, state, near, far, low)
    return (
        state_out.reshape(CAP, 2, 128, HID),
        left.reshape(CAP, 2, 128, RANK),
        right_out,
    )


def solution(mesh):
    fine = Mesh(mesh.devices.reshape(4, 4, 2, 16), ("x", "y", "c", "z"))
    return jax.shard_map(
        shards,
        mesh=fine,
        in_specs=(
            P(None, None, FSDP, "z"),
            P(None, None, FSDP, "z"),
            P(None, None, "z", None),
            P(),
        ),
        out_specs=(
            P("z", None, FSDP, None),
            P("z", None, FSDP, None),
            P(None, None, "z", None),
        ),
        check_vma=False,
    )
```

```python
import functools
import math

import jax
import jax.numpy as jnp
from jax import lax
from jax.experimental import pallas as pl
from jax.experimental.pallas import tpu as pltpu
from jax.sharding import Mesh
from jax.sharding import PartitionSpec as P

D = 4096
HID = 1536
CAP = 2
EXPERTS = 10
GROUPS = 16
BLOCK = 96
RANK = 128

ridge_term = 0.001
feedback = 0.1
epsilon = 1e-06

F32 = jnp.float32
BF16 = jnp.bfloat16
HIGHEST = lax.Precision.HIGHEST
XY = ("x", "y")
FSDP = ("x", "y", "c")
SWAP = [(0, 1), (1, 0)]
VMEM = pl.BlockSpec(memory_space=pltpu.VMEM)
SMEM = pl.BlockSpec(memory_space=pltpu.SMEM)


def call(body, outs, scratch=(), flops=0, specs=None, n_in=0):
    return pl.pallas_call(
        body,
        out_shape=outs,
        in_specs=specs if specs is not None else [VMEM] * n_in,
        out_specs=jax.tree.map(lambda _: VMEM, outs),
        scratch_shapes=list(scratch),
        compiler_params=pltpu.CompilerParams(vmem_limit_bytes=48 * 1024 * 1024),
        cost_estimate=pl.CostEstimate(flops=flops, bytes_accessed=4_000_000, transcendentals=0),
    )


def dot(a, b, contract=((1,), (0,)), precision=None):
    return lax.dot_general(
        a, b, (contract, ((), ())), precision=precision, preferred_element_type=F32
    )


def iota(shape, dim):
    return lax.broadcasted_iota(jnp.int32, shape, dim)


def fill_table(own, table, count):
    for g in range(GROUPS):
        count[g] = 0
    for s in range(GROUPS * CAP):
        table[s] = EXPERTS
    for e in range(EXPERTS):
        g = own[e]
        p = count[g]
        count[g] = p + 1
        table[g * CAP + p] = e


def tile_row(position):
    t = position & 7
    return jnp.where(t >= 3, t - 3 + BLOCK, t)


def slice_right(own, place, right, out, table, count, held):
    fill_table(own, table, count)
    f = place[0] * 8 + place[1] * 2 + place[2]
    t = iota((8, 192), 0)
    pick = ((iota((8, 192), 1) == tile_row(t) + 3 * f) & (t < 6)).astype(BF16)
    for e in range(EXPERTS):
        held[e] = dot(pick, right[e].reshape(192, RANK))
    held[EXPERTS] = jnp.zeros((8, RANK), F32)

    def group(g, _):
        pair = jnp.concatenate([held[table[g * CAP]], held[table[g * CAP + 1]]], axis=0)
        out[g] = pair.astype(BF16)
        return 0

    lax.fori_loop(0, GROUPS, group, 0)


def place_state(own, momentum, gradient, out, table, count):
    fill_table(own, table, count)

    def slot(s, _):
        e = table[s]

        @pl.when(e < EXPERTS)
        def _():
            total = momentum[e].astype(F32) + gradient[e].astype(F32)
            out[s] = total.astype(BF16).reshape(192, 128)

        @pl.when(e >= EXPERTS)
        def _():
            out[s] = jnp.zeros((192, 128), BF16)

        return 0

    lax.fori_loop(0, GROUPS * CAP, slot, 0)


def offset(i):
    return jnp.where(i == 1, 3, jnp.where(i == 2, 1, jnp.where(i == 3, 2, 0)))


def unpermute_matrix(place, core, relative):
    col = iota((384, 256), 1)
    chip = col >> 4
    if relative:
        x = (place[0] + offset(chip & 3)) & 3
        y = (place[1] + offset(chip >> 2)) & 3
        chip = x * 4 + y
    f = chip * 2 + core
    target = ((col >> 3) & 1) * 192 + tile_row(col) + 3 * f
    return ((iota((384, 256), 0) == target) & ((col & 7) < 6)).astype(BF16)


def join_right(place, near, far, out, matrix):
    c = place[2]
    matrix[:, :256] = unpermute_matrix(place, c, True)
    matrix[:, 256:] = unpermute_matrix(place, 1 - c, True)

    def block(z, _):
        a = near[:, z].reshape(256, RANK)
        b = far[:, z].reshape(256, RANK)
        both = jnp.concatenate([a, b], axis=0)
        out[z] = dot(matrix[...], both).astype(BF16)
        return 0

    lax.fori_loop(0, GROUPS, block, 0)


def split3(value):
    high = value.astype(BF16)
    rest = value - high.astype(F32)
    middle = rest.astype(BF16)
    low = (rest - middle.astype(F32)).astype(BF16)
    return high, middle, low


def permute_matrix(place, kind):
    row = iota((256, BLOCK), 0)
    f = ((row >> 3) & 15) * 2 + ((row >> 7) ^ place[2])
    t = row & 7
    j = t - 3 * kind
    return ((iota((256, BLOCK), 1) == 3 * f + j) & (j >= 0) & (j < 3)).astype(BF16)


def panels(state, right, panel, gram):
    for i in range(2 * CAP):
        rows = pl.ds(i * BLOCK, BLOCK)

        def block(z, total):
            return total + dot(state[z, rows, :], right[z, rows, :], ((0,), (0,)))

        value = lax.fori_loop(0, GROUPS, block, jnp.zeros((128, RANK), F32), unroll=4)
        panel[i] = value
        gram[i] = dot(value, value, ((0,), (0,)), HIGHEST)


def weigh(place, state, panel, keep, send):
    order = [permute_matrix(place, k) for k in range(2)]
    for s in range(CAP):
        parts = [split3(panel[2 * s + k]) for k in range(2)]
        stacked = [jnp.concatenate([parts[0][i], parts[1][i]], axis=0) for i in range(3)]

        def block(z, _):
            moved = [
                dot(order[k], state[z, pl.ds((2 * s + k) * BLOCK, BLOCK), :]).astype(BF16)
                for k in range(2)
            ]
            wide = jnp.concatenate(moved, axis=1)
            value = dot(wide, stacked[0]) + (dot(wide, stacked[1]) + dot(wide, stacked[2]))
            rows = pl.ds(s * 8, 8)
            keep[:, z, rows, :] = value[:128].reshape(16, 8, RANK)
            send[:, z, rows, :] = value[128:].reshape(16, 8, RANK)
            return 0

        lax.fori_loop(0, GROUPS, block, 0, unroll=4)


def invert(gram, out, work, *, count, size):
    n = RANK
    eye = (iota((n, n), 0) == iota((n, n), 1)).astype(F32)
    for m in range(count):
        work[m, :, :n] = gram[m] + ridge_term * eye
        work[m, :, n:] = eye
    row = iota((size, 2 * n), 0)
    lane = iota((size, n), 1)
    for k in range(0, n, size):
        blocks = [work[m, k : k + size, :] for m in range(count)]
        for i in range(size):
            for m in range(count):
                b = blocks[m]
                scale = lax.rsqrt(b[i : i + 1, k + i : k + i + 1])
                line = b[i : i + 1, :] * scale
                column = jnp.where(row > i, b[:, k + i : k + i + 1] * scale, 0.0)
                blocks[m] = jnp.where(row == i, line, b - column * line)
        for m in range(count):
            b = blocks[m]
            out[m, k : k + size, :] = b[:, n:]
            if k + size < n:
                left = jnp.where(lane >= k + size, b[:, :n], 0.0)
                change = dot(left, b, ((0,), (0,)), HIGHEST)
                work[m, k + size :, :] -= change[k + size :, :]


def scale_factor(parts, inverse, out):
    total = parts[0]
    for i in range(1, 16):
        total = total + parts[i]
    rows = GROUPS * 8
    t = iota((rows, RANK), 0) & 7
    tiles = []
    for s in range(CAP):
        w = total[:, s * 8 : (s + 1) * 8, :].reshape(rows, RANK)
        both = [dot(w, inverse[2 * s + k], ((1,), (1,)), HIGHEST) for k in range(2)]
        value = jnp.where(t < 3, both[0], both[1])
        square = value * value
        sums = [
            jnp.sum(jnp.where((t >= 3 * k) & (t < 3 * k + 3), square, 0.0), axis=0, keepdims=True)
            for k in range(2)
        ]
        value = jnp.where(t == 6, sums[0], jnp.where(t == 7, sums[1], value))
        tiles.append(value.reshape(GROUPS, 8, RANK))
    out[...] = jnp.concatenate(tiles, axis=1).astype(BF16)


def orthonormal(panel, inverse, left, low):
    for i in range(2 * CAP):
        ortho = dot(panel[i], inverse[i], ((1,), (1,)), HIGHEST)
        left[i] = ortho * math.sqrt(D)
        low[i] = (ortho * (-feedback)).astype(BF16)


def select(own, mine, tiles, out, table, count, held, packed):
    fill_table(own, table, count)
    for g in range(GROUPS):
        value = tiles[g].astype(F32)
        for s in range(CAP):
            held[table[g * CAP + s]] = value[s * 8 : (s + 1) * 8]
    for e in range(0, EXPERTS, 2):
        packed[256 + e * 8 : 272 + e * 8, :] = jnp.concatenate([held[e], held[e + 1]], axis=0).astype(BF16)
    packed[:256, :] = mine[...].reshape(256, RANK)
    value = packed[...]
    for i in range(16):
        out[i] = value


def finish_right(place, near, far, out):
    col = iota((392, 256), 1)
    row = iota((392, 256), 0)
    t = col & 7
    s = (col >> 3) & 1
    matrices = []
    for core in (place[2], 1 - place[2]):
        f = (col >> 4) * 2 + core
        target = jnp.where(t < 6, s * 192 + tile_row(col) + 3 * f, 384 + s * 2 + (t - 6))
        matrices.append((row == target).astype(BF16))
    both = jnp.concatenate(matrices, axis=1)
    for g in range(EXPERTS // 2):
        rows = slice(256 + g * 16, 272 + g * 16)
        data = jnp.concatenate(
            [near[:, rows, :].reshape(256, RANK), far[:, rows, :].reshape(256, RANK)], axis=0
        )
        value = dot(both, data)
        for s in range(2):
            for k in range(2):
                i = 2 * s + k
                scale = lax.rsqrt(value[384 + i : 385 + i, :] * (1.0 / HID) + epsilon)
                out[2 * g + s, k] = value[i * BLOCK : (i + 1) * BLOCK, :] * scale


def finish_state(place, state, near, far, low, out, matrix, wide):
    c = place[2]
    matrix[:, :256] = unpermute_matrix(place, c, False)
    matrix[:, 256:] = unpermute_matrix(place, 1 - c, False)

    def block(z, _):
        tile = pl.ds(pl.multiple_of(z * 16, 16), 16)
        both = jnp.concatenate(
            [near[:, tile, :].reshape(256, RANK), far[:, tile, :].reshape(256, RANK)], axis=0
        )
        value = dot(matrix[...], both).astype(BF16)
        rows = pl.ds(pl.multiple_of(z * BLOCK, BLOCK), BLOCK)
        for i in range(2 * CAP):
            wide[i, rows, :128] = state[z, i * BLOCK : (i + 1) * BLOCK, :]
            wide[i, rows, 128:] = value[i * BLOCK : (i + 1) * BLOCK, :]
        return 0

    lax.fori_loop(0, GROUPS, block, 0)
    eye = (iota((128, 128), 0) == iota((128, 128), 1)).astype(BF16)
    for i in range(2 * CAP):
        lhs = jnp.concatenate([eye, low[i]], axis=1)
        out[i] = dot(lhs, wide[i], ((1,), (1,))).astype(BF16)


def gather_slices(x):
    ring = lambda shift: [(i, (i + shift) % 4) for i in range(4)]
    for axis in ("x", "y"):
        x = jnp.stack([x] + [lax.ppermute(x, axis, ring(d)) for d in (1, 3, 2)])
    x = x.reshape((16,) + x.shape[2:])
    return x, lax.ppermute(x, "c", SWAP)


def exchange(x, axis):
    return lax.all_to_all(x, axis, split_axis=0, concat_axis=0, tiled=True)


def shards(momentum, gradient, right_in, owners):
    sds = jax.ShapeDtypeStruct
    place = jnp.stack([lax.axis_index("x"), lax.axis_index("y"), lax.axis_index("c")]).astype(
        jnp.int32
    )
    tables = [pltpu.SMEM((GROUPS * CAP,), jnp.int32), pltpu.SMEM((GROUPS,), jnp.int32)]
    n = 2 * CAP
    slices = call(
        slice_right,
        sds((16, 16, RANK), BF16),
        tables + [pltpu.VMEM((EXPERTS + 1, 8, RANK), F32)],
        specs=[SMEM, SMEM, VMEM],
    )(owners, place, right_in)
    slices = exchange(slices, "z")
    sent = call(
        place_state, sds((32, 192, 128), BF16), tables, specs=[SMEM, VMEM, VMEM]
    )(owners, jnp.swapaxes(momentum, 2, 3), jnp.swapaxes(gradient, 2, 3))
    sent, slices = lax.optimization_barrier((sent, slices))
    state = exchange(sent.reshape(16, 384, 128), "z")
    near, far = gather_slices(slices)
    matrix = pltpu.VMEM((384, 512), BF16)
    right = call(
        join_right, sds((16, 384, RANK), BF16), [matrix], flops=800_000_000, specs=[SMEM, VMEM, VMEM]
    )(place, near, far)
    panel, gram = call(
        panels, (sds((n, 128, RANK), F32), sds((n, RANK, RANK), F32)), n_in=2, flops=500_000_000
    )(state, right)
    gram = exchange(gram.reshape(32, 4 * n, RANK), FSDP)
    gram = jnp.broadcast_to(jnp.sum(gram, axis=0)[None], gram.shape)
    gram = exchange(gram, FSDP).reshape(n, RANK, RANK)
    half = sds((16, 16, 16, RANK), F32)
    keep, send = call(weigh, (half, half), specs=[SMEM, VMEM, VMEM], flops=2_000_000_000)(
        place, state, panel
    )
    parts = keep + lax.ppermute(send, "c", SWAP)
    parts = exchange(parts.reshape(16, 256, RANK), XY).reshape(16, 16, 16, RANK)
    inverse = call(
        functools.partial(invert, count=n, size=8),
        sds((n, RANK, RANK), F32),
        [pltpu.VMEM((n, RANK, 2 * RANK), F32)],
        n_in=1,
        flops=8_000_000_000,
    )(gram)
    tiles = call(scale_factor, sds((16, 16, RANK), BF16), n_in=2, flops=100_000_000)(parts, inverse)
    left, low = call(
        orthonormal,
        (sds((n, 128, RANK), F32), sds((n, 128, RANK), BF16)),
        n_in=2,
        flops=100_000_000,
    )(panel, inverse)
    back = exchange(tiles, "z")
    chosen = call(
        select,
        sds((16, 336, RANK), BF16),
        tables + [pltpu.VMEM((EXPERTS + 1, 8, RANK), F32), pltpu.VMEM((336, RANK), BF16)],
        specs=[SMEM, VMEM, VMEM],
    )(owners, tiles, back)
    near = exchange(chosen, XY)
    far = lax.ppermute(near, "c", SWAP)
    right_out = call(
        finish_right, sds((EXPERTS, 2, BLOCK, RANK), F32), specs=[SMEM, VMEM, VMEM], flops=300_000_000
    )(place, near, far)
    state_out = call(
        finish_state,
        sds((n, 128, HID), BF16),
        [matrix, pltpu.VMEM((n, HID, 256), BF16)],
        specs=[SMEM, VMEM, VMEM, VMEM, VMEM],
        flops=1_200_000_000,
    )(place, state, near, far, low)
    return (
        state_out.reshape(CAP, 2, 128, HID),
        left.reshape(CAP, 2, 128, RANK),
        right_out,
    )


def solution(mesh):
    fine = Mesh(mesh.devices.reshape(4, 4, 2, 16), ("x", "y", "c", "z"))
    return jax.shard_map(
        shards,
        mesh=fine,
        in_specs=(
            P(None, None, FSDP, "z"),
            P(None, None, FSDP, "z"),
            P(None, None, "z", None),
            P(),
        ),
        out_specs=(
            P("z", None, FSDP, None),
            P("z", None, FSDP, None),
            P(None, None, "z", None),
        ),
        check_vma=False,
    )
```

```python
import functools
import math

import jax
import jax.numpy as jnp
from jax import lax
from jax.experimental import pallas as pl
from jax.experimental.pallas import tpu as pltpu
from jax.sharding import Mesh
from jax.sharding import PartitionSpec as P

D = 4096
HID = 1536
CAP = 2
EXPERTS = 10
GROUPS = 16
BLOCK = 96
RANK = 128

ridge_term = 0.001
feedback = 0.1
epsilon = 1e-06

F32 = jnp.float32
BF16 = jnp.bfloat16
HIGHEST = lax.Precision.HIGHEST
XY = ("x", "y")
FSDP = ("x", "y", "c")
SWAP = [(0, 1), (1, 0)]
VMEM = pl.BlockSpec(memory_space=pltpu.VMEM)
SMEM = pl.BlockSpec(memory_space=pltpu.SMEM)


def call(body, outs, scratch=(), flops=0, specs=None, n_in=0):
    return pl.pallas_call(
        body,
        out_shape=outs,
        in_specs=specs if specs is not None else [VMEM] * n_in,
        out_specs=jax.tree.map(lambda _: VMEM, outs),
        scratch_shapes=list(scratch),
        compiler_params=pltpu.CompilerParams(vmem_limit_bytes=48 * 1024 * 1024),
        cost_estimate=pl.CostEstimate(flops=flops, bytes_accessed=4_000_000, transcendentals=0),
    )


def dot(a, b, contract=((1,), (0,)), precision=None):
    return lax.dot_general(
        a, b, (contract, ((), ())), precision=precision, preferred_element_type=F32
    )


def iota(shape, dim):
    return lax.broadcasted_iota(jnp.int32, shape, dim)


COUNT, WORK, SECOND, HELPER, WHERE, FREE, TABLE = 0, 17, 34, 51, 68, 80, 97
NONE = GROUPS


def fill_table(own, table):
    for g in range(GROUPS + 1):
        table[COUNT + g] = 0
        table[WORK + g] = EXPERTS
        table[SECOND + g] = EXPERTS
        table[HELPER + g] = 0
    for e in range(EXPERTS):
        g = own[e]
        p = table[COUNT + g]
        table[COUNT + g] = p + 1
        table[WORK + jnp.where(p == 0, g, NONE)] = e
        table[SECOND + jnp.where(p == 0, NONE, g)] = e
    free = jnp.int32(0)
    for g in range(GROUPS):
        table[FREE + free] = g
        free = free + jnp.where(table[COUNT + g] == 0, 1, 0)
    used = jnp.int32(0)
    for e in range(EXPERTS):
        g = own[e]
        second = table[SECOND + g] == e
        h = table[FREE + used]
        table[WORK + jnp.where(second, h, NONE)] = e
        table[HELPER + jnp.where(second, g, NONE)] = h
        table[WHERE + e] = jnp.where(second, h, g)
        used = used + jnp.where(second, 1, 0)


def slice_right(own, place, right, out, table, held):
    fill_table(own, table)
    f = place[0] * 8 + place[1] * 2 + place[2]
    pick = (iota((8, 192), 1) == iota((8, 192), 0) + 8 * f).astype(BF16)
    for e in range(EXPERTS):
        held[e] = dot(pick, right[e].reshape(192, RANK))
    held[EXPERTS] = jnp.zeros((8, RANK), F32)

    def group(g, _):
        pair = jnp.concatenate([held[table[WORK + g]], held[table[SECOND + g]]], axis=0)
        out[g] = pair.astype(BF16)
        return 0

    lax.fori_loop(0, GROUPS, group, 0)


def place_state(table, momentum, gradient, first, other):
    def slot(g, _):
        for base, out in ((WORK, first), (SECOND, other)):
            e = table[base + g]

            @pl.when(e < EXPERTS)
            def _():
                total = momentum[e].astype(F32) + gradient[e].astype(F32)
                out[g] = total.astype(BF16).reshape(192, 128)

            @pl.when(e >= EXPERTS)
            def _():
                out[g] = jnp.zeros((192, 128), BF16)

        return 0

    lax.fori_loop(0, GROUPS, slot, 0)


def offset(i):
    return jnp.where(i == 1, 3, jnp.where(i == 2, 1, jnp.where(i == 3, 2, 0)))


def join_matrix(place, core, relative, chips):
    col = iota((384, 16 * chips), 1)
    chip = col >> 4
    if relative:
        x = (place[0] + offset(chip & 3)) & 3
        y = (place[1] + offset(chip >> 2)) & 3
        chip = x * 4 + y
    f = chip * 2 + core
    target = ((col >> 3) & 1) * 192 + 8 * f + (col & 7)
    return ((iota((384, 16 * chips), 0) == target) & (f < 24)).astype(BF16)


def join_right(place, near, far, out, matrix):
    c = place[2]
    matrix[:, :256] = join_matrix(place, c, True, 16)
    matrix[:, 256:] = join_matrix(place, 1 - c, True, 16)

    def block(z, _):
        a = near[:, z].reshape(256, RANK)
        b = far[:, z].reshape(256, RANK)
        both = jnp.concatenate([a, b], axis=0)
        out[z] = dot(matrix[...], both).astype(BF16)
        return 0

    lax.fori_loop(0, GROUPS, block, 0)


def split3(value):
    high = value.astype(BF16)
    rest = value - high.astype(F32)
    middle = rest.astype(BF16)
    low = (rest - middle.astype(F32)).astype(BF16)
    return high, middle, low


def panel_of(state, right, kind, slot):
    def block(z, total):
        a = state[z, kind * BLOCK : (kind + 1) * BLOCK, :]
        b = right[z, pl.ds(slot * 192 + kind * BLOCK, BLOCK), :]
        return total + dot(a, b, ((0,), (0,)))

    return lax.fori_loop(0, GROUPS, block, jnp.zeros((128, RANK), F32), unroll=4)


def panels(place, state, right, panel, keep, send):
    grams = []
    for k in range(2):
        value = panel_of(state, right, k, 0)
        panel[k] = value
        grams.append(dot(value, value, ((0,), (0,)), HIGHEST))
    mine = place[2] == 0
    keep[...] = jnp.where(mine, grams[0], grams[1])
    send[...] = jnp.where(mine, grams[1], grams[0])


def second_panels(state, right, panel):
    for k in range(2):
        panel[k] = panel_of(state, right, k, 1)


def weigh(place, state, panel, keep, send, rows):
    weights = [jnp.concatenate(split3(panel[k]), axis=1) for k in range(2)]
    rows[192:, :] = jnp.zeros((64, RANK), F32)

    def block(z, _):
        for k in range(2):
            value = dot(state[z, k * BLOCK : (k + 1) * BLOCK, :], weights[k])
            total = value[:, :128] + (value[:, 128:256] + value[:, 256:])
            rows[k * BLOCK : (k + 1) * BLOCK, :] = total
        for i in range(16):
            x = (place[0] + offset(i & 3)) & 3
            y = (place[1] + offset(i >> 2)) & 3
            base = (x * 4 + y) * 16
            near = pl.multiple_of(base + 8 * place[2], 8)
            far = pl.multiple_of(base + 8 - 8 * place[2], 8)
            keep[i, z] = rows[pl.ds(near, 8), :]
            send[i, z] = rows[pl.ds(far, 8), :]
        return 0

    lax.fori_loop(0, GROUPS, block, 0, unroll=2)


def invert(place, near, far, out, work, *, size):
    n = RANK
    eye = (iota((n, n), 0) == iota((n, n), 1)).astype(F32)
    mine = place[2] == 0
    first, other = near[...], far[...]
    work[0, :, :n] = jnp.where(mine, first, other) + ridge_term * eye
    work[1, :, :n] = jnp.where(mine, other, first) + ridge_term * eye
    for m in range(2):
        work[m, :, n:] = eye
    row = iota((size, 2 * n), 0)
    lane = iota((size, n), 1)
    for k in range(0, n, size):
        blocks = [work[m, k : k + size, :] for m in range(2)]
        for i in range(size):
            for m in range(2):
                b = blocks[m]
                scale = lax.rsqrt(b[i : i + 1, k + i : k + i + 1])
                line = b[i : i + 1, :] * scale
                column = jnp.where(row > i, b[:, k + i : k + i + 1] * scale, 0.0)
                blocks[m] = jnp.where(row == i, line, b - column * line)
        for m in range(2):
            b = blocks[m]
            out[m, k : k + size, :] = b[:, n:]
            if k + size < n:
                left = jnp.where(lane >= k + size, b[:, :n], 0.0)
                change = dot(left, b, ((0,), (0,)), HIGHEST)
                work[m, k + size :, :] -= change[k + size :, :]


def scale_factor(place, inverse, a, b, c, d, out):
    f = place[0] * 8 + place[1] * 2 + place[2]
    total = ((a[...] + b[...]) + (c[...] + d[...])).reshape(128, RANK)
    kind = jnp.where(f >= 12, 1, 0)
    out[:128] = dot(total, inverse[kind], ((1,), (1,)), HIGHEST).astype(BF16)
    half = jnp.where(f >= 16, 1, 0)
    start = pl.multiple_of(8 * f - 128 * half, 8)
    rows = inverse[half, pl.ds(start, 8), :]
    high = rows.astype(BF16).astype(F32)
    out[128:] = jnp.concatenate([high, rows - high], axis=0).astype(BF16)


def orthonormal(table, place, panel, inverse, left, low):
    owned = table[COUNT + place[3]] > 0
    for k in range(2):
        ortho = dot(panel[k], inverse[k], ((1,), (1,)), HIGHEST)
        ortho = jnp.where(owned, ortho, 0.0)
        left[k] = ortho * math.sqrt(D)
        low[k] = (ortho * (-feedback)).astype(BF16)


def turn(table, place, first, second, out):
    owned = table[COUNT + place[3]] > 0
    eye = (iota((128, 128), 0) == iota((128, 128), 1)).astype(BF16)
    some = jnp.where(owned, eye, jnp.zeros_like(eye))
    for s, (state, unit) in enumerate(((first, some), (second, eye))):
        for k in range(2):
            rows = state[:, k * BLOCK : (k + 1) * BLOCK, :].reshape(HID, 128)
            out[2 * s + k] = dot(unit, rows, ((1,), (1,))).astype(BF16)


ROWS = 368


def select(table, place, mine, tiles, out, packed):
    z = place[3]
    packed[:128, :] = mine[:128, :]
    packed[128:272, :] = tiles[table[HELPER + z]]
    start = pl.multiple_of((z >> 1) * 16, 16)
    upper = (z & 1) == 1
    sums = []
    for e in range(0, EXPERTS, 2):
        pair = []
        for i in range(2):
            p = table[WHERE + e + i]
            value = tiles[p, pl.ds(start, 16), :].astype(F32)
            pair.append(jnp.where(upper, value[8:], value[:8]))
            whole = tiles[p, :128, :].astype(F32)
            sums.append(jnp.sum(whole * whole, axis=0, keepdims=True))
        packed[272 + e * 8 : 288 + e * 8, :] = jnp.concatenate(pair, axis=0).astype(BF16)
    sums.append(jnp.zeros((16 - EXPERTS, RANK), F32))
    packed[352:, :] = jnp.concatenate(sums, axis=0).astype(BF16)
    value = packed[...]
    for i in range(16):
        out[i] = value


def finish_right(place, near, far, out):
    c = place[2]
    matrix = jnp.concatenate(
        [join_matrix(place, c, False, 12), join_matrix(place, 1 - c, False, 12)], axis=1
    )
    parts = near[:, 352:, :].astype(F32) + far[:, 352:, :].astype(F32)
    sums = [jnp.sum(parts[6 * k : 6 * k + 6], axis=0) for k in range(2)]
    scales = [lax.rsqrt(s * (1.0 / HID) + epsilon) for s in sums]
    for g in range(EXPERTS // 2):
        rows = slice(272 + g * 16, 288 + g * 16)
        data = jnp.concatenate(
            [near[:12, rows, :].reshape(192, RANK), far[:12, rows, :].reshape(192, RANK)], axis=0
        )
        value = dot(matrix, data)
        for s in range(2):
            e = 2 * g + s
            for k in range(2):
                i = 2 * s + k
                out[e, k] = value[i * BLOCK : (i + 1) * BLOCK, :] * scales[k][e : e + 1, :]


def finish_state(table, place, turned, near, far, low, panel, left, out, left_out, inverse, wide):
    c = place[2]
    matrix = jnp.concatenate(
        [join_matrix(place, c, False, 12), join_matrix(place, 1 - c, False, 12)], axis=1
    )
    for part, core in ((near, c), (far, 1 - c)):
        for chip in range(16):
            value = part[chip, 256:272, :].astype(F32)
            row = pl.multiple_of(16 * chip + 8 * core, 8)
            inverse[pl.ds(row, 8), :] = value[:8] + value[8:]
    some = table[SECOND + place[3]] < EXPERTS
    lows = [low[0], low[1]]
    for k in range(2):
        ortho = dot(panel[k], inverse[k * RANK : (k + 1) * RANK, :], ((1,), (1,)), HIGHEST)
        ortho = jnp.where(some, ortho, 0.0)
        left_out[k] = left[k]
        left_out[2 + k] = ortho * math.sqrt(D)
        lows.append((ortho * (-feedback)).astype(BF16))
    for s in range(2):
        for g in range(8):
            rows = slice(s * 128 + g * 16, s * 128 + g * 16 + 16)
            data = jnp.concatenate(
                [near[:12, rows, :].reshape(192, RANK), far[:12, rows, :].reshape(192, RANK)],
                axis=0,
            )
            value = dot(matrix, data).astype(BF16)
            for p in range(2):
                for k in range(2):
                    i = 2 * p + k
                    first = (2 * g + p) * BLOCK
                    wide[2 * s + k, first : first + BLOCK, :] = value[i * BLOCK : (i + 1) * BLOCK]
    for i in range(4):
        change = dot(lows[i], wide[i], ((1,), (1,)))
        out[i] = (turned[i].astype(F32) + change).astype(BF16)


def ring(shift):
    return [(i, (i + shift) % 4) for i in range(4)]


SHIFTS = (3, 1, 2)


def gather_slices(x):
    for axis in ("x", "y"):
        x = jnp.stack([x] + [lax.ppermute(x, axis, ring((4 - d) % 4)) for d in SHIFTS])
    x = x.reshape((16,) + x.shape[2:])
    return x, lax.ppermute(x, "c", SWAP)


def spread_sum(x, axis):
    parts = [lax.ppermute(x, axis, ring(d)) for d in SHIFTS]
    return (x + parts[0]) + (parts[1] + parts[2])


def exchange(x, axis):
    return lax.all_to_all(x, axis, split_axis=0, concat_axis=0, tiled=True)


def shards(momentum, gradient, right_in, owners):
    sds = jax.ShapeDtypeStruct
    barrier = lax.optimization_barrier
    place = jnp.stack([lax.axis_index(a) for a in ("x", "y", "c", "z")]).astype(jnp.int32)
    slices, table = pl.pallas_call(
        slice_right,
        out_shape=(sds((16, 16, RANK), BF16), sds((TABLE,), jnp.int32)),
        in_specs=[SMEM, SMEM, VMEM],
        out_specs=(VMEM, SMEM),
        scratch_shapes=[pltpu.VMEM((EXPERTS + 1, 8, RANK), F32)],
    )(owners, place, right_in)
    slices = exchange(slices, "z")
    block = sds((16, 192, 128), BF16)
    sent, late = call(place_state, (block, block), specs=[SMEM, VMEM, VMEM])(
        table, jnp.swapaxes(momentum, 2, 3), jnp.swapaxes(gradient, 2, 3)
    )
    sent, slices = barrier((sent, slices))
    state = exchange(sent, "z")
    near, far = gather_slices(slices)
    right = call(
        join_right,
        sds((16, 384, RANK), BF16),
        [pltpu.VMEM((384, 512), BF16)],
        flops=800_000_000,
        specs=[SMEM, VMEM, VMEM],
    )(place, near, far)
    square = sds((RANK, RANK), F32)
    two = sds((2, 128, RANK), F32)
    panel, keep, send = call(
        panels, (two, square, square), specs=[SMEM, VMEM, VMEM], flops=300_000_000
    )(place, state, right)
    late, send = barrier((late, send))
    second = exchange(late, "z")
    gram = keep + lax.ppermute(send, "c", SWAP)
    half = sds((16, 16, 8, RANK), F32)
    keep, send = call(
        weigh, (half, half), [pltpu.VMEM((256, RANK), F32)], specs=[SMEM, VMEM, VMEM], flops=400_000_000
    )(place, state, panel)
    gram = spread_sum(spread_sum(gram, "x"), "y")
    other = lax.ppermute(gram, "c", SWAP)
    parts = keep + lax.ppermute(send, "c", SWAP)
    parts = parts.reshape(4, 4, 16, 8, RANK)
    moved = [lax.ppermute(parts[:, i + 1], "x", ring(SHIFTS[i])) for i in range(3)]
    parts = (parts[:, 0] + moved[0]) + (moved[1] + moved[2])
    parts = [parts[0]] + [lax.ppermute(parts[i + 1], "y", ring(SHIFTS[i])) for i in range(3)]
    inverse = call(
        functools.partial(invert, size=8),
        sds((2, RANK, RANK), F32),
        [pltpu.VMEM((2, RANK, 2 * RANK), F32)],
        specs=[SMEM, VMEM, VMEM],
        flops=4_000_000_000,
    )(place, gram, other)
    mine = call(
        scale_factor, sds((144, RANK), BF16), specs=[SMEM] + [VMEM] * 5, flops=100_000_000
    )(place, inverse, *parts)
    left, low = call(
        orthonormal, (two, sds((2, 128, RANK), BF16)), specs=[SMEM, SMEM, VMEM, VMEM], flops=100_000_000
    )(table, place, panel, inverse)
    tiles = lax.all_gather(mine, "z")
    second_panel = call(second_panels, two, n_in=2, flops=200_000_000)(second, right)
    turned = call(
        turn, sds((4, 128, HID), BF16), specs=[SMEM, SMEM, VMEM, VMEM], flops=200_000_000
    )(table, place, state, second)
    chosen = call(
        select,
        sds((16, ROWS, RANK), BF16),
        [pltpu.VMEM((ROWS, RANK), BF16)],
        specs=[SMEM, SMEM, VMEM, VMEM],
    )(table, place, mine, tiles)
    near = exchange(chosen, XY)
    far = lax.ppermute(near, "c", SWAP)
    right_out = call(
        finish_right, sds((EXPERTS, 2, BLOCK, RANK), F32), specs=[SMEM, VMEM, VMEM], flops=300_000_000
    )(place, near, far)
    state_out, left_out = call(
        finish_state,
        (sds((4, 128, HID), BF16), sds((4, 128, RANK), F32)),
        [pltpu.VMEM((2 * RANK, RANK), F32), pltpu.VMEM((4, HID, RANK), BF16)],
        specs=[SMEM, SMEM] + [VMEM] * 6,
        flops=1_200_000_000,
    )(table, place, turned, near, far, low, second_panel, left)
    return (
        state_out.reshape(CAP, 2, 128, HID),
        left_out.reshape(CAP, 2, 128, RANK),
        right_out,
    )


def solution(mesh):
    fine = Mesh(mesh.devices.reshape(4, 4, 2, 16), ("x", "y", "c", "z"))
    return jax.shard_map(
        shards,
        mesh=fine,
        in_specs=(
            P(None, None, FSDP, "z"),
            P(None, None, FSDP, "z"),
            P(None, None, "z", None),
            P(),
        ),
        out_specs=(
            P("z", None, FSDP, None),
            P("z", None, FSDP, None),
            P(None, None, "z", None),
        ),
        check_vma=False,
    )
```

```python
import functools
import math

import jax
import jax.numpy as jnp
from jax import lax
from jax.experimental import pallas as pl
from jax.experimental.pallas import tpu as pltpu
from jax.sharding import Mesh
from jax.sharding import PartitionSpec as P

D = 4096
HID = 1536
CAP = 2
EXPERTS = 10
GROUPS = 16
BLOCK = 96
RANK = 128

ridge_term = 0.001
feedback = 0.1
epsilon = 1e-06

F32 = jnp.float32
BF16 = jnp.bfloat16
HIGHEST = lax.Precision.HIGHEST
XY = ("x", "y")
FSDP = ("x", "y", "c")
SWAP = [(0, 1), (1, 0)]
VMEM = pl.BlockSpec(memory_space=pltpu.VMEM)
SMEM = pl.BlockSpec(memory_space=pltpu.SMEM)
ANY = pl.BlockSpec(memory_space=pl.ANY)


def call(body, outs, scratch=(), flops=0, specs=None, n_in=0):
    return pl.pallas_call(
        body,
        out_shape=outs,
        in_specs=specs if specs is not None else [VMEM] * n_in,
        out_specs=jax.tree.map(lambda _: VMEM, outs),
        scratch_shapes=list(scratch),
        compiler_params=pltpu.CompilerParams(vmem_limit_bytes=48 * 1024 * 1024),
        cost_estimate=pl.CostEstimate(flops=flops, bytes_accessed=4_000_000, transcendentals=0),
    )


def dot(a, b, contract=((1,), (0,)), precision=None):
    return lax.dot_general(
        a, b, (contract, ((), ())), precision=precision, preferred_element_type=F32
    )


def iota(shape, dim):
    return lax.broadcasted_iota(jnp.int32, shape, dim)


COUNT, WORK, SECOND, HELPER, WHERE, FREE, TABLE = 0, 17, 34, 51, 68, 80, 97
NONE = GROUPS


def fill_table(own, table):
    for g in range(GROUPS + 1):
        table[COUNT + g] = 0
        table[WORK + g] = EXPERTS
        table[SECOND + g] = EXPERTS
        table[HELPER + g] = 0
    for e in range(EXPERTS):
        g = own[e]
        p = table[COUNT + g]
        table[COUNT + g] = p + 1
        table[WORK + jnp.where(p == 0, g, NONE)] = e
        table[SECOND + jnp.where(p == 0, NONE, g)] = e
    free = jnp.int32(0)
    for g in range(GROUPS):
        table[FREE + free] = g
        free = free + jnp.where(table[COUNT + g] == 0, 1, 0)
    used = jnp.int32(0)
    for e in range(EXPERTS):
        g = own[e]
        second = table[SECOND + g] == e
        h = table[FREE + used]
        table[WORK + jnp.where(second, h, NONE)] = e
        table[HELPER + jnp.where(second, g, NONE)] = h
        table[WHERE + e] = jnp.where(second, h, g)
        used = used + jnp.where(second, 1, 0)


def slice_right(own, place, right, out, table, held):
    fill_table(own, table)
    f = place[0] * 8 + place[1] * 2 + place[2]
    pick = (iota((8, 192), 1) == iota((8, 192), 0) + 8 * f).astype(BF16)
    for e in range(EXPERTS):
        held[e] = dot(pick, right[e].reshape(192, RANK))
    held[EXPERTS] = jnp.zeros((8, RANK), F32)

    def group(g, _):
        pair = jnp.concatenate([held[table[WORK + g]], held[table[SECOND + g]]], axis=0)
        out[g] = pair.astype(BF16)
        return 0

    lax.fori_loop(0, GROUPS, group, 0)


def place_state(table, momentum, gradient, first, other):
    def slot(g, _):
        for base, out in ((WORK, first), (SECOND, other)):
            e = table[base + g]

            @pl.when(e < EXPERTS)
            def _():
                total = momentum[e].astype(F32) + gradient[e].astype(F32)
                out[g] = total.astype(BF16).reshape(192, 128)

            @pl.when(e >= EXPERTS)
            def _():
                out[g] = jnp.zeros((192, 128), BF16)

        return 0

    lax.fori_loop(0, GROUPS, slot, 0)


def offset(i):
    return jnp.where(i == 1, 3, jnp.where(i == 2, 1, jnp.where(i == 3, 2, 0)))


def join_matrix(place, core, relative, chips):
    col = iota((384, 16 * chips), 1)
    chip = col >> 4
    if relative:
        x = (place[0] + offset(chip & 3)) & 3
        y = (place[1] + offset(chip >> 2)) & 3
        chip = x * 4 + y
    f = chip * 2 + core
    target = ((col >> 3) & 1) * 192 + 8 * f + (col & 7)
    return ((iota((384, 16 * chips), 0) == target) & (f < 24)).astype(BF16)


def join_right(place, near, far, out, matrix):
    c = place[2]
    matrix[:, :256] = join_matrix(place, c, True, 16)
    matrix[:, 256:] = join_matrix(place, 1 - c, True, 16)

    def block(z, _):
        a = near[:, z].reshape(256, RANK)
        b = far[:, z].reshape(256, RANK)
        both = jnp.concatenate([a, b], axis=0)
        out[z] = dot(matrix[...], both).astype(BF16)
        return 0

    lax.fori_loop(0, GROUPS, block, 0)


def split3(value):
    high = value.astype(BF16)
    rest = value - high.astype(F32)
    middle = rest.astype(BF16)
    low = (rest - middle.astype(F32)).astype(BF16)
    return high, middle, low


def panel_of(state, right, kind, slot):
    def block(z, total):
        a = state[z, kind * BLOCK : (kind + 1) * BLOCK, :]
        b = right[z, pl.ds(slot * 192 + kind * BLOCK, BLOCK), :]
        return total + dot(a, b, ((0,), (0,)))

    return lax.fori_loop(0, GROUPS, block, jnp.zeros((128, RANK), F32), unroll=4)


def panels(place, state, right, panel, keep, send):
    grams = []
    for k in range(2):
        value = panel_of(state, right, k, 0)
        panel[k] = value
        grams.append(dot(value, value, ((0,), (0,)), HIGHEST))
    mine = place[2] == 0
    keep[...] = jnp.where(mine, grams[0], grams[1])
    send[...] = jnp.where(mine, grams[1], grams[0])


def second_panels(state, right, panel):
    for k in range(2):
        panel[k] = panel_of(state, right, k, 1)


def weigh(place, state, panel, keep, send, rows):
    weights = [jnp.concatenate(split3(panel[k]), axis=1) for k in range(2)]
    rows[192:, :] = jnp.zeros((64, RANK), F32)

    def block(z, _):
        for k in range(2):
            value = dot(state[z, k * BLOCK : (k + 1) * BLOCK, :], weights[k])
            total = value[:, :128] + (value[:, 128:256] + value[:, 256:])
            rows[k * BLOCK : (k + 1) * BLOCK, :] = total
        for i in range(16):
            x = (place[0] + offset(i & 3)) & 3
            y = (place[1] + offset(i >> 2)) & 3
            base = (x * 4 + y) * 16
            near = pl.multiple_of(base + 8 * place[2], 8)
            far = pl.multiple_of(base + 8 - 8 * place[2], 8)
            keep[i, z] = rows[pl.ds(near, 8), :]
            send[i, z] = rows[pl.ds(far, 8), :]
        return 0

    lax.fori_loop(0, GROUPS, block, 0, unroll=2)


def invert(place, near, far, out, work, *, size):
    n = RANK
    eye = (iota((n, n), 0) == iota((n, n), 1)).astype(F32)
    mine = place[2] == 0
    first, other = near[...], far[...]
    work[0, :, :n] = jnp.where(mine, first, other) + ridge_term * eye
    work[1, :, :n] = jnp.where(mine, other, first) + ridge_term * eye
    for m in range(2):
        work[m, :, n:] = eye
    row = iota((size, 2 * n), 0)
    lane = iota((size, n), 1)
    for k in range(0, n, size):
        blocks = [work[m, k : k + size, :] for m in range(2)]
        for i in range(size):
            for m in range(2):
                b = blocks[m]
                scale = lax.rsqrt(b[i : i + 1, k + i : k + i + 1])
                line = b[i : i + 1, :] * scale
                column = jnp.where(row > i, b[:, k + i : k + i + 1] * scale, 0.0)
                blocks[m] = jnp.where(row == i, line, b - column * line)
        for m in range(2):
            b = blocks[m]
            out[m, k : k + size, :] = b[:, n:]
            if k + size < n:
                left = jnp.where(lane >= k + size, b[:, :n], 0.0)
                change = dot(left, b, ((0,), (0,)), HIGHEST)
                work[m, k + size :, :] -= change[k + size :, :]


def scale_factor(place, inverse, a, b, c, d, _, out):
    f = place[0] * 8 + place[1] * 2 + place[2]
    total = ((a[...] + b[...]) + (c[...] + d[...])).reshape(128, RANK)
    kind = jnp.where(f >= 12, 1, 0)
    out[:128] = dot(total, inverse[kind], ((1,), (1,)), HIGHEST).astype(BF16)
    half = jnp.where(f >= 16, 1, 0)
    start = pl.multiple_of(8 * f - 128 * half, 8)
    rows = inverse[half, pl.ds(start, 8), :]
    high = rows.astype(BF16).astype(F32)
    out[128:] = jnp.concatenate([high, rows - high], axis=0).astype(BF16)


def orthonormal(table, place, panel, inverse, left, low):
    owned = table[COUNT + place[3]] > 0
    for k in range(2):
        ortho = dot(panel[k], inverse[k], ((1,), (1,)), HIGHEST)
        ortho = jnp.where(owned, ortho, 0.0)
        left[k] = ortho * math.sqrt(D)
        low[k] = (ortho * (-feedback)).astype(BF16)


def turn(table, place, first, second, out):
    owned = table[COUNT + place[3]] > 0
    eye = (iota((128, 128), 0) == iota((128, 128), 1)).astype(BF16)
    some = jnp.where(owned, eye, jnp.zeros_like(eye))
    for s, (state, unit) in enumerate(((first, some), (second, eye))):
        for k in range(2):
            rows = state[:, k * BLOCK : (k + 1) * BLOCK, :].reshape(HID, 128)
            out[2 * s + k] = dot(unit, rows, ((1,), (1,))).astype(BF16)


ROWS = 368


def select(table, place, mine, tiles, out, packed):
    z = place[3]
    packed[:128, :] = mine[:128, :]
    packed[128:272, :] = tiles[table[HELPER + z]]
    start = pl.multiple_of((z >> 1) * 16, 16)
    upper = (z & 1) == 1
    sums = []
    for e in range(0, EXPERTS, 2):
        pair = []
        for i in range(2):
            p = table[WHERE + e + i]
            value = tiles[p, pl.ds(start, 16), :].astype(F32)
            pair.append(jnp.where(upper, value[8:], value[:8]))
            whole = tiles[p, :128, :].astype(F32)
            sums.append(jnp.sum(whole * whole, axis=0, keepdims=True))
        packed[272 + e * 8 : 288 + e * 8, :] = jnp.concatenate(pair, axis=0).astype(BF16)
    sums.append(jnp.zeros((16 - EXPERTS, RANK), F32))
    packed[352:, :] = jnp.concatenate(sums, axis=0).astype(BF16)
    value = packed[...]
    for i in range(16):
        out[i] = value


def finish_right(place, near, far, out):
    c = place[2]
    matrix = jnp.concatenate(
        [join_matrix(place, c, False, 12), join_matrix(place, 1 - c, False, 12)], axis=1
    )
    parts = near[:, 352:, :].astype(F32) + far[:, 352:, :].astype(F32)
    sums = [jnp.sum(parts[6 * k : 6 * k + 6], axis=0) for k in range(2)]
    scales = [lax.rsqrt(s * (1.0 / HID) + epsilon) for s in sums]
    for g in range(EXPERTS // 2):
        rows = slice(272 + g * 16, 288 + g * 16)
        data = jnp.concatenate(
            [near[:12, rows, :].reshape(192, RANK), far[:12, rows, :].reshape(192, RANK)], axis=0
        )
        value = dot(matrix, data)
        for s in range(2):
            e = 2 * g + s
            for k in range(2):
                i = 2 * s + k
                out[e, k] = value[i * BLOCK : (i + 1) * BLOCK, :] * scales[k][e : e + 1, :]


def finish_state(table, place, turned, near, far, low, panel, left, out, left_out, inverse, wide):
    c = place[2]
    matrix = jnp.concatenate(
        [join_matrix(place, c, False, 12), join_matrix(place, 1 - c, False, 12)], axis=1
    )
    for part, core in ((near, c), (far, 1 - c)):
        for chip in range(16):
            value = part[chip, 256:272, :].astype(F32)
            row = pl.multiple_of(16 * chip + 8 * core, 8)
            inverse[pl.ds(row, 8), :] = value[:8] + value[8:]
    some = table[SECOND + place[3]] < EXPERTS
    lows = [low[0], low[1]]
    for k in range(2):
        ortho = dot(panel[k], inverse[k * RANK : (k + 1) * RANK, :], ((1,), (1,)), HIGHEST)
        ortho = jnp.where(some, ortho, 0.0)
        left_out[k] = left[k]
        left_out[2 + k] = ortho * math.sqrt(D)
        lows.append((ortho * (-feedback)).astype(BF16))
    for s in range(2):
        for g in range(8):
            rows = slice(s * 128 + g * 16, s * 128 + g * 16 + 16)
            data = jnp.concatenate(
                [near[:12, rows, :].reshape(192, RANK), far[:12, rows, :].reshape(192, RANK)],
                axis=0,
            )
            value = dot(matrix, data).astype(BF16)
            for p in range(2):
                for k in range(2):
                    i = 2 * p + k
                    first = (2 * g + p) * BLOCK
                    wide[2 * s + k, first : first + BLOCK, :] = value[i * BLOCK : (i + 1) * BLOCK]
    for i in range(4):
        change = dot(lows[i], wide[i], ((1,), (1,)))
        out[i] = (turned[i].astype(F32) + change).astype(BF16)


def ring(shift):
    return [(i, (i + shift) % 4) for i in range(4)]


SHIFTS = (3, 1, 2)


def gather_slices(x):
    for axis in ("x", "y"):
        x = jnp.stack([x] + [lax.ppermute(x, axis, ring((4 - d) % 4)) for d in SHIFTS])
    x = x.reshape((16,) + x.shape[2:])
    return x, lax.ppermute(x, "c", SWAP)


def spread_sum(x, axis):
    parts = [lax.ppermute(x, axis, ring(d)) for d in SHIFTS]
    return (x + parts[0]) + (parts[1] + parts[2])


def exchange(x, axis):
    return lax.all_to_all(x, axis, split_axis=0, concat_axis=0, tiled=True)


def shards(momentum, gradient, right_in, owners):
    sds = jax.ShapeDtypeStruct
    barrier = lax.optimization_barrier
    place = jnp.stack([lax.axis_index(a) for a in ("x", "y", "c", "z")]).astype(jnp.int32)
    slices, table = pl.pallas_call(
        slice_right,
        out_shape=(sds((16, 16, RANK), BF16), sds((TABLE,), jnp.int32)),
        in_specs=[SMEM, SMEM, VMEM],
        out_specs=(VMEM, SMEM),
        scratch_shapes=[pltpu.VMEM((EXPERTS + 1, 8, RANK), F32)],
    )(owners, place, right_in)
    slices = exchange(slices, "z")
    block = sds((16, 192, 128), BF16)
    sent, late = call(place_state, (block, block), specs=[SMEM, VMEM, VMEM])(
        table, jnp.swapaxes(momentum, 2, 3), jnp.swapaxes(gradient, 2, 3)
    )
    sent, slices = barrier((sent, slices))
    state = exchange(sent, "z")
    near, far = gather_slices(slices)
    right = call(
        join_right,
        sds((16, 384, RANK), BF16),
        [pltpu.VMEM((384, 512), BF16)],
        flops=800_000_000,
        specs=[SMEM, VMEM, VMEM],
    )(place, near, far)
    square = sds((RANK, RANK), F32)
    two = sds((2, 128, RANK), F32)
    panel, keep, send = call(
        panels, (two, square, square), specs=[SMEM, VMEM, VMEM], flops=300_000_000
    )(place, state, right)
    late, send = barrier((late, send))
    second = exchange(late, "z")
    gram = keep + lax.ppermute(send, "c", SWAP)
    half = sds((16, 16, 8, RANK), F32)
    keep, send = call(
        weigh, (half, half), [pltpu.VMEM((256, RANK), F32)], specs=[SMEM, VMEM, VMEM], flops=400_000_000
    )(place, state, panel)
    parts = keep + lax.ppermute(send, "c", SWAP)
    parts, gram = barrier((parts, spread_sum(gram, "x")))
    parts = parts.reshape(4, 4, 16, 8, RANK)
    moved = [lax.ppermute(parts[:, i + 1], "x", ring(SHIFTS[i])) for i in range(3)]
    parts = (parts[:, 0] + moved[0]) + (moved[1] + moved[2])
    parts, gram = barrier((parts, spread_sum(gram, "y")))
    other = lax.ppermute(gram, "c", SWAP)
    parts = [parts[0]] + [lax.ppermute(parts[i + 1], "y", ring(SHIFTS[i])) for i in range(3)]
    inverse = call(
        functools.partial(invert, size=8),
        sds((2, RANK, RANK), F32),
        [pltpu.VMEM((2, RANK, 2 * RANK), F32)],
        specs=[SMEM, VMEM, VMEM],
        flops=4_000_000_000,
    )(place, gram, other)
    mine = call(
        scale_factor, sds((144, RANK), BF16), specs=[SMEM] + [VMEM] * 5 + [ANY], flops=100_000_000
    )(place, inverse, *parts, second)
    left, low = call(
        orthonormal, (two, sds((2, 128, RANK), BF16)), specs=[SMEM, SMEM, VMEM, VMEM], flops=100_000_000
    )(table, place, panel, inverse)
    tiles = lax.all_gather(mine, "z")
    second_panel = call(second_panels, two, n_in=2, flops=200_000_000)(second, right)
    turned = call(
        turn, sds((4, 128, HID), BF16), specs=[SMEM, SMEM, VMEM, VMEM], flops=200_000_000
    )(table, place, state, second)
    chosen = call(
        select,
        sds((16, ROWS, RANK), BF16),
        [pltpu.VMEM((ROWS, RANK), BF16)],
        specs=[SMEM, SMEM, VMEM, VMEM],
    )(table, place, mine, tiles)
    near = exchange(chosen, XY)
    far = lax.ppermute(near, "c", SWAP)
    right_out = call(
        finish_right, sds((EXPERTS, 2, BLOCK, RANK), F32), specs=[SMEM, VMEM, VMEM], flops=300_000_000
    )(place, near, far)
    state_out, left_out = call(
        finish_state,
        (sds((4, 128, HID), BF16), sds((4, 128, RANK), F32)),
        [pltpu.VMEM((2 * RANK, RANK), F32), pltpu.VMEM((4, HID, RANK), BF16)],
        specs=[SMEM, SMEM] + [VMEM] * 6,
        flops=1_200_000_000,
    )(table, place, turned, near, far, low, second_panel, left)
    return (
        state_out.reshape(CAP, 2, 128, HID),
        left_out.reshape(CAP, 2, 128, RANK),
        right_out,
    )


def solution(mesh):
    fine = Mesh(mesh.devices.reshape(4, 4, 2, 16), ("x", "y", "c", "z"))
    return jax.shard_map(
        shards,
        mesh=fine,
        in_specs=(
            P(None, None, FSDP, "z"),
            P(None, None, FSDP, "z"),
            P(None, None, "z", None),
            P(),
        ),
        out_specs=(
            P("z", None, FSDP, None),
            P("z", None, FSDP, None),
            P(None, None, "z", None),
        ),
        check_vma=False,
    )
```

```python
import functools
import math

import jax
import jax.numpy as jnp
from jax import lax
from jax.experimental import pallas as pl
from jax.experimental.pallas import tpu as pltpu
from jax.sharding import Mesh
from jax.sharding import PartitionSpec as P

D = 4096
HID = 1536
CAP = 2
EXPERTS = 10
GROUPS = 16
BLOCK = 96
RANK = 128

ridge_term = 0.001
feedback = 0.1
epsilon = 1e-06

F32 = jnp.float32
BF16 = jnp.bfloat16
HIGHEST = lax.Precision.HIGHEST
XY = ("x", "y")
FSDP = ("x", "y", "c")
SWAP = [(0, 1), (1, 0)]
VMEM = pl.BlockSpec(memory_space=pltpu.VMEM)
SMEM = pl.BlockSpec(memory_space=pltpu.SMEM)
ANY = pl.BlockSpec(memory_space=pl.ANY)


def call(body, outs, scratch=(), flops=0, specs=None, n_in=0):
    return pl.pallas_call(
        body,
        out_shape=outs,
        in_specs=specs if specs is not None else [VMEM] * n_in,
        out_specs=jax.tree.map(lambda _: VMEM, outs),
        scratch_shapes=list(scratch),
        compiler_params=pltpu.CompilerParams(vmem_limit_bytes=48 * 1024 * 1024),
        cost_estimate=pl.CostEstimate(flops=flops, bytes_accessed=4_000_000, transcendentals=0),
    )


def dot(a, b, contract=((1,), (0,)), precision=None):
    return lax.dot_general(
        a, b, (contract, ((), ())), precision=precision, preferred_element_type=F32
    )


def iota(shape, dim):
    return lax.broadcasted_iota(jnp.int32, shape, dim)


COUNT, WORK, SECOND, HELPER, WHERE, FREE, TABLE = 0, 17, 34, 51, 68, 80, 97
NONE = GROUPS


def fill_table(own, table):
    for g in range(GROUPS + 1):
        table[COUNT + g] = 0
        table[WORK + g] = EXPERTS
        table[SECOND + g] = EXPERTS
        table[HELPER + g] = 0
    for e in range(EXPERTS):
        g = own[e]
        p = table[COUNT + g]
        table[COUNT + g] = p + 1
        table[WORK + jnp.where(p == 0, g, NONE)] = e
        table[SECOND + jnp.where(p == 0, NONE, g)] = e
    free = jnp.int32(0)
    for g in range(GROUPS):
        table[FREE + free] = g
        free = free + jnp.where(table[COUNT + g] == 0, 1, 0)
    used = jnp.int32(0)
    for e in range(EXPERTS):
        g = own[e]
        second = table[SECOND + g] == e
        h = table[FREE + used]
        table[WORK + jnp.where(second, h, NONE)] = e
        table[HELPER + jnp.where(second, g, NONE)] = h
        table[WHERE + e] = jnp.where(second, h, g)
        used = used + jnp.where(second, 1, 0)


def slice_right(own, place, right, out, table, held):
    fill_table(own, table)
    f = place[0] * 8 + place[1] * 2 + place[2]
    pick = (iota((8, 192), 1) == iota((8, 192), 0) + 8 * f).astype(BF16)
    for e in range(EXPERTS):
        held[e] = dot(pick, right[e].reshape(192, RANK))
    held[EXPERTS] = jnp.zeros((8, RANK), F32)

    def group(g, _):
        pair = jnp.concatenate([held[table[WORK + g]], held[table[SECOND + g]]], axis=0)
        out[g] = pair.astype(BF16)
        return 0

    lax.fori_loop(0, GROUPS, group, 0)


def place_state(table, momentum, gradient, first, other):
    def slot(g, _):
        for base, out in ((WORK, first), (SECOND, other)):
            e = table[base + g]

            @pl.when(e < EXPERTS)
            def _():
                total = momentum[e].astype(F32) + gradient[e].astype(F32)
                out[g] = total.astype(BF16).reshape(192, 128)

            @pl.when(e >= EXPERTS)
            def _():
                out[g] = jnp.zeros((192, 128), BF16)

        return 0

    lax.fori_loop(0, GROUPS, slot, 0)


def offset(i):
    return jnp.where(i == 1, 3, jnp.where(i == 2, 1, jnp.where(i == 3, 2, 0)))


def join_matrix(place, core, relative, chips):
    col = iota((384, 16 * chips), 1)
    chip = col >> 4
    if relative:
        x = (place[0] + offset(chip & 3)) & 3
        y = (place[1] + offset(chip >> 2)) & 3
        chip = x * 4 + y
    f = chip * 2 + core
    target = ((col >> 3) & 1) * 192 + 8 * f + (col & 7)
    return ((iota((384, 16 * chips), 0) == target) & (f < 24)).astype(BF16)


def join_right(place, near, far, out, matrix):
    c = place[2]
    matrix[:, :256] = join_matrix(place, c, True, 16)
    matrix[:, 256:] = join_matrix(place, 1 - c, True, 16)

    def block(z, _):
        a = near[:, z].reshape(256, RANK)
        b = far[:, z].reshape(256, RANK)
        both = jnp.concatenate([a, b], axis=0)
        out[z] = dot(matrix[...], both).astype(BF16)
        return 0

    lax.fori_loop(0, GROUPS, block, 0, unroll=4)


def split3(value):
    high = value.astype(BF16)
    rest = value - high.astype(F32)
    middle = rest.astype(BF16)
    low = (rest - middle.astype(F32)).astype(BF16)
    return high, middle, low


def panel_of(state, right, kind, slot):
    def block(z, total):
        a = state[z, kind * BLOCK : (kind + 1) * BLOCK, :]
        b = right[z, pl.ds(slot * 192 + kind * BLOCK, BLOCK), :]
        return total + dot(a, b, ((0,), (0,)))

    return lax.fori_loop(0, GROUPS, block, jnp.zeros((128, RANK), F32), unroll=4)


def panels(place, state, right, panel, keep, send):
    grams = []
    for k in range(2):
        value = panel_of(state, right, k, 0)
        panel[k] = value
        grams.append(dot(value, value, ((0,), (0,)), HIGHEST))
    mine = place[2] == 0
    keep[...] = jnp.where(mine, grams[0], grams[1])
    send[...] = jnp.where(mine, grams[1], grams[0])


def second_panels(state, right, panel):
    for k in range(2):
        panel[k] = panel_of(state, right, k, 1)


def weigh(place, state, panel, keep, send, rows):
    weights = [jnp.concatenate(split3(panel[k]), axis=1) for k in range(2)]
    rows[192:, :] = jnp.zeros((64, RANK), F32)

    def block(z, _):
        for k in range(2):
            value = dot(state[z, k * BLOCK : (k + 1) * BLOCK, :], weights[k])
            total = value[:, :128] + (value[:, 128:256] + value[:, 256:])
            rows[k * BLOCK : (k + 1) * BLOCK, :] = total
        for i in range(16):
            near = pl.multiple_of(16 * i + 8 * place[2], 8)
            far = pl.multiple_of(16 * i + 8 - 8 * place[2], 8)
            keep[i, z] = rows[pl.ds(near, 8), :]
            send[i, z] = rows[pl.ds(far, 8), :]
        return 0

    lax.fori_loop(0, GROUPS, block, 0, unroll=4)


def invert(place, near, far, out, work, *, size):
    n = RANK
    eye = (iota((n, n), 0) == iota((n, n), 1)).astype(F32)
    mine = place[2] == 0
    first, other = near[...], far[...]
    work[0, :, :n] = jnp.where(mine, first, other) + ridge_term * eye
    work[1, :, :n] = jnp.where(mine, other, first) + ridge_term * eye
    for m in range(2):
        work[m, :, n:] = eye
    row = iota((size, 2 * n), 0)
    lane = iota((size, n), 1)
    for k in range(0, n, size):
        blocks = [work[m, k : k + size, :] for m in range(2)]
        for i in range(size):
            for m in range(2):
                b = blocks[m]
                scale = lax.rsqrt(b[i : i + 1, k + i : k + i + 1])
                line = b[i : i + 1, :] * scale
                column = jnp.where(row > i, b[:, k + i : k + i + 1] * scale, 0.0)
                blocks[m] = jnp.where(row == i, line, b - column * line)
        for m in range(2):
            b = blocks[m]
            out[m, k : k + size, :] = b[:, n:]
            if k + size < n:
                left = jnp.where(lane >= k + size, b[:, :n], 0.0)
                change = dot(left, b, ((0,), (0,)), HIGHEST)
                work[m, k + size :, :] -= change[k + size :, :]


def scale_factor(place, inverse, parts, _panel, _turned, mine, out):
    f = place[0] * 8 + place[1] * 2 + place[2]
    total = parts[0]
    for i in range(1, 16):
        total = total + parts[i]
    kind = jnp.where(f >= 12, 1, 0)
    factor = dot(total, inverse[kind], ((1,), (1,)), HIGHEST).astype(BF16)
    mine[...] = factor
    half = jnp.where(f >= 16, 1, 0)
    start = pl.multiple_of(8 * f - 128 * half, 8)
    rows = inverse[half, pl.ds(start, 8), :]
    high = rows.astype(BF16).astype(F32)
    both = jnp.concatenate([high, rows - high], axis=0).astype(BF16)
    for i in range(GROUPS):
        out[i, :128] = factor
        out[i, 128:] = both


def orthonormal(table, place, panel, inverse, left, low):
    owned = table[COUNT + place[3]] > 0
    for k in range(2):
        ortho = dot(panel[k], inverse[k], ((1,), (1,)), HIGHEST)
        ortho = jnp.where(owned, ortho, 0.0)
        left[k] = ortho * math.sqrt(D)
        low[k] = (ortho * (-feedback)).astype(BF16)


def turn(table, place, first, second, out):
    owned = table[COUNT + place[3]] > 0
    eye = (iota((128, 128), 0) == iota((128, 128), 1)).astype(BF16)
    some = jnp.where(owned, eye, jnp.zeros_like(eye))
    for s, (state, unit) in enumerate(((first, some), (second, eye))):
        for k in range(2):
            rows = state[:, k * BLOCK : (k + 1) * BLOCK, :].reshape(HID, 128)
            out[2 * s + k] = dot(unit, rows, ((1,), (1,))).astype(BF16)


ROWS = 240


def select(table, place, tiles, out, packed):
    z = place[3]
    packed[:144, :] = tiles[table[HELPER + z]]
    start = pl.multiple_of((z >> 1) * 16, 16)
    upper = (z & 1) == 1
    sums = []
    for e in range(0, EXPERTS, 2):
        pair = []
        for i in range(2):
            p = table[WHERE + e + i]
            value = tiles[p, pl.ds(start, 16), :].astype(F32)
            pair.append(jnp.where(upper, value[8:], value[:8]))
            whole = tiles[p, :128, :].astype(F32)
            sums.append(jnp.sum(whole * whole, axis=0, keepdims=True))
        packed[144 + e * 8 : 160 + e * 8, :] = jnp.concatenate(pair, axis=0).astype(BF16)
    sums.append(jnp.zeros((16 - EXPERTS, RANK), F32))
    packed[224:, :] = jnp.concatenate(sums, axis=0).astype(BF16)
    value = packed[...]
    for i in range(16):
        out[i] = value


def finish_right(place, near, far, out):
    c = place[2]
    matrix = jnp.concatenate(
        [join_matrix(place, c, False, 12), join_matrix(place, 1 - c, False, 12)], axis=1
    )
    parts = near[:, 224:, :].astype(F32) + far[:, 224:, :].astype(F32)
    sums = [jnp.sum(parts[6 * k : 6 * k + 6], axis=0) for k in range(2)]
    scales = [lax.rsqrt(s * (1.0 / HID) + epsilon) for s in sums]
    for g in range(EXPERTS // 2):
        rows = slice(144 + g * 16, 160 + g * 16)
        data = jnp.concatenate(
            [near[:12, rows, :].reshape(192, RANK), far[:12, rows, :].reshape(192, RANK)], axis=0
        )
        value = dot(matrix, data)
        for s in range(2):
            e = 2 * g + s
            for k in range(2):
                i = 2 * s + k
                out[e, k] = value[i * BLOCK : (i + 1) * BLOCK, :] * scales[k][e : e + 1, :]


def update(matrix, chips, near, far, wide):
    for g in range(8):
        rows = slice(g * 16, g * 16 + 16)
        data = jnp.concatenate(
            [part[:chips, rows, :].reshape(16 * chips, RANK) for part in (near, far)], axis=0
        )
        value = dot(matrix, data).astype(BF16)
        for p in range(2):
            for k in range(2):
                i = 2 * p + k
                first = (2 * g + p) * BLOCK
                wide[k, first : first + BLOCK, :] = value[i * BLOCK : (i + 1) * BLOCK]


def finish_first(place, turned, near, far, low, out, wide):
    c = place[2]
    matrix = jnp.concatenate(
        [join_matrix(place, c, True, 16), join_matrix(place, 1 - c, True, 16)], axis=1
    )
    update(matrix, 16, near, far, wide)
    for k in range(2):
        change = dot(low[k], wide[k], ((1,), (1,)))
        out[k] = (turned[k].astype(F32) + change).astype(BF16)


def finish_second(table, place, turned, near, far, first, panel, left, out, left_out, inverse, wide):
    c = place[2]
    matrix = jnp.concatenate(
        [join_matrix(place, c, False, 12), join_matrix(place, 1 - c, False, 12)], axis=1
    )
    for part, core in ((near, c), (far, 1 - c)):
        for chip in range(16):
            value = part[chip, 128:144, :].astype(F32)
            row = pl.multiple_of(16 * chip + 8 * core, 8)
            inverse[pl.ds(row, 8), :] = value[:8] + value[8:]
    some = table[SECOND + place[3]] < EXPERTS
    update(matrix, 12, near, far, wide)
    for k in range(2):
        ortho = dot(panel[k], inverse[k * RANK : (k + 1) * RANK, :], ((1,), (1,)), HIGHEST)
        ortho = jnp.where(some, ortho, 0.0)
        left_out[k] = left[k]
        left_out[2 + k] = ortho * math.sqrt(D)
        change = dot((ortho * (-feedback)).astype(BF16), wide[k], ((1,), (1,)))
        out[k] = first[k]
        out[2 + k] = (turned[2 + k].astype(F32) + change).astype(BF16)


def ring(shift):
    return [(i, (i + shift) % 4) for i in range(4)]


SHIFTS = (3, 1, 2)


def gather_slices(x):
    for axis in ("x", "y"):
        x = jnp.stack([x] + [lax.ppermute(x, axis, ring((4 - d) % 4)) for d in SHIFTS])
    x = x.reshape((16,) + x.shape[2:])
    return x, lax.ppermute(x, "c", SWAP)


def spread_sum(x, axis):
    parts = [lax.ppermute(x, axis, ring(d)) for d in SHIFTS]
    return (x + parts[0]) + (parts[1] + parts[2])


def exchange(x, axis):
    return lax.all_to_all(x, axis, split_axis=0, concat_axis=0, tiled=True)


def shards(momentum, gradient, right_in, owners):
    sds = jax.ShapeDtypeStruct
    barrier = lax.optimization_barrier
    place = jnp.stack([lax.axis_index(a) for a in ("x", "y", "c", "z")]).astype(jnp.int32)
    slices, table = pl.pallas_call(
        slice_right,
        out_shape=(sds((16, 16, RANK), BF16), sds((TABLE,), jnp.int32)),
        in_specs=[SMEM, SMEM, VMEM],
        out_specs=(VMEM, SMEM),
        scratch_shapes=[pltpu.VMEM((EXPERTS + 1, 8, RANK), F32)],
    )(owners, place, right_in)
    slices = exchange(slices, "z")
    block = sds((16, 192, 128), BF16)
    sent, late = call(place_state, (block, block), specs=[SMEM, VMEM, VMEM])(
        table, jnp.swapaxes(momentum, 2, 3), jnp.swapaxes(gradient, 2, 3)
    )
    sent, slices = barrier((sent, slices))
    state = exchange(sent, "z")
    near, far = gather_slices(slices)
    right = call(
        join_right,
        sds((16, 384, RANK), BF16),
        [pltpu.VMEM((384, 512), BF16)],
        flops=800_000_000,
        specs=[SMEM, VMEM, VMEM],
    )(place, near, far)
    square = sds((RANK, RANK), F32)
    two = sds((2, 128, RANK), F32)
    panel, keep, send = call(
        panels, (two, square, square), specs=[SMEM, VMEM, VMEM], flops=300_000_000
    )(place, state, right)
    late, send = barrier((late, send))
    second = exchange(late, "z")
    gram = keep + lax.ppermute(send, "c", SWAP)
    half = sds((16, 16, 8, RANK), F32)
    keep, send = call(
        weigh, (half, half), [pltpu.VMEM((256, RANK), F32)], specs=[SMEM, VMEM, VMEM], flops=400_000_000
    )(place, state, panel)
    gram = spread_sum(spread_sum(gram, "x"), "y")
    other = lax.ppermute(gram, "c", SWAP)
    parts = keep + lax.ppermute(send, "c", SWAP)
    parts = exchange(parts.reshape(16, 128, RANK), XY)
    inverse = call(
        functools.partial(invert, size=8),
        sds((2, RANK, RANK), F32),
        [pltpu.VMEM((2, RANK, 2 * RANK), F32)],
        specs=[SMEM, VMEM, VMEM],
        flops=4_000_000_000,
    )(place, gram, other)
    second_panel = call(second_panels, two, n_in=2, flops=200_000_000)(second, right)
    turned = call(
        turn, sds((4, 128, HID), BF16), specs=[SMEM, SMEM, VMEM, VMEM], flops=200_000_000
    )(table, place, state, second)
    mine, copies = call(
        scale_factor,
        (sds((128, RANK), BF16), sds((16, 144, RANK), BF16)),
        specs=[SMEM, VMEM, VMEM, ANY, ANY],
        flops=100_000_000,
    )(place, inverse, parts, second_panel, turned)
    tiles = exchange(copies, "z")
    left, low = call(
        orthonormal, (two, sds((2, 128, RANK), BF16)), specs=[SMEM, SMEM, VMEM, VMEM], flops=100_000_000
    )(table, place, panel, inverse)
    near, far = gather_slices(mine)
    first = call(
        finish_first,
        sds((2, 128, HID), BF16),
        [pltpu.VMEM((2, HID, RANK), BF16)],
        specs=[SMEM] + [VMEM] * 4,
        flops=600_000_000,
    )(place, turned, near, far, low)
    chosen = call(
        select,
        sds((16, ROWS, RANK), BF16),
        [pltpu.VMEM((ROWS, RANK), BF16)],
        specs=[SMEM, SMEM, VMEM],
    )(table, place, tiles)
    near = exchange(chosen, XY)
    far = lax.ppermute(near, "c", SWAP)
    right_out = call(
        finish_right, sds((EXPERTS, 2, BLOCK, RANK), F32), specs=[SMEM, VMEM, VMEM], flops=300_000_000
    )(place, near, far)
    state_out, left_out = call(
        finish_second,
        (sds((4, 128, HID), BF16), sds((4, 128, RANK), F32)),
        [pltpu.VMEM((2 * RANK, RANK), F32), pltpu.VMEM((2, HID, RANK), BF16)],
        specs=[SMEM, SMEM] + [VMEM] * 6,
        flops=600_000_000,
    )(table, place, turned, near, far, first, second_panel, left)
    return (
        state_out.reshape(CAP, 2, 128, HID),
        left_out.reshape(CAP, 2, 128, RANK),
        right_out,
    )


def solution(mesh):
    fine = Mesh(mesh.devices.reshape(4, 4, 2, 16), ("x", "y", "c", "z"))
    return jax.shard_map(
        shards,
        mesh=fine,
        in_specs=(
            P(None, None, FSDP, "z"),
            P(None, None, FSDP, "z"),
            P(None, None, "z", None),
            P(),
        ),
        out_specs=(
            P("z", None, FSDP, None),
            P("z", None, FSDP, None),
            P(None, None, "z", None),
        ),
        check_vma=False,
    )
```

```python
import functools
import math

import jax
import jax.numpy as jnp
from jax import lax
from jax.experimental import pallas as pl
from jax.experimental.pallas import tpu as pltpu
from jax.sharding import Mesh
from jax.sharding import PartitionSpec as P

D = 4096
HID = 1536
CAP = 2
EXPERTS = 10
GROUPS = 16
BLOCK = 96
RANK = 128

ridge_term = 0.001
feedback = 0.1
epsilon = 1e-06

F32 = jnp.float32
BF16 = jnp.bfloat16
HIGHEST = lax.Precision.HIGHEST
XY = ("x", "y")
FSDP = ("x", "y", "c")
SWAP = [(0, 1), (1, 0)]
VMEM = pl.BlockSpec(memory_space=pltpu.VMEM)
SMEM = pl.BlockSpec(memory_space=pltpu.SMEM)
ANY = pl.BlockSpec(memory_space=pl.ANY)


def call(body, outs, scratch=(), flops=0, specs=None, n_in=0):
    return pl.pallas_call(
        body,
        out_shape=outs,
        in_specs=specs if specs is not None else [VMEM] * n_in,
        out_specs=jax.tree.map(lambda _: VMEM, outs),
        scratch_shapes=list(scratch),
        compiler_params=pltpu.CompilerParams(vmem_limit_bytes=48 * 1024 * 1024),
        cost_estimate=pl.CostEstimate(flops=flops, bytes_accessed=4_000_000, transcendentals=0),
    )


def dot(a, b, contract=((1,), (0,)), precision=None):
    return lax.dot_general(
        a, b, (contract, ((), ())), precision=precision, preferred_element_type=F32
    )


def iota(shape, dim):
    return lax.broadcasted_iota(jnp.int32, shape, dim)


COUNT, WORK, SECOND, HELPER, WHERE, FREE, SLOT, LIST, TABLE = 0, 17, 34, 51, 68, 80, 97, 114, 128
SECONDS = EXPERTS // 2
NONE = GROUPS


def fill_table(own, table):
    for g in range(GROUPS + 1):
        table[COUNT + g] = 0
        table[WORK + g] = EXPERTS
        table[SECOND + g] = EXPERTS
        table[HELPER + g] = 0
        table[SLOT + g] = 0
    for j in range(TABLE - LIST):
        table[LIST + j] = EXPERTS
    for e in range(EXPERTS):
        g = own[e]
        p = table[COUNT + g]
        table[COUNT + g] = p + 1
        table[WORK + jnp.where(p == 0, g, NONE)] = e
        table[SECOND + jnp.where(p == 0, NONE, g)] = e
    free = jnp.int32(0)
    for g in range(GROUPS):
        table[FREE + free] = g
        free = free + jnp.where(table[COUNT + g] == 0, 1, 0)
    used = jnp.int32(0)
    for e in range(EXPERTS):
        g = own[e]
        second = table[SECOND + g] == e
        h = table[FREE + used]
        table[WORK + jnp.where(second, h, NONE)] = e
        table[HELPER + jnp.where(second, g, NONE)] = h
        table[WHERE + e] = jnp.where(second, h, g)
        table[SLOT + jnp.where(second, g, NONE)] = used
        table[LIST + jnp.where(second, used, SECONDS)] = e
        used = used + jnp.where(second, 1, 0)


def slice_right(own, place, right, out, table, held):
    fill_table(own, table)
    f = place[0] * 8 + place[1] * 2 + place[2]
    pick = (iota((8, 192), 1) == iota((8, 192), 0) + 8 * f).astype(BF16)
    for e in range(EXPERTS):
        held[e] = dot(pick, right[e].reshape(192, RANK))
    held[EXPERTS] = jnp.zeros((8, RANK), F32)

    def group(g, _):
        pair = jnp.concatenate([held[table[WORK + g]], held[table[SECOND + g]]], axis=0)
        out[g] = pair.astype(BF16)
        return 0

    lax.fori_loop(0, GROUPS, group, 0)


def place_state(table, momentum, gradient, first, other):
    def put(out, i, e):
        @pl.when(e < EXPERTS)
        def _():
            total = momentum[e].astype(F32) + gradient[e].astype(F32)
            out[i] = total.astype(BF16).reshape(192, 128)

        @pl.when(e >= EXPERTS)
        def _():
            out[i] = jnp.zeros((192, 128), BF16)

    def slot(g, _):
        put(first, g, table[WORK + g])
        return 0

    lax.fori_loop(0, GROUPS, slot, 0)
    for j in range(SECONDS):
        put(other, j, table[LIST + j])


def offset(i):
    return jnp.where(i == 1, 3, jnp.where(i == 2, 1, jnp.where(i == 3, 2, 0)))


def join_matrix(place, core, relative, chips):
    col = iota((384, 16 * chips), 1)
    chip = col >> 4
    if relative:
        x = (place[0] + offset(chip & 3)) & 3
        y = (place[1] + offset(chip >> 2)) & 3
        chip = x * 4 + y
    f = chip * 2 + core
    target = ((col >> 3) & 1) * 192 + 8 * f + (col & 7)
    return ((iota((384, 16 * chips), 0) == target) & (f < 24)).astype(BF16)


def join_right(place, near, far, out, matrix):
    c = place[2]
    matrix[:, :256] = join_matrix(place, c, True, 16)
    matrix[:, 256:] = join_matrix(place, 1 - c, True, 16)

    def block(z, _):
        a = near[:, z].reshape(256, RANK)
        b = far[:, z].reshape(256, RANK)
        both = jnp.concatenate([a, b], axis=0)
        out[z] = dot(matrix[...], both).astype(BF16)
        return 0

    lax.fori_loop(0, GROUPS, block, 0, unroll=4)


def split3(value):
    high = value.astype(BF16)
    rest = value - high.astype(F32)
    middle = rest.astype(BF16)
    low = (rest - middle.astype(F32)).astype(BF16)
    return high, middle, low


def panel_of(block_of, right, kind, slot):
    def block(z, total):
        b = right[z, pl.ds(slot * 192 + kind * BLOCK, BLOCK), :]
        return total + dot(block_of(z), b, ((0,), (0,)))

    return lax.fori_loop(0, GROUPS, block, jnp.zeros((128, RANK), F32), unroll=4)


def panels(state, right, panel, gram):
    for k in range(2):
        rows = slice(k * BLOCK, (k + 1) * BLOCK)
        value = panel_of(lambda z: state[z, rows, :], right, k, 0)
        panel[k] = value
        gram[k] = dot(value, value, ((0,), (0,)), HIGHEST)


def unit():
    return (iota((128, 128), 0) == iota((128, 128), 1)).astype(BF16)


def second_panels(table, place, state, right, panel, turned):
    some = table[SECOND + place[3]] < EXPERTS
    eye = jnp.where(some, unit(), jnp.zeros((128, 128), BF16))
    for k in range(2):
        rows = slice(k * BLOCK, (k + 1) * BLOCK)
        panel[k] = panel_of(lambda z: state[z, 0, rows, :], right, k, 1)
        whole = state[:, 0, rows, :].reshape(HID, 128)
        turned[k] = dot(eye, whole, ((1,), (1,))).astype(BF16)


def weigh(place, state, panel, keep, send, rows):
    weights = [jnp.concatenate(split3(panel[k]), axis=1) for k in range(2)]
    rows[192:, :] = jnp.zeros((64, RANK), F32)

    def block(z, _):
        for k in range(2):
            value = dot(state[z, k * BLOCK : (k + 1) * BLOCK, :], weights[k])
            total = value[:, :128] + (value[:, 128:256] + value[:, 256:])
            rows[k * BLOCK : (k + 1) * BLOCK, :] = total
        for i in range(16):
            near = pl.multiple_of(16 * i + 8 * place[2], 8)
            far = pl.multiple_of(16 * i + 8 - 8 * place[2], 8)
            keep[i, z] = rows[pl.ds(near, 8), :]
            send[i, z] = rows[pl.ds(far, 8), :]
        return 0

    lax.fori_loop(0, GROUPS, block, 0, unroll=4)


def invert(gram, out, work, *, size):
    n = RANK
    eye = (iota((n, n), 0) == iota((n, n), 1)).astype(F32)
    for m in range(2):
        work[m, :, :n] = gram[m] + ridge_term * eye
    for m in range(2):
        work[m, :, n:] = eye
    row = iota((size, 2 * n), 0)
    lane = iota((size, n), 1)
    for k in range(0, n, size):
        blocks = [work[m, k : k + size, :] for m in range(2)]
        for i in range(size):
            for m in range(2):
                b = blocks[m]
                scale = lax.rsqrt(b[i : i + 1, k + i : k + i + 1])
                line = b[i : i + 1, :] * scale
                column = jnp.where(row > i, b[:, k + i : k + i + 1] * scale, 0.0)
                blocks[m] = jnp.where(row == i, line, b - column * line)
        for m in range(2):
            b = blocks[m]
            out[m, k : k + size, :] = b[:, n:]
            if k + size < n:
                left = jnp.where(lane >= k + size, b[:, :n], 0.0)
                change = dot(left, b, ((0,), (0,)), HIGHEST)
                work[m, k + size :, :] -= change[k + size :, :]


def scale_factor(place, inverse, parts, out):
    f = place[0] * 8 + place[1] * 2 + place[2]
    total = parts[0]
    for i in range(1, 16):
        total = total + parts[i]
    kind = jnp.where(f >= 12, 1, 0)
    out[:128] = dot(total, inverse[kind], ((1,), (1,)), HIGHEST).astype(BF16)
    half = jnp.where(f >= 16, 1, 0)
    start = pl.multiple_of(8 * f - 128 * half, 8)
    rows = inverse[half, pl.ds(start, 8), :]
    high = rows.astype(BF16).astype(F32)
    out[128:] = jnp.concatenate([high, rows - high], axis=0).astype(BF16)


def orthonormal(table, place, panel, inverse, left, low):
    owned = table[COUNT + place[3]] > 0
    for k in range(2):
        ortho = dot(panel[k], inverse[k], ((1,), (1,)), HIGHEST)
        ortho = jnp.where(owned, ortho, 0.0)
        left[k] = ortho * math.sqrt(D)
        low[k] = (ortho * (-feedback)).astype(BF16)


def turn(table, place, state, out):
    owned = table[COUNT + place[3]] > 0
    eye = jnp.where(owned, unit(), jnp.zeros((128, 128), BF16))
    for k in range(2):
        rows = state[:, k * BLOCK : (k + 1) * BLOCK, :].reshape(HID, 128)
        out[k] = dot(eye, rows, ((1,), (1,))).astype(BF16)


ROWS = 368


def select(table, place, mine, tiles, _, out, packed):
    z = place[3]
    packed[:128, :] = mine[:128, :]
    packed[128:272, :] = tiles[table[HELPER + z]]
    start = pl.multiple_of((z >> 1) * 16, 16)
    upper = (z & 1) == 1
    sums = []
    for e in range(0, EXPERTS, 2):
        pair = []
        for i in range(2):
            p = table[WHERE + e + i]
            value = tiles[p, pl.ds(start, 16), :].astype(F32)
            pair.append(jnp.where(upper, value[8:], value[:8]))
            whole = tiles[p, :128, :].astype(F32)
            sums.append(jnp.sum(whole * whole, axis=0, keepdims=True))
        packed[272 + e * 8 : 288 + e * 8, :] = jnp.concatenate(pair, axis=0).astype(BF16)
    sums.append(jnp.zeros((16 - EXPERTS, RANK), F32))
    packed[352:, :] = jnp.concatenate(sums, axis=0).astype(BF16)
    value = packed[...]
    for i in range(16):
        out[i] = value


def finish_right(place, near, far, out):
    c = place[2]
    matrix = jnp.concatenate(
        [join_matrix(place, c, False, 12), join_matrix(place, 1 - c, False, 12)], axis=1
    )
    parts = near[:, 352:, :].astype(F32) + far[:, 352:, :].astype(F32)
    sums = [jnp.sum(parts[6 * k : 6 * k + 6], axis=0) for k in range(2)]
    scales = [lax.rsqrt(s * (1.0 / HID) + epsilon) for s in sums]
    for g in range(EXPERTS // 2):
        rows = slice(272 + g * 16, 288 + g * 16)
        data = jnp.concatenate(
            [near[:12, rows, :].reshape(192, RANK), far[:12, rows, :].reshape(192, RANK)], axis=0
        )
        value = dot(matrix, data)
        for s in range(2):
            e = 2 * g + s
            for k in range(2):
                i = 2 * s + k
                out[e, k] = value[i * BLOCK : (i + 1) * BLOCK, :] * scales[k][e : e + 1, :]


def finish_state(
    table, place, turned, second, near, far, low, panel, left, out, left_out, inverse, wide
):
    c = place[2]
    matrix = jnp.concatenate(
        [join_matrix(place, c, False, 12), join_matrix(place, 1 - c, False, 12)], axis=1
    )
    for part, core in ((near, c), (far, 1 - c)):
        for chip in range(16):
            value = part[chip, 256:272, :].astype(F32)
            row = pl.multiple_of(16 * chip + 8 * core, 8)
            inverse[pl.ds(row, 8), :] = value[:8] + value[8:]
    some = table[SECOND + place[3]] < EXPERTS
    lows = [low[0], low[1]]
    for k in range(2):
        ortho = dot(panel[k], inverse[k * RANK : (k + 1) * RANK, :], ((1,), (1,)), HIGHEST)
        ortho = jnp.where(some, ortho, 0.0)
        left_out[k] = left[k]
        left_out[2 + k] = ortho * math.sqrt(D)
        lows.append((ortho * (-feedback)).astype(BF16))
    for s, state in enumerate((turned, second)):
        for g in range(8):
            rows = slice(s * 128 + g * 16, s * 128 + g * 16 + 16)
            data = jnp.concatenate(
                [near[:12, rows, :].reshape(192, RANK), far[:12, rows, :].reshape(192, RANK)],
                axis=0,
            )
            value = dot(matrix, data).astype(BF16)
            for p in range(2):
                for k in range(2):
                    i = 2 * p + k
                    first = (2 * g + p) * BLOCK
                    wide[2 * s + k, first : first + BLOCK, :] = value[i * BLOCK : (i + 1) * BLOCK]
        for k in range(2):
            change = dot(lows[2 * s + k], wide[2 * s + k], ((1,), (1,)))
            out[2 * s + k] = (state[k].astype(F32) + change).astype(BF16)


def ring(shift):
    return [(i, (i + shift) % 4) for i in range(4)]


SHIFTS = (3, 1, 2)


def gather_slices(x):
    for axis in ("x", "y"):
        x = jnp.stack([x] + [lax.ppermute(x, axis, ring((4 - d) % 4)) for d in SHIFTS])
    x = x.reshape((16,) + x.shape[2:])
    return x, lax.ppermute(x, "c", SWAP)


def exchange(x, axis):
    return lax.all_to_all(x, axis, split_axis=0, concat_axis=0, tiled=True)


def shards(momentum, gradient, right_in, owners):
    sds = jax.ShapeDtypeStruct
    barrier = lax.optimization_barrier
    place = jnp.stack([lax.axis_index(a) for a in ("x", "y", "c", "z")]).astype(jnp.int32)
    slices, table = pl.pallas_call(
        slice_right,
        out_shape=(sds((16, 16, RANK), BF16), sds((TABLE,), jnp.int32)),
        in_specs=[SMEM, SMEM, VMEM],
        out_specs=(VMEM, SMEM),
        scratch_shapes=[pltpu.VMEM((EXPERTS + 1, 8, RANK), F32)],
    )(owners, place, right_in)
    slices = exchange(slices, "z")
    sent, late = call(
        place_state,
        (sds((16, 192, 128), BF16), sds((SECONDS, 192, 128), BF16)),
        specs=[SMEM, VMEM, VMEM],
    )(table, jnp.swapaxes(momentum, 2, 3), jnp.swapaxes(gradient, 2, 3))
    sent, slices = barrier((sent, slices))
    state = exchange(sent, "z")
    near, far = gather_slices(slices)
    right = call(
        join_right,
        sds((16, 384, RANK), BF16),
        [pltpu.VMEM((384, 512), BF16)],
        flops=800_000_000,
        specs=[SMEM, VMEM, VMEM],
    )(place, near, far)
    late, state = barrier((late, state))
    seconds = lax.all_gather(late, "z")
    square = sds((2, RANK, RANK), F32)
    two = sds((2, 128, RANK), F32)
    panel, gram = call(panels, (two, square), n_in=2, flops=300_000_000)(state, right)
    gram = exchange(gram.reshape(32, 8, RANK), FSDP)
    half = sds((16, 16, 8, RANK), F32)
    keep, send = call(
        weigh, (half, half), [pltpu.VMEM((256, RANK), F32)], specs=[SMEM, VMEM, VMEM], flops=400_000_000
    )(place, state, panel)
    parts = keep + lax.ppermute(send, "c", SWAP)
    gram = jnp.broadcast_to(jnp.sum(gram, axis=0)[None], gram.shape)
    gram = exchange(gram, FSDP).reshape(2, RANK, RANK)
    parts, gram = barrier((parts, gram))
    parts = exchange(parts.reshape(16, 128, RANK), XY)
    inverse = call(
        functools.partial(invert, size=8),
        square,
        [pltpu.VMEM((2, RANK, 2 * RANK), F32)],
        n_in=1,
        flops=4_000_000_000,
    )(gram)
    mine = call(scale_factor, sds((144, RANK), BF16), specs=[SMEM, VMEM, VMEM], flops=100_000_000)(
        place, inverse, parts
    )
    turned = call(turn, sds((2, 128, HID), BF16), specs=[SMEM, SMEM, VMEM], flops=100_000_000)(
        table, place, state
    )
    left, low = call(
        orthonormal, (two, sds((2, 128, RANK), BF16)), specs=[SMEM, SMEM, VMEM, VMEM], flops=100_000_000
    )(table, place, panel, inverse)
    tiles = lax.all_gather(mine, "z")
    second_panel, second_turned = pl.pallas_call(
        second_panels,
        grid_spec=pltpu.PrefetchScalarGridSpec(
            num_scalar_prefetch=2,
            grid=(1,),
            in_specs=[
                pl.BlockSpec((16, 1, 192, 128), lambda i, t, p: (0, t[SLOT + p[3]], 0, 0)),
                pl.BlockSpec((16, 384, RANK), lambda i, t, p: (0, 0, 0)),
            ],
            out_specs=[
                pl.BlockSpec((2, 128, RANK), lambda i, t, p: (0, 0, 0)),
                pl.BlockSpec((2, 128, HID), lambda i, t, p: (0, 0, 0)),
            ],
        ),
        out_shape=[two, sds((2, 128, HID), BF16)],
        compiler_params=pltpu.CompilerParams(vmem_limit_bytes=24 * 1024 * 1024),
        cost_estimate=pl.CostEstimate(flops=300_000_000, bytes_accessed=3_000_000, transcendentals=0),
    )(table, place, seconds, right)
    chosen = call(
        select,
        sds((16, ROWS, RANK), BF16),
        [pltpu.VMEM((ROWS, RANK), BF16)],
        specs=[SMEM, SMEM, VMEM, VMEM, ANY],
    )(table, place, mine, tiles, seconds)
    near = exchange(chosen, XY)
    far = lax.ppermute(near, "c", SWAP)
    right_out = call(
        finish_right, sds((EXPERTS, 2, BLOCK, RANK), F32), specs=[SMEM, VMEM, VMEM], flops=300_000_000
    )(place, near, far)
    state_out, left_out = call(
        finish_state,
        (sds((4, 128, HID), BF16), sds((4, 128, RANK), F32)),
        [pltpu.VMEM((2 * RANK, RANK), F32), pltpu.VMEM((4, HID, RANK), BF16)],
        specs=[SMEM, SMEM] + [VMEM] * 7,
        flops=1_200_000_000,
    )(table, place, turned, second_turned, near, far, low, second_panel, left)
    return (
        state_out.reshape(CAP, 2, 128, HID),
        left_out.reshape(CAP, 2, 128, RANK),
        right_out,
    )


def solution(mesh):
    fine = Mesh(mesh.devices.reshape(4, 4, 2, 16), ("x", "y", "c", "z"))
    return jax.shard_map(
        shards,
        mesh=fine,
        in_specs=(
            P(None, None, FSDP, "z"),
            P(None, None, FSDP, "z"),
            P(None, None, "z", None),
            P(),
        ),
        out_specs=(
            P("z", None, FSDP, None),
            P("z", None, FSDP, None),
            P(None, None, "z", None),
        ),
        check_vma=False,
    )
```

```python
import functools
import math

import jax
import jax.numpy as jnp
from jax import lax
from jax.experimental import pallas as pl
from jax.experimental.pallas import tpu as pltpu
from jax.sharding import Mesh
from jax.sharding import PartitionSpec as P

D = 4096
HID = 1536
CAP = 2
EXPERTS = 10
GROUPS = 16
BLOCK = 96
RANK = 128

ridge_term = 0.001
feedback = 0.1
epsilon = 1e-06

F32 = jnp.float32
BF16 = jnp.bfloat16
HIGHEST = lax.Precision.HIGHEST
XY = ("x", "y")
FSDP = ("x", "y", "c")
SWAP = [(0, 1), (1, 0)]
VMEM = pl.BlockSpec(memory_space=pltpu.VMEM)
SMEM = pl.BlockSpec(memory_space=pltpu.SMEM)
ANY = pl.BlockSpec(memory_space=pl.ANY)
HBM = pl.BlockSpec(memory_space=pltpu.HBM)


def call(body, outs, scratch=(), flops=0, specs=None, n_in=0):
    return pl.pallas_call(
        body,
        out_shape=outs,
        in_specs=specs if specs is not None else [VMEM] * n_in,
        out_specs=jax.tree.map(lambda _: VMEM, outs),
        scratch_shapes=list(scratch),
        compiler_params=pltpu.CompilerParams(vmem_limit_bytes=48 * 1024 * 1024),
        cost_estimate=pl.CostEstimate(flops=flops, bytes_accessed=4_000_000, transcendentals=0),
    )


def dot(a, b, contract=((1,), (0,)), precision=None):
    return lax.dot_general(
        a, b, (contract, ((), ())), precision=precision, preferred_element_type=F32
    )


def iota(shape, dim):
    return lax.broadcasted_iota(jnp.int32, shape, dim)


COUNT, WORK, SECOND, HELPER, WHERE, FREE, SLOT, LIST, TABLE = 0, 17, 34, 51, 68, 80, 97, 114, 128
SECONDS = EXPERTS // 2
NONE = GROUPS


def fill_table(own, table):
    for g in range(GROUPS + 1):
        table[COUNT + g] = 0
        table[WORK + g] = EXPERTS
        table[SECOND + g] = EXPERTS
        table[HELPER + g] = 0
        table[SLOT + g] = 0
    for j in range(TABLE - LIST):
        table[LIST + j] = EXPERTS
    for e in range(EXPERTS):
        g = own[e]
        p = table[COUNT + g]
        table[COUNT + g] = p + 1
        table[WORK + jnp.where(p == 0, g, NONE)] = e
        table[SECOND + jnp.where(p == 0, NONE, g)] = e
    free = jnp.int32(0)
    for g in range(GROUPS):
        table[FREE + free] = g
        free = free + jnp.where(table[COUNT + g] == 0, 1, 0)
    used = jnp.int32(0)
    for e in range(EXPERTS):
        g = own[e]
        second = table[SECOND + g] == e
        h = table[FREE + used]
        table[WORK + jnp.where(second, h, NONE)] = e
        table[HELPER + jnp.where(second, g, NONE)] = h
        table[WHERE + e] = jnp.where(second, h, g)
        table[SLOT + jnp.where(second, g, NONE)] = used
        table[LIST + jnp.where(second, used, SECONDS)] = e
        used = used + jnp.where(second, 1, 0)


def slice_right(own, place, right, out, table, held):
    fill_table(own, table)
    f = place[0] * 8 + place[1] * 2 + place[2]
    pick = (iota((8, 192), 1) == iota((8, 192), 0) + 8 * f).astype(BF16)
    for e in range(EXPERTS):
        held[e] = dot(pick, right[e].reshape(192, RANK))
    held[EXPERTS] = jnp.zeros((8, RANK), F32)

    def group(g, _):
        pair = jnp.concatenate([held[table[WORK + g]], held[table[SECOND + g]]], axis=0)
        out[g] = pair.astype(BF16)
        return 0

    lax.fori_loop(0, GROUPS, group, 0)


def place_state(table, momentum, gradient, first, other):
    def put(out, i, e):
        @pl.when(e < EXPERTS)
        def _():
            total = momentum[e].astype(F32) + gradient[e].astype(F32)
            out[i] = total.astype(BF16).reshape(192, 128)

        @pl.when(e >= EXPERTS)
        def _():
            out[i] = jnp.zeros((192, 128), BF16)

    def slot(g, _):
        put(first, g, table[WORK + g])
        return 0

    lax.fori_loop(0, GROUPS, slot, 0)
    for j in range(SECONDS):
        put(other, j, table[LIST + j])


def offset(i):
    return jnp.where(i == 1, 3, jnp.where(i == 2, 1, jnp.where(i == 3, 2, 0)))


def join_matrix(place, core, relative, chips):
    col = iota((384, 16 * chips), 1)
    chip = col >> 4
    if relative:
        x = (place[0] + offset(chip & 3)) & 3
        y = (place[1] + offset(chip >> 2)) & 3
        chip = x * 4 + y
    f = chip * 2 + core
    target = ((col >> 3) & 1) * 192 + 8 * f + (col & 7)
    return ((iota((384, 16 * chips), 0) == target) & (f < 24)).astype(BF16)


def join_right(place, near, far, out, matrix):
    c = place[2]
    matrix[:, :256] = join_matrix(place, c, True, 16)
    matrix[:, 256:] = join_matrix(place, 1 - c, True, 16)

    def block(z, _):
        a = near[:, z].reshape(256, RANK)
        b = far[:, z].reshape(256, RANK)
        both = jnp.concatenate([a, b], axis=0)
        out[z] = dot(matrix[...], both).astype(BF16)
        return 0

    lax.fori_loop(0, GROUPS, block, 0, unroll=4)


def split3(value):
    high = value.astype(BF16)
    rest = value - high.astype(F32)
    middle = rest.astype(BF16)
    low = (rest - middle.astype(F32)).astype(BF16)
    return high, middle, low


def panel_of(block_of, right, kind, slot):
    def block(z, total):
        b = right[z, pl.ds(slot * 192 + kind * BLOCK, BLOCK), :]
        return total + dot(block_of(z), b, ((0,), (0,)))

    return lax.fori_loop(0, GROUPS, block, jnp.zeros((128, RANK), F32), unroll=4)


def panels(state, right, panel, gram):
    for k in range(2):
        rows = slice(k * BLOCK, (k + 1) * BLOCK)
        value = panel_of(lambda z: state[z, rows, :], right, k, 0)
        panel[k] = value
        gram[k] = dot(value, value, ((0,), (0,)), HIGHEST)


def unit():
    return (iota((128, 128), 0) == iota((128, 128), 1)).astype(BF16)


def second_panels(table, place, state, right, panel, turned):
    some = table[SECOND + place[3]] < EXPERTS
    eye = jnp.where(some, unit(), jnp.zeros((128, 128), BF16))
    for k in range(2):
        rows = slice(k * BLOCK, (k + 1) * BLOCK)
        panel[k] = panel_of(lambda z: state[z, 0, rows, :], right, k, 1)
        whole = state[:, 0, rows, :].reshape(HID, 128)
        turned[k] = dot(eye, whole, ((1,), (1,))).astype(BF16)


def weigh(place, state, panel, _, keep, send, rows):
    weights = [jnp.concatenate(split3(panel[k]), axis=1) for k in range(2)]
    rows[192:, :] = jnp.zeros((64, RANK), F32)

    def block(z, _):
        for k in range(2):
            value = dot(state[z, k * BLOCK : (k + 1) * BLOCK, :], weights[k])
            total = value[:, :128] + (value[:, 128:256] + value[:, 256:])
            rows[k * BLOCK : (k + 1) * BLOCK, :] = total
        for i in range(16):
            near = pl.multiple_of(16 * i + 8 * place[2], 8)
            far = pl.multiple_of(16 * i + 8 - 8 * place[2], 8)
            keep[i, z] = rows[pl.ds(near, 8), :]
            send[i, z] = rows[pl.ds(far, 8), :]
        return 0

    lax.fori_loop(0, GROUPS, block, 0, unroll=4)


def invert(gram, out, work, *, size):
    n = RANK
    eye = (iota((n, n), 0) == iota((n, n), 1)).astype(F32)
    for m in range(2):
        work[m, :, :n] = gram[m] + ridge_term * eye
    for m in range(2):
        work[m, :, n:] = eye
    row = iota((size, 2 * n), 0)
    lane = iota((size, n), 1)
    for k in range(0, n, size):
        blocks = [work[m, k : k + size, :] for m in range(2)]
        for i in range(size):
            for m in range(2):
                b = blocks[m]
                scale = lax.rsqrt(b[i : i + 1, k + i : k + i + 1])
                line = b[i : i + 1, :] * scale
                column = jnp.where(row > i, b[:, k + i : k + i + 1] * scale, 0.0)
                blocks[m] = jnp.where(row == i, line, b - column * line)
        for m in range(2):
            b = blocks[m]
            out[m, k : k + size, :] = b[:, n:]
            if k + size < n:
                left = jnp.where(lane >= k + size, b[:, :n], 0.0)
                change = dot(left, b, ((0,), (0,)), HIGHEST)
                work[m, k + size :, :] -= change[k + size :, :]


def scale_factor(place, inverse, parts, out):
    f = place[0] * 8 + place[1] * 2 + place[2]
    total = parts[0]
    for i in range(1, 16):
        total = total + parts[i]
    kind = jnp.where(f >= 12, 1, 0)
    out[:128] = dot(total, inverse[kind], ((1,), (1,)), HIGHEST).astype(BF16)
    half = jnp.where(f >= 16, 1, 0)
    start = pl.multiple_of(8 * f - 128 * half, 8)
    rows = inverse[half, pl.ds(start, 8), :]
    high = rows.astype(BF16).astype(F32)
    out[128:] = jnp.concatenate([high, rows - high], axis=0).astype(BF16)


def orthonormal(table, place, panel, inverse, left, low):
    owned = table[COUNT + place[3]] > 0
    for k in range(2):
        ortho = dot(panel[k], inverse[k], ((1,), (1,)), HIGHEST)
        ortho = jnp.where(owned, ortho, 0.0)
        left[k] = ortho * math.sqrt(D)
        low[k] = (ortho * (-feedback)).astype(BF16)


def turn(table, place, state, out):
    owned = table[COUNT + place[3]] > 0
    eye = jnp.where(owned, unit(), jnp.zeros((128, 128), BF16))
    for k in range(2):
        rows = state[:, k * BLOCK : (k + 1) * BLOCK, :].reshape(HID, 128)
        out[k] = dot(eye, rows, ((1,), (1,))).astype(BF16)


ROWS = 368


def select(table, place, mine, tiles, _, out, packed):
    z = place[3]
    packed[:128, :] = mine[:128, :]
    packed[128:272, :] = tiles[table[HELPER + z]]
    start = pl.multiple_of((z >> 1) * 16, 16)
    upper = (z & 1) == 1
    sums = []
    for e in range(0, EXPERTS, 2):
        pair = []
        for i in range(2):
            p = table[WHERE + e + i]
            value = tiles[p, pl.ds(start, 16), :].astype(F32)
            pair.append(jnp.where(upper, value[8:], value[:8]))
            whole = tiles[p, :128, :].astype(F32)
            sums.append(jnp.sum(whole * whole, axis=0, keepdims=True))
        packed[272 + e * 8 : 288 + e * 8, :] = jnp.concatenate(pair, axis=0).astype(BF16)
    sums.append(jnp.zeros((16 - EXPERTS, RANK), F32))
    packed[352:, :] = jnp.concatenate(sums, axis=0).astype(BF16)
    value = packed[...]
    for i in range(16):
        out[i] = value


def finish_right(place, near, far, out):
    c = place[2]
    matrix = jnp.concatenate(
        [join_matrix(place, c, False, 12), join_matrix(place, 1 - c, False, 12)], axis=1
    )
    parts = near[:, 352:, :].astype(F32) + far[:, 352:, :].astype(F32)
    sums = [jnp.sum(parts[6 * k : 6 * k + 6], axis=0) for k in range(2)]
    scales = [lax.rsqrt(s * (1.0 / HID) + epsilon) for s in sums]
    for g in range(EXPERTS // 2):
        rows = slice(272 + g * 16, 288 + g * 16)
        data = jnp.concatenate(
            [near[:12, rows, :].reshape(192, RANK), far[:12, rows, :].reshape(192, RANK)], axis=0
        )
        value = dot(matrix, data)
        for s in range(2):
            e = 2 * g + s
            for k in range(2):
                i = 2 * s + k
                out[e, k] = value[i * BLOCK : (i + 1) * BLOCK, :] * scales[k][e : e + 1, :]


def finish_state(
    table, place, turned, second, near, far, low, panel, left, out, left_out, inverse, wide
):
    c = place[2]
    matrix = jnp.concatenate(
        [join_matrix(place, c, False, 12), join_matrix(place, 1 - c, False, 12)], axis=1
    )
    for part, core in ((near, c), (far, 1 - c)):
        for chip in range(16):
            value = part[chip, 256:272, :].astype(F32)
            row = pl.multiple_of(16 * chip + 8 * core, 8)
            inverse[pl.ds(row, 8), :] = value[:8] + value[8:]
    some = table[SECOND + place[3]] < EXPERTS
    lows = [low[0], low[1]]
    for k in range(2):
        ortho = dot(panel[k], inverse[k * RANK : (k + 1) * RANK, :], ((1,), (1,)), HIGHEST)
        ortho = jnp.where(some, ortho, 0.0)
        left_out[k] = left[k]
        left_out[2 + k] = ortho * math.sqrt(D)
        lows.append((ortho * (-feedback)).astype(BF16))
    for s, state in enumerate((turned, second)):
        for g in range(8):
            rows = slice(s * 128 + g * 16, s * 128 + g * 16 + 16)
            data = jnp.concatenate(
                [near[:12, rows, :].reshape(192, RANK), far[:12, rows, :].reshape(192, RANK)],
                axis=0,
            )
            value = dot(matrix, data).astype(BF16)
            for p in range(2):
                for k in range(2):
                    i = 2 * p + k
                    first = (2 * g + p) * BLOCK
                    wide[2 * s + k, first : first + BLOCK, :] = value[i * BLOCK : (i + 1) * BLOCK]
        for k in range(2):
            change = dot(lows[2 * s + k], wide[2 * s + k], ((1,), (1,)))
            out[2 * s + k] = (state[k].astype(F32) + change).astype(BF16)


def ring(shift):
    return [(i, (i + shift) % 4) for i in range(4)]


SHIFTS = (3, 1, 2)


def gather_slices(x):
    for axis in ("x", "y"):
        x = jnp.stack([x] + [lax.ppermute(x, axis, ring((4 - d) % 4)) for d in SHIFTS])
    x = x.reshape((16,) + x.shape[2:])
    return x, lax.ppermute(x, "c", SWAP)


def exchange(x, axis):
    return lax.all_to_all(x, axis, split_axis=0, concat_axis=0, tiled=True)


def shards(momentum, gradient, right_in, owners):
    sds = jax.ShapeDtypeStruct
    barrier = lax.optimization_barrier
    place = jnp.stack([lax.axis_index(a) for a in ("x", "y", "c", "z")]).astype(jnp.int32)
    slices, table = pl.pallas_call(
        slice_right,
        out_shape=(sds((16, 16, RANK), BF16), sds((TABLE,), jnp.int32)),
        in_specs=[SMEM, SMEM, VMEM],
        out_specs=(VMEM, SMEM),
        scratch_shapes=[pltpu.VMEM((EXPERTS + 1, 8, RANK), F32)],
    )(owners, place, right_in)
    slices = exchange(slices, "z")
    sent, late = call(
        place_state,
        (sds((16, 192, 128), BF16), sds((SECONDS, 192, 128), BF16)),
        specs=[SMEM, VMEM, VMEM],
    )(table, jnp.swapaxes(momentum, 2, 3), jnp.swapaxes(gradient, 2, 3))
    sent, slices = barrier((sent, slices))
    state = exchange(sent, "z")
    near, far = gather_slices(slices)
    right = call(
        join_right,
        sds((16, 384, RANK), BF16),
        [pltpu.VMEM((384, 512), BF16)],
        flops=800_000_000,
        specs=[SMEM, VMEM, VMEM],
    )(place, near, far)
    square = sds((2, RANK, RANK), F32)
    two = sds((2, 128, RANK), F32)
    panel, gram = call(panels, (two, square), n_in=2, flops=300_000_000)(state, right)
    late, gram = barrier((late, gram))
    seconds = lax.all_gather(late, "z")
    gram = jnp.sum(exchange(gram.reshape(32, 8, RANK), FSDP), axis=0)
    half = sds((16, 16, 8, RANK), F32)
    keep, send = call(
        weigh, (half, half), [pltpu.VMEM((256, RANK), F32)], specs=[SMEM, VMEM, VMEM, ANY], flops=400_000_000
    )(place, state, panel, gram)
    parts = keep + lax.ppermute(send, "c", SWAP)
    gram = exchange(jnp.broadcast_to(gram[None], (32, 8, RANK)), FSDP).reshape(2, RANK, RANK)
    parts, gram = barrier((parts, gram))
    parts = exchange(parts.reshape(16, 128, RANK), XY)
    inverse = call(
        functools.partial(invert, size=8),
        square,
        [pltpu.VMEM((2, RANK, 2 * RANK), F32)],
        n_in=1,
        flops=4_000_000_000,
    )(gram)
    mine = call(scale_factor, sds((144, RANK), BF16), specs=[SMEM, VMEM, VMEM], flops=100_000_000)(
        place, inverse, parts
    )
    turned = call(turn, sds((2, 128, HID), BF16), specs=[SMEM, SMEM, VMEM], flops=100_000_000)(
        table, place, state
    )
    left, low = call(
        orthonormal, (two, sds((2, 128, RANK), BF16)), specs=[SMEM, SMEM, VMEM, VMEM], flops=100_000_000
    )(table, place, panel, inverse)
    tiles = lax.all_gather(mine, "z")
    second_panel, second_turned = pl.pallas_call(
        second_panels,
        grid_spec=pltpu.PrefetchScalarGridSpec(
            num_scalar_prefetch=2,
            grid=(1,),
            in_specs=[
                pl.BlockSpec((16, 1, 192, 128), lambda i, t, p: (0, t[SLOT + p[3]], 0, 0)),
                pl.BlockSpec((16, 384, RANK), lambda i, t, p: (0, 0, 0)),
            ],
            out_specs=[
                pl.BlockSpec((2, 128, RANK), lambda i, t, p: (0, 0, 0)),
                pl.BlockSpec((2, 128, HID), lambda i, t, p: (0, 0, 0)),
            ],
        ),
        out_shape=[two, sds((2, 128, HID), BF16)],
        compiler_params=pltpu.CompilerParams(vmem_limit_bytes=24 * 1024 * 1024),
        cost_estimate=pl.CostEstimate(flops=300_000_000, bytes_accessed=3_000_000, transcendentals=0),
    )(table, place, seconds, right)
    chosen = call(
        select,
        sds((16, ROWS, RANK), BF16),
        [pltpu.VMEM((ROWS, RANK), BF16)],
        specs=[SMEM, SMEM, VMEM, VMEM, HBM],
    )(table, place, mine, tiles, seconds)
    near = exchange(chosen, XY)
    near, turned, low, left, second_panel, second_turned = barrier(
        (near, turned, low, left, second_panel, second_turned)
    )
    far = lax.ppermute(near, "c", SWAP)
    right_out = call(
        finish_right, sds((EXPERTS, 2, BLOCK, RANK), F32), specs=[SMEM, VMEM, VMEM], flops=300_000_000
    )(place, near, far)
    state_out, left_out = call(
        finish_state,
        (sds((4, 128, HID), BF16), sds((4, 128, RANK), F32)),
        [pltpu.VMEM((2 * RANK, RANK), F32), pltpu.VMEM((4, HID, RANK), BF16)],
        specs=[SMEM, SMEM] + [VMEM] * 7,
        flops=1_200_000_000,
    )(table, place, turned, second_turned, near, far, low, second_panel, left)
    return (
        state_out.reshape(CAP, 2, 128, HID),
        left_out.reshape(CAP, 2, 128, RANK),
        right_out,
    )


def solution(mesh):
    fine = Mesh(mesh.devices.reshape(4, 4, 2, 16), ("x", "y", "c", "z"))
    return jax.shard_map(
        shards,
        mesh=fine,
        in_specs=(
            P(None, None, FSDP, "z"),
            P(None, None, FSDP, "z"),
            P(None, None, "z", None),
            P(),
        ),
        out_specs=(
            P("z", None, FSDP, None),
            P("z", None, FSDP, None),
            P(None, None, "z", None),
        ),
        check_vma=False,
    )
```

```python
import functools
import math

import jax
import jax.numpy as jnp
from jax import lax
from jax.experimental import pallas as pl
from jax.experimental.pallas import tpu as pltpu
from jax.sharding import Mesh
from jax.sharding import PartitionSpec as P

D = 4096
HID = 1536
CAP = 2
EXPERTS = 10
GROUPS = 16
BLOCK = 96
RANK = 128

ridge_term = 0.001
feedback = 0.1
epsilon = 1e-06

F32 = jnp.float32
BF16 = jnp.bfloat16
HIGHEST = lax.Precision.HIGHEST
XY = ("x", "y")
FSDP = ("x", "y", "c")
SWAP = [(0, 1), (1, 0)]
VMEM = pl.BlockSpec(memory_space=pltpu.VMEM)
SMEM = pl.BlockSpec(memory_space=pltpu.SMEM)
ANY = pl.BlockSpec(memory_space=pl.ANY)


def call(body, outs, scratch=(), flops=0, specs=None, n_in=0):
    return pl.pallas_call(
        body,
        out_shape=outs,
        in_specs=specs if specs is not None else [VMEM] * n_in,
        out_specs=jax.tree.map(lambda _: VMEM, outs),
        scratch_shapes=list(scratch),
        compiler_params=pltpu.CompilerParams(vmem_limit_bytes=16 * 1024 * 1024),
        cost_estimate=pl.CostEstimate(flops=flops, bytes_accessed=4_000_000, transcendentals=0),
    )


def dot(a, b, contract=((1,), (0,)), precision=None):
    return lax.dot_general(
        a, b, (contract, ((), ())), precision=precision, preferred_element_type=F32
    )


def iota(shape, dim):
    return lax.broadcasted_iota(jnp.int32, shape, dim)


COUNT, WORK, SECOND, HELPER, WHERE, FREE, SLOT, LIST, TABLE = 0, 17, 34, 51, 68, 80, 97, 114, 128
SECONDS = EXPERTS // 2
NONE = GROUPS


def fill_table(own, table):
    for g in range(GROUPS + 1):
        table[COUNT + g] = 0
        table[WORK + g] = EXPERTS
        table[SECOND + g] = EXPERTS
        table[HELPER + g] = 0
        table[SLOT + g] = 0
    for j in range(TABLE - LIST):
        table[LIST + j] = EXPERTS
    for e in range(EXPERTS):
        g = own[e]
        p = table[COUNT + g]
        table[COUNT + g] = p + 1
        table[WORK + jnp.where(p == 0, g, NONE)] = e
        table[SECOND + jnp.where(p == 0, NONE, g)] = e
    free = jnp.int32(0)
    for g in range(GROUPS):
        table[FREE + free] = g
        free = free + jnp.where(table[COUNT + g] == 0, 1, 0)
    used = jnp.int32(0)
    for e in range(EXPERTS):
        g = own[e]
        second = table[SECOND + g] == e
        h = table[FREE + used]
        table[WORK + jnp.where(second, h, NONE)] = e
        table[HELPER + jnp.where(second, g, NONE)] = h
        table[WHERE + e] = jnp.where(second, h, g)
        table[SLOT + jnp.where(second, g, NONE)] = used
        table[LIST + jnp.where(second, used, SECONDS)] = e
        used = used + jnp.where(second, 1, 0)


def slice_right(own, place, right, out, table, held):
    fill_table(own, table)
    f = place[0] * 8 + place[1] * 2 + place[2]
    pick = (iota((8, 192), 1) == iota((8, 192), 0) + 8 * f).astype(BF16)
    for e in range(EXPERTS):
        held[e] = dot(pick, right[e].reshape(192, RANK))
    held[EXPERTS] = jnp.zeros((8, RANK), F32)

    def group(g, _):
        pair = jnp.concatenate([held[table[WORK + g]], held[table[SECOND + g]]], axis=0)
        out[g] = pair.astype(BF16)
        return 0

    lax.fori_loop(0, GROUPS, group, 0)


def place_state(table, momentum, gradient, first, other):
    def put(out, i, e):
        @pl.when(e < EXPERTS)
        def _():
            total = momentum[e].astype(F32) + gradient[e].astype(F32)
            out[i] = total.astype(BF16).reshape(192, 128)

        @pl.when(e >= EXPERTS)
        def _():
            out[i] = jnp.zeros((192, 128), BF16)

    def slot(g, _):
        put(first, g, table[WORK + g])
        return 0

    lax.fori_loop(0, GROUPS, slot, 0)
    for j in range(SECONDS):
        put(other, j, table[LIST + j])


def offset(i):
    return jnp.where(i == 1, 3, jnp.where(i == 2, 1, jnp.where(i == 3, 2, 0)))


def join_matrix(place, core, relative, chips):
    col = iota((384, 16 * chips), 1)
    chip = col >> 4
    if relative:
        x = (place[0] + offset(chip & 3)) & 3
        y = (place[1] + offset(chip >> 2)) & 3
        chip = x * 4 + y
    f = chip * 2 + core
    target = ((col >> 3) & 1) * 192 + 8 * f + (col & 7)
    return ((iota((384, 16 * chips), 0) == target) & (f < 24)).astype(BF16)


def join_right(place, near, far, out, matrix):
    c = place[2]
    matrix[:, :256] = join_matrix(place, c, True, 16)
    matrix[:, 256:] = join_matrix(place, 1 - c, True, 16)

    def block(z, _):
        a = near[:, z].reshape(256, RANK)
        b = far[:, z].reshape(256, RANK)
        both = jnp.concatenate([a, b], axis=0)
        out[z] = dot(matrix[...], both).astype(BF16)
        return 0

    lax.fori_loop(0, GROUPS, block, 0, unroll=4)


def split3(value):
    high = value.astype(BF16)
    rest = value - high.astype(F32)
    middle = rest.astype(BF16)
    low = (rest - middle.astype(F32)).astype(BF16)
    return high, middle, low


def panel_of(block_of, right, kind, slot):
    def block(z, total):
        b = right[z, pl.ds(slot * 192 + kind * BLOCK, BLOCK), :]
        return total + dot(block_of(z), b, ((0,), (0,)))

    return lax.fori_loop(0, GROUPS, block, jnp.zeros((128, RANK), F32), unroll=4)


def panels(state, right, panel, gram):
    for k in range(2):
        rows = slice(k * BLOCK, (k + 1) * BLOCK)
        value = panel_of(lambda z: state[z, rows, :], right, k, 0)
        panel[k] = value
        gram[k] = dot(value, value, ((0,), (0,)), HIGHEST)


def unit():
    return (iota((128, 128), 0) == iota((128, 128), 1)).astype(BF16)


def second_panels(table, place, states, right, panel, turned, state, arrived):
    copy = pltpu.make_async_copy(states.at[:, table[SLOT + place[3]]], state, arrived)
    copy.start()
    some = table[SECOND + place[3]] < EXPERTS
    eye = jnp.where(some, unit(), jnp.zeros((128, 128), BF16))
    copy.wait()
    for k in range(2):
        rows = slice(k * BLOCK, (k + 1) * BLOCK)
        panel[k] = panel_of(lambda z: state[z, rows, :], right, k, 1)
        whole = state[:, rows, :].reshape(HID, 128)
        turned[k] = dot(eye, whole, ((1,), (1,))).astype(BF16)


def tile_of(x, y, core, q):
    return 8 * (x - jnp.where(x > q, 1, 0)) + 2 * y + core


def place_of(x, z):
    q = z & 3
    return 3 * (z >> 2) + q - jnp.where(q > x, 1, 0)


def row_kinds(place):
    m = iota((96, RANK), 0) >> 3
    v = m - 3 * ((m * 11) >> 5)
    q = v + jnp.where(v >= place[0], 1, 0)
    return jnp.where(tile_of(place[0], place[1], place[2], q) >= 12, 1, 0)


def weigh(place, state, panel, _, keep, send, rows):
    weights = [jnp.concatenate(split3(panel[k]), axis=1) for k in range(2)]

    def block(g, _):
        for q in range(4):
            z = 4 * g + q
            for k in range(2):
                value = dot(state[z, k * BLOCK : (k + 1) * BLOCK, :], weights[k])
                total = value[:, :128] + (value[:, 128:256] + value[:, 256:])
                rows[q, k * BLOCK : (k + 1) * BLOCK, :] = total
            for x in range(4):
                if x == q:
                    continue
                m = 3 * g + q - int(q > x)
                for y in range(4):
                    first = 64 * (x - int(x > q)) + 16 * y
                    near = pl.multiple_of(first + 8 * place[2], 8)
                    far = pl.multiple_of(first + 8 - 8 * place[2], 8)
                    keep[4 * x + y, m] = rows[q, pl.ds(near, 8), :]
                    send[4 * x + y, m] = rows[q, pl.ds(far, 8), :]
        return 0

    lax.fori_loop(0, 4, block, 0)


def invert(gram, out, work, *, size):
    n = RANK
    eye = (iota((n, n), 0) == iota((n, n), 1)).astype(F32)
    for m in range(2):
        work[m, :, :n] = gram[m] + ridge_term * eye
    for m in range(2):
        work[m, :, n:] = eye
    row = iota((size, 2 * n), 0)
    lane = iota((size, n), 1)
    for k in range(0, n, size):
        blocks = [work[m, k : k + size, :] for m in range(2)]
        for i in range(size):
            for m in range(2):
                b = blocks[m]
                scale = lax.rsqrt(b[i : i + 1, k + i : k + i + 1])
                line = b[i : i + 1, :] * scale
                column = jnp.where(row > i, b[:, k + i : k + i + 1] * scale, 0.0)
                blocks[m] = jnp.where(row == i, line, b - column * line)
        for m in range(2):
            b = blocks[m]
            out[m, k : k + size, :] = b[:, n:]
            if k + size < n:
                left = jnp.where(lane >= k + size, b[:, :n], 0.0)
                change = dot(left, b, ((0,), (0,)), HIGHEST)
                work[m, k + size :, :] -= change[k + size :, :]


def scale_factor(place, inverse, parts, out):
    f = place[0] * 8 + place[1] * 2 + place[2]
    total = parts[0]
    for i in range(1, 16):
        total = total + parts[i]
    both = [dot(total, inverse[k], ((1,), (1,)), HIGHEST) for k in range(2)]
    out[:96] = jnp.where(row_kinds(place) == 0, both[0], both[1]).astype(BF16)
    half = jnp.where(f >= 16, 1, 0)
    start = pl.multiple_of(8 * f - 128 * half, 8)
    rows = inverse[half, pl.ds(start, 8), :]
    high = rows.astype(BF16).astype(F32)
    out[96:] = jnp.concatenate([high, rows - high], axis=0).astype(BF16)


def orthonormal(table, place, panel, inverse, left, low):
    owned = table[COUNT + place[3]] > 0
    for k in range(2):
        ortho = dot(panel[k], inverse[k], ((1,), (1,)), HIGHEST)
        ortho = jnp.where(owned, ortho, 0.0)
        left[k] = ortho * math.sqrt(D)
        low[k] = (ortho * (-feedback)).astype(BF16)


def turn(table, place, state, out):
    owned = table[COUNT + place[3]] > 0
    eye = jnp.where(owned, unit(), jnp.zeros((128, 128), BF16))
    for k in range(2):
        rows = state[:, k * BLOCK : (k + 1) * BLOCK, :].reshape(HID, 128)
        out[k] = dot(eye, rows, ((1,), (1,))).astype(BF16)


SECOND_ROWS, RIGHT_ROWS, SUM_ROWS, ROWS = 96, 208, 288, 320


def select(table, place, mine, tiles, out, packed):
    z = place[3]
    packed[:SECOND_ROWS, :] = mine[:96, :]
    packed[SECOND_ROWS:RIGHT_ROWS, :] = tiles[table[HELPER + z]]
    m = place_of(place[0], z)
    start = pl.multiple_of((m >> 1) * 16, 16)
    upper = (m & 1) == 1
    kinds = row_kinds(place)
    sums = []
    for e in range(0, EXPERTS, 2):
        pair = []
        for i in range(2):
            p = table[WHERE + e + i]
            value = tiles[p, pl.ds(start, 16), :].astype(F32)
            pair.append(jnp.where(upper, value[8:], value[:8]))
            whole = tiles[p, :96, :].astype(F32)
            square = whole * whole
            for k in range(2):
                sums.append(jnp.sum(jnp.where(kinds == k, square, 0.0), axis=0, keepdims=True))
        first = RIGHT_ROWS + e * 8
        packed[first : first + 16, :] = jnp.concatenate(pair, axis=0).astype(BF16)
    sums.append(jnp.zeros((ROWS - SUM_ROWS - 2 * EXPERTS, RANK), F32))
    packed[SUM_ROWS:, :] = jnp.concatenate(sums, axis=0).astype(BF16)
    value = packed[...]
    for i in range(16):
        out[i] = value


def finish_right(place, near, far, out, blocks):
    q = place[3] & 3
    parts = near[:, SUM_ROWS:, :].astype(F32) + far[:, SUM_ROWS:, :].astype(F32)
    scale = lax.rsqrt(jnp.sum(parts, axis=0) * (1.0 / HID) + epsilon)
    for part, core in ((near, place[2]), (far, 1 - place[2])):
        for chip in range(16):
            x, y = chip // 4, chip % 4
            t = jnp.where(q == x, 24, tile_of(x, y, core, q))
            row = pl.ds(pl.multiple_of(8 * t, 8), 8)
            for e in range(0, EXPERTS, 2):
                first = RIGHT_ROWS + e * 8
                value = part[chip, first : first + 16, :].astype(F32)
                blocks[e, row, :] = value[:8]
                blocks[e + 1, row, :] = value[8:]
    for e in range(EXPERTS):
        for k in range(2):
            rows = slice(k * BLOCK, (k + 1) * BLOCK)
            out[e, k] = blocks[e, rows, :] * scale[2 * e + k : 2 * e + k + 1, :]


def finish_state(
    table, place, turned, second, near, far, low, panel, left, out, left_out, inverse, factor
):
    for part, core in ((near, place[2]), (far, 1 - place[2])):
        for chip in range(16):
            x, y = chip // 4, chip % 4
            value = part[chip, SECOND_ROWS + 96 : SECOND_ROWS + 112, :].astype(F32)
            row = pl.multiple_of(16 * chip + 8 * core, 8)
            inverse[pl.ds(row, 8), :] = value[:8] + value[8:]
            for s in range(2):
                for g in range(6):
                    first = s * SECOND_ROWS + 16 * g
                    value = part[chip, first : first + 16, :].astype(F32)
                    for i in range(2):
                        m = 2 * g + i
                        v = m % 3
                        q = v + int(v >= x)
                        t = 8 * (x - int(x > q)) + 2 * y
                        base = (4 * (m // 3) + q) * BLOCK + 8 * (t % 12)
                        row = pl.ds(pl.multiple_of(base + 8 * core, 8), 8)
                        factor[2 * s + t // 12, row, :] = value[8 * i : 8 * i + 8]
    some = table[SECOND + place[3]] < EXPERTS
    lows = [low[0], low[1]]
    for k in range(2):
        ortho = dot(panel[k], inverse[k * RANK : (k + 1) * RANK, :], ((1,), (1,)), HIGHEST)
        ortho = jnp.where(some, ortho, 0.0)
        left_out[k] = left[k]
        left_out[2 + k] = ortho * math.sqrt(D)
        lows.append((ortho * (-feedback)).astype(BF16))
    for s, state in enumerate((turned, second)):
        for k in range(2):
            i = 2 * s + k
            change = dot(lows[i], factor[i].astype(BF16), ((1,), (1,)))
            out[i] = (state[k].astype(F32) + change).astype(BF16)


def ring(shift):
    return [(i, (i + shift) % 4) for i in range(4)]


SHIFTS = (3, 1, 2)


def gather_slices(x):
    for axis in ("x", "y"):
        x = jnp.stack([x] + [lax.ppermute(x, axis, ring((4 - d) % 4)) for d in SHIFTS])
    x = x.reshape((16,) + x.shape[2:])
    return x, lax.ppermute(x, "c", SWAP)


def exchange(x, axis):
    return lax.all_to_all(x, axis, split_axis=0, concat_axis=0, tiled=True)


def shards(momentum, gradient, right_in, owners):
    sds = jax.ShapeDtypeStruct
    barrier = lax.optimization_barrier
    place = jnp.stack([lax.axis_index(a) for a in ("x", "y", "c", "z")]).astype(jnp.int32)
    slices, table = pl.pallas_call(
        slice_right,
        out_shape=(sds((16, 16, RANK), BF16), sds((TABLE,), jnp.int32)),
        in_specs=[SMEM, SMEM, VMEM],
        out_specs=(VMEM, SMEM),
        scratch_shapes=[pltpu.VMEM((EXPERTS + 1, 8, RANK), F32)],
    )(owners, place, right_in)
    slices = exchange(slices, "z")
    sent, late = call(
        place_state,
        (sds((16, 192, 128), BF16), sds((SECONDS, 192, 128), BF16)),
        specs=[SMEM, VMEM, VMEM],
    )(table, jnp.swapaxes(momentum, 2, 3), jnp.swapaxes(gradient, 2, 3))
    sent, slices = barrier((sent, slices))
    state = exchange(sent, "z")
    near, far = gather_slices(slices)
    right = call(
        join_right,
        sds((16, 384, RANK), BF16),
        [pltpu.VMEM((384, 512), BF16)],
        flops=800_000_000,
        specs=[SMEM, VMEM, VMEM],
    )(place, near, far)
    square = sds((2, RANK, RANK), F32)
    two = sds((2, 128, RANK), F32)
    panel, gram = call(panels, (two, square), n_in=2, flops=300_000_000)(state, right)
    late, gram = barrier((late, gram))
    seconds = lax.all_gather(late, "z")
    gram = jnp.sum(exchange(gram.reshape(32, 8, RANK), FSDP), axis=0)
    half = sds((16, 12, 8, RANK), F32)
    keep, send = call(
        weigh, (half, half), [pltpu.VMEM((4, 192, RANK), F32)], specs=[SMEM, VMEM, VMEM, ANY], flops=400_000_000
    )(place, state, panel, gram)
    parts = keep + lax.ppermute(send, "c", SWAP)
    gram = exchange(jnp.broadcast_to(gram[None], (32, 8, RANK)), FSDP).reshape(2, RANK, RANK)
    parts, gram = barrier((parts, gram))
    parts = exchange(parts.reshape(16, 96, RANK), XY)
    inverse = call(
        functools.partial(invert, size=32),
        square,
        [pltpu.VMEM((2, RANK, 2 * RANK), F32)],
        n_in=1,
        flops=4_000_000_000,
    )(gram)
    mine = call(scale_factor, sds((112, RANK), BF16), specs=[SMEM, VMEM, VMEM], flops=100_000_000)(
        place, inverse, parts
    )
    turned = call(turn, sds((2, 128, HID), BF16), specs=[SMEM, SMEM, VMEM], flops=100_000_000)(
        table, place, state
    )
    left, low = call(
        orthonormal, (two, sds((2, 128, RANK), BF16)), specs=[SMEM, SMEM, VMEM, VMEM], flops=100_000_000
    )(table, place, panel, inverse)
    tiles = lax.all_gather(mine, "z")
    second_panel, second_turned = call(
        second_panels,
        (two, sds((2, 128, HID), BF16)),
        [pltpu.VMEM((16, 192, 128), BF16), pltpu.SemaphoreType.DMA],
        specs=[SMEM, SMEM, ANY, VMEM],
        flops=300_000_000,
    )(table, place, seconds, right)
    chosen = call(
        select,
        sds((16, ROWS, RANK), BF16),
        [pltpu.VMEM((ROWS, RANK), BF16)],
        specs=[SMEM, SMEM, VMEM, VMEM],
    )(table, place, mine, tiles)
    near = exchange(chosen, XY)
    near, turned, low, left, second_panel, second_turned = barrier(
        (near, turned, low, left, second_panel, second_turned)
    )
    far = lax.ppermute(near, "c", SWAP)
    right_out = call(
        finish_right, sds((EXPERTS, 2, BLOCK, RANK), F32), [pltpu.VMEM((EXPERTS, 200, RANK), F32)],
        specs=[SMEM, VMEM, VMEM], flops=1_000_000
    )(place, near, far)
    state_out, left_out = call(
        finish_state,
        (sds((4, 128, HID), BF16), sds((4, 128, RANK), F32)),
        [pltpu.VMEM((2 * RANK, RANK), F32), pltpu.VMEM((4, HID, RANK), F32)],
        specs=[SMEM, SMEM] + [VMEM] * 7,
        flops=1_200_000_000,
    )(table, place, turned, second_turned, near, far, low, second_panel, left)
    return (
        state_out.reshape(CAP, 2, 128, HID),
        left_out.reshape(CAP, 2, 128, RANK),
        right_out,
    )


def solution(mesh):
    fine = Mesh(mesh.devices.reshape(4, 4, 2, 16), ("x", "y", "c", "z"))
    return jax.shard_map(
        shards,
        mesh=fine,
        in_specs=(
            P(None, None, FSDP, "z"),
            P(None, None, FSDP, "z"),
            P(None, None, "z", None),
            P(),
        ),
        out_specs=(
            P("z", None, FSDP, None),
            P("z", None, FSDP, None),
            P(None, None, "z", None),
        ),
        check_vma=False,
    )
```

```python
import functools
import math

import jax
import jax.numpy as jnp
from jax import lax
from jax.experimental import pallas as pl
from jax.experimental.pallas import tpu as pltpu
from jax.sharding import Mesh
from jax.sharding import PartitionSpec as P

D = 4096
HID = 1536
CAP = 2
EXPERTS = 10
GROUPS = 16
BLOCK = 96
RANK = 128

ridge_term = 0.001
feedback = 0.1
epsilon = 1e-06

F32 = jnp.float32
BF16 = jnp.bfloat16
HIGHEST = lax.Precision.HIGHEST
XY = ("x", "y")
FSDP = ("x", "y", "c")
SWAP = [(0, 1), (1, 0)]
VMEM = pl.BlockSpec(memory_space=pltpu.VMEM)
SMEM = pl.BlockSpec(memory_space=pltpu.SMEM)
ANY = pl.BlockSpec(memory_space=pl.ANY)


def call(body, outs, scratch=(), flops=0, specs=None, n_in=0):
    return pl.pallas_call(
        body,
        out_shape=outs,
        in_specs=specs if specs is not None else [VMEM] * n_in,
        out_specs=jax.tree.map(lambda _: VMEM, outs),
        scratch_shapes=list(scratch),
        compiler_params=pltpu.CompilerParams(vmem_limit_bytes=16 * 1024 * 1024),
        cost_estimate=pl.CostEstimate(flops=flops, bytes_accessed=4_000_000, transcendentals=0),
    )


def dot(a, b, contract=((1,), (0,)), precision=None):
    return lax.dot_general(
        a, b, (contract, ((), ())), precision=precision, preferred_element_type=F32
    )


def iota(shape, dim):
    return lax.broadcasted_iota(jnp.int32, shape, dim)


COUNT, WORK, SECOND, HELPER, WHERE, BUSY, SLOT, VIA = 0, 17, 34, 51, 68, 80, 97, 114
LIST, USED, GOOD, TABLE = 131, 140, 141, 142
SECONDS = EXPERTS // 2
NONE = GROUPS
STEPS = (1, -1, 2, -2, 3, -3, 4, -4, 5, -5, 6, -6, 7, -7, 8)
NEAR = 6


def fill_table(own, table):
    for g in range(GROUPS + 1):
        for base in (COUNT, HELPER, BUSY, SLOT, VIA):
            table[base + g] = 0
        table[WORK + g] = EXPERTS
        table[SECOND + g] = EXPERTS
    for j in range(SECONDS):
        table[LIST + j] = EXPERTS
    table[USED] = 0
    table[GOOD] = 1
    for e in range(EXPERTS):
        g = own[e]
        p = table[COUNT + g]
        table[COUNT + g] = p + 1
        table[BUSY + g] = 1
        table[WORK + jnp.where(p == 0, g, NONE)] = e
        table[SECOND + jnp.where(p == 0, NONE, g)] = e
        table[WHERE + e] = g
    for e in range(EXPERTS):
        g = own[e]

        @pl.when(table[SECOND + g] == e)
        def _():
            h, via = jnp.int32(-1), jnp.int32(0)
            for j, step in enumerate(STEPS):
                other = (g + step) & (GROUPS - 1)
                take = (h < 0) & (table[BUSY + other] == 0)
                h, via = jnp.where(take, other, h), jnp.where(take, j, via)
            table[BUSY + h] = 1
            table[WORK + h] = e
            table[HELPER + g] = h
            table[WHERE + e] = h
            table[VIA + g] = via
            table[GOOD] = jnp.where(via < NEAR, table[GOOD], 0)
            used = table[USED]
            table[SLOT + g] = used
            table[LIST + used] = e
            table[USED] = used + 1


def slice_right(own, place, right, out, table, held):
    fill_table(own, table)
    f = place[0] * 8 + place[1] * 2 + place[2]
    pick = (iota((8, 192), 1) == iota((8, 192), 0) + 8 * f).astype(BF16)
    for e in range(EXPERTS):
        held[e] = dot(pick, right[e].reshape(192, RANK))
    held[EXPERTS] = jnp.zeros((8, RANK), F32)

    def group(g, _):
        pair = jnp.concatenate([held[table[WORK + g]], held[table[SECOND + g]]], axis=0)
        out[g] = pair.astype(BF16)
        return 0

    lax.fori_loop(0, GROUPS, group, 0)


def place_state(table, momentum, gradient, first, other):
    def put(out, i, e):
        @pl.when(e < EXPERTS)
        def _():
            total = momentum[e].astype(F32) + gradient[e].astype(F32)
            out[i] = total.astype(BF16).reshape(192, 128)

        @pl.when(e >= EXPERTS)
        def _():
            out[i] = jnp.zeros((192, 128), BF16)

    def slot(g, _):
        put(first, g, table[WORK + g])
        return 0

    lax.fori_loop(0, GROUPS, slot, 0)
    for j in range(SECONDS):
        put(other, j, table[LIST + j])


def offset(i):
    return jnp.where(i == 1, 3, jnp.where(i == 2, 1, jnp.where(i == 3, 2, 0)))


def join_matrix(place, core, relative, chips):
    col = iota((384, 16 * chips), 1)
    chip = col >> 4
    if relative:
        x = (place[0] + offset(chip & 3)) & 3
        y = (place[1] + offset(chip >> 2)) & 3
        chip = x * 4 + y
    f = chip * 2 + core
    target = ((col >> 3) & 1) * 192 + 8 * f + (col & 7)
    return ((iota((384, 16 * chips), 0) == target) & (f < 24)).astype(BF16)


def join_right(place, near, far, out, matrix):
    c = place[2]
    matrix[:, :256] = join_matrix(place, c, True, 16)
    matrix[:, 256:] = join_matrix(place, 1 - c, True, 16)

    def block(z, _):
        a = near[:, z].reshape(256, RANK)
        b = far[:, z].reshape(256, RANK)
        both = jnp.concatenate([a, b], axis=0)
        out[z] = dot(matrix[...], both).astype(BF16)
        return 0

    lax.fori_loop(0, GROUPS, block, 0, unroll=4)


def split3(value):
    high = value.astype(BF16)
    rest = value - high.astype(F32)
    middle = rest.astype(BF16)
    low = (rest - middle.astype(F32)).astype(BF16)
    return high, middle, low


def panel_of(block_of, right, kind, slot):
    def block(z, total):
        b = right[z, pl.ds(slot * 192 + kind * BLOCK, BLOCK), :]
        return total + dot(block_of(z), b, ((0,), (0,)))

    return lax.fori_loop(0, GROUPS, block, jnp.zeros((128, RANK), F32), unroll=4)


def panels(state, right, panel, gram):
    for k in range(2):
        rows = slice(k * BLOCK, (k + 1) * BLOCK)
        value = panel_of(lambda z: state[z, rows, :], right, k, 0)
        panel[k] = value
        gram[k] = dot(value, value, ((0,), (0,)), HIGHEST)


def unit():
    return (iota((128, 128), 0) == iota((128, 128), 1)).astype(BF16)


def second_panels(table, place, states, right, panel, turned, state, arrived):
    copy = pltpu.make_async_copy(states.at[:, table[SLOT + place[3]]], state, arrived)
    copy.start()
    some = table[SECOND + place[3]] < EXPERTS
    eye = jnp.where(some, unit(), jnp.zeros((128, 128), BF16))
    copy.wait()
    for k in range(2):
        rows = slice(k * BLOCK, (k + 1) * BLOCK)
        panel[k] = panel_of(lambda z: state[z, rows, :], right, k, 1)
        whole = state[:, rows, :].reshape(HID, 128)
        turned[k] = dot(eye, whole, ((1,), (1,))).astype(BF16)


def tile_of(x, y, core, q):
    return 8 * (x - jnp.where(x > q, 1, 0)) + 2 * y + core


def place_of(x, z):
    q = z & 3
    return 3 * (z >> 2) + q - jnp.where(q > x, 1, 0)


def row_kinds(place):
    m = iota((96, RANK), 0) >> 3
    v = m - 3 * ((m * 11) >> 5)
    q = v + jnp.where(v >= place[0], 1, 0)
    return jnp.where(tile_of(place[0], place[1], place[2], q) >= 12, 1, 0)


def weigh(place, state, panel, _, keep, send, rows):
    weights = [jnp.concatenate(split3(panel[k]), axis=1) for k in range(2)]

    def block(g, _):
        for q in range(4):
            z = 4 * g + q
            for k in range(2):
                value = dot(state[z, k * BLOCK : (k + 1) * BLOCK, :], weights[k])
                total = value[:, :128] + (value[:, 128:256] + value[:, 256:])
                rows[q, k * BLOCK : (k + 1) * BLOCK, :] = total
            for x in range(4):
                if x == q:
                    continue
                m = 3 * g + q - int(q > x)
                for y in range(4):
                    first = 64 * (x - int(x > q)) + 16 * y
                    near = pl.multiple_of(first + 8 * place[2], 8)
                    far = pl.multiple_of(first + 8 - 8 * place[2], 8)
                    keep[4 * x + y, m] = rows[q, pl.ds(near, 8), :]
                    send[4 * x + y, m] = rows[q, pl.ds(far, 8), :]
        return 0

    lax.fori_loop(0, 4, block, 0)


def invert(gram, out, work, *, size):
    n = RANK
    eye = (iota((n, n), 0) == iota((n, n), 1)).astype(F32)
    for m in range(2):
        work[m, :, :n] = gram[m] + ridge_term * eye
    for m in range(2):
        work[m, :, n:] = eye
    row = iota((size, 2 * n), 0)
    lane = iota((size, n), 1)
    for k in range(0, n, size):
        blocks = [work[m, k : k + size, :] for m in range(2)]
        for i in range(size):
            for m in range(2):
                b = blocks[m]
                scale = lax.rsqrt(b[i : i + 1, k + i : k + i + 1])
                line = b[i : i + 1, :] * scale
                column = jnp.where(row > i, b[:, k + i : k + i + 1] * scale, 0.0)
                blocks[m] = jnp.where(row == i, line, b - column * line)
        for m in range(2):
            b = blocks[m]
            out[m, k : k + size, :] = b[:, n:]
            if k + size < n:
                left = jnp.where(lane >= k + size, b[:, :n], 0.0)
                change = dot(left, b, ((0,), (0,)), HIGHEST)
                work[m, k + size :, :] -= change[k + size :, :]


def scale_factor(place, inverse, parts, out, back, tiles):
    f = place[0] * 8 + place[1] * 2 + place[2]
    total = parts[0]
    for i in range(1, 16):
        total = total + parts[i]
    both = [dot(total, inverse[k], ((1,), (1,)), HIGHEST) for k in range(2)]
    kinds = row_kinds(place)
    value = jnp.where(kinds == 0, both[0], both[1])
    out[:96] = value.astype(BF16)
    tiles[:96] = value
    tiles[96:] = jnp.zeros((8, RANK), F32)
    square = value * value
    sums = [
        jnp.sum(jnp.where(kinds == k, square, 0.0), axis=0, keepdims=True) for k in range(2)
    ]
    tail = jnp.concatenate(sums + [jnp.zeros((6, RANK), F32)], axis=0)
    for z in range(GROUPS):
        m = jnp.where(place[0] == (z & 3), 12, place_of(place[0], z))
        tile = tiles[pl.ds(pl.multiple_of(8 * m, 8), 8), :]
        back[z] = jnp.concatenate([tile, tail], axis=0).astype(BF16)
    half = jnp.where(f >= 16, 1, 0)
    start = pl.multiple_of(8 * f - 128 * half, 8)
    rows = inverse[half, pl.ds(start, 8), :]
    high = rows.astype(BF16).astype(F32)
    out[96:] = jnp.concatenate([high, rows - high], axis=0).astype(BF16)


def orthonormal(table, place, panel, inverse, left, low):
    owned = table[COUNT + place[3]] > 0
    for k in range(2):
        ortho = dot(panel[k], inverse[k], ((1,), (1,)), HIGHEST)
        ortho = jnp.where(owned, ortho, 0.0)
        left[k] = ortho * math.sqrt(D)
        low[k] = (ortho * (-feedback)).astype(BF16)


def turn(table, place, state, out):
    owned = table[COUNT + place[3]] > 0
    eye = jnp.where(owned, unit(), jnp.zeros((128, 128), BF16))
    for k in range(2):
        rows = state[:, k * BLOCK : (k + 1) * BLOCK, :].reshape(HID, 128)
        out[k] = dot(eye, rows, ((1,), (1,))).astype(BF16)


SECOND_ROWS, RIGHT_ROWS, SUM_ROWS, ROWS = 96, 208, 288, 320


def pick(table, place, *refs):
    via = table[VIA + place[3]]
    value = refs[0][...]
    for j in range(1, NEAR):
        value = jnp.where(via == j, refs[j][...], value)
    refs[NEAR][...] = value


def select(table, place, mine, second, tiles, out, packed):
    packed[:SECOND_ROWS, :] = mine[:96, :]
    packed[SECOND_ROWS:RIGHT_ROWS, :] = second[...]
    sums = []
    for e in range(0, EXPERTS, 2):
        pair = [tiles[table[WHERE + e + i]].astype(F32) for i in range(2)]
        sums += [value[8:10] for value in pair]
        first = RIGHT_ROWS + e * 8
        packed[first : first + 16, :] = jnp.concatenate(
            [value[:8] for value in pair], axis=0
        ).astype(BF16)
    sums.append(jnp.zeros((ROWS - SUM_ROWS - 2 * EXPERTS, RANK), F32))
    packed[SUM_ROWS:, :] = jnp.concatenate(sums, axis=0).astype(BF16)
    value = packed[...]
    for i in range(16):
        out[i] = value


def finish_right(place, near, far, out, blocks):
    q = place[3] & 3
    parts = near[:, SUM_ROWS:, :].astype(F32) + far[:, SUM_ROWS:, :].astype(F32)
    scale = lax.rsqrt(jnp.sum(parts, axis=0) * (1.0 / HID) + epsilon)
    for part, core in ((near, place[2]), (far, 1 - place[2])):
        for chip in range(16):
            x, y = chip // 4, chip % 4
            t = jnp.where(q == x, 24, tile_of(x, y, core, q))
            row = pl.ds(pl.multiple_of(8 * t, 8), 8)
            for e in range(0, EXPERTS, 2):
                first = RIGHT_ROWS + e * 8
                value = part[chip, first : first + 16, :].astype(F32)
                blocks[e, row, :] = value[:8]
                blocks[e + 1, row, :] = value[8:]
    for e in range(EXPERTS):
        for k in range(2):
            rows = slice(k * BLOCK, (k + 1) * BLOCK)
            out[e, k] = blocks[e, rows, :] * scale[2 * e + k : 2 * e + k + 1, :]


def finish_state(
    table, place, turned, second, near, far, low, panel, left, out, left_out, inverse, factor
):
    for part, core in ((near, place[2]), (far, 1 - place[2])):
        for chip in range(16):
            x, y = chip // 4, chip % 4
            value = part[chip, SECOND_ROWS + 96 : SECOND_ROWS + 112, :].astype(F32)
            row = pl.multiple_of(16 * chip + 8 * core, 8)
            inverse[pl.ds(row, 8), :] = value[:8] + value[8:]
            for s in range(2):
                for g in range(6):
                    first = s * SECOND_ROWS + 16 * g
                    value = part[chip, first : first + 16, :].astype(F32)
                    for i in range(2):
                        m = 2 * g + i
                        v = m % 3
                        q = v + int(v >= x)
                        t = 8 * (x - int(x > q)) + 2 * y
                        base = (4 * (m // 3) + q) * BLOCK + 8 * (t % 12)
                        row = pl.ds(pl.multiple_of(base + 8 * core, 8), 8)
                        factor[2 * s + t // 12, row, :] = value[8 * i : 8 * i + 8]
    some = table[SECOND + place[3]] < EXPERTS
    lows = [low[0], low[1]]
    for k in range(2):
        ortho = dot(panel[k], inverse[k * RANK : (k + 1) * RANK, :], ((1,), (1,)), HIGHEST)
        ortho = jnp.where(some, ortho, 0.0)
        left_out[k] = left[k]
        left_out[2 + k] = ortho * math.sqrt(D)
        lows.append((ortho * (-feedback)).astype(BF16))
    for s, state in enumerate((turned, second)):
        for k in range(2):
            i = 2 * s + k
            change = dot(lows[i], factor[i].astype(BF16), ((1,), (1,)))
            out[i] = (state[k].astype(F32) + change).astype(BF16)


def ring(shift):
    return [(i, (i + shift) % 4) for i in range(4)]


SHIFTS = (3, 1, 2)


def gather_slices(x):
    for axis in ("x", "y"):
        x = jnp.stack([x] + [lax.ppermute(x, axis, ring((4 - d) % 4)) for d in SHIFTS])
    x = x.reshape((16,) + x.shape[2:])
    return x, lax.ppermute(x, "c", SWAP)


def exchange(x, axis):
    return lax.all_to_all(x, axis, split_axis=0, concat_axis=0, tiled=True)


def shards(momentum, gradient, right_in, owners):
    sds = jax.ShapeDtypeStruct
    barrier = lax.optimization_barrier
    place = jnp.stack([lax.axis_index(a) for a in ("x", "y", "c", "z")]).astype(jnp.int32)
    slices, table = pl.pallas_call(
        slice_right,
        out_shape=(sds((16, 16, RANK), BF16), sds((TABLE,), jnp.int32)),
        in_specs=[SMEM, SMEM, VMEM],
        out_specs=(VMEM, SMEM),
        scratch_shapes=[pltpu.VMEM((EXPERTS + 1, 8, RANK), F32)],
    )(owners, place, right_in)
    slices = exchange(slices, "z")
    sent, late = call(
        place_state,
        (sds((16, 192, 128), BF16), sds((SECONDS, 192, 128), BF16)),
        specs=[SMEM, VMEM, VMEM],
    )(table, jnp.swapaxes(momentum, 2, 3), jnp.swapaxes(gradient, 2, 3))
    sent, slices = barrier((sent, slices))
    state = exchange(sent, "z")
    near, far = gather_slices(slices)
    right = call(
        join_right,
        sds((16, 384, RANK), BF16),
        [pltpu.VMEM((384, 512), BF16)],
        flops=800_000_000,
        specs=[SMEM, VMEM, VMEM],
    )(place, near, far)
    square = sds((2, RANK, RANK), F32)
    two = sds((2, 128, RANK), F32)
    panel, gram = call(panels, (two, square), n_in=2, flops=300_000_000)(state, right)
    late, gram = barrier((late, gram))
    seconds = lax.all_gather(late, "z")
    gram = jnp.sum(exchange(gram.reshape(32, 8, RANK), FSDP), axis=0)
    half = sds((16, 12, 8, RANK), F32)
    keep, send = call(
        weigh, (half, half), [pltpu.VMEM((4, 192, RANK), F32)], specs=[SMEM, VMEM, VMEM, ANY], flops=400_000_000
    )(place, state, panel, gram)
    parts = keep + lax.ppermute(send, "c", SWAP)
    gram = exchange(jnp.broadcast_to(gram[None], (32, 8, RANK)), FSDP).reshape(2, RANK, RANK)
    parts, gram = barrier((parts, gram))
    parts = exchange(parts.reshape(16, 96, RANK), XY)
    inverse = call(
        functools.partial(invert, size=32),
        square,
        [pltpu.VMEM((2, RANK, 2 * RANK), F32)],
        n_in=1,
        flops=4_000_000_000,
    )(gram)
    mine, back = call(
        scale_factor,
        (sds((112, RANK), BF16), sds((16, 16, RANK), BF16)),
        [pltpu.VMEM((104, RANK), F32)],
        specs=[SMEM, VMEM, VMEM],
        flops=100_000_000,
    )(place, inverse, parts)
    turned = call(turn, sds((2, 128, HID), BF16), specs=[SMEM, SMEM, VMEM], flops=100_000_000)(
        table, place, state
    )
    left, low = call(
        orthonormal, (two, sds((2, 128, RANK), BF16)), specs=[SMEM, SMEM, VMEM, VMEM], flops=100_000_000
    )(table, place, panel, inverse)

    def from_near(mine, back):
        moved = [
            lax.ppermute(mine, "z", [(i, (i - step) % GROUPS) for i in range(GROUPS)])
            for step in STEPS[:NEAR]
        ]
        tiles = exchange(back, "z")
        other = call(pick, sds((112, RANK), BF16), specs=[SMEM, SMEM] + [VMEM] * NEAR)(
            table, place, *moved
        )
        return tiles, other

    def from_any(mine, back):
        gathered = lax.all_gather(mine, "z")
        other = lax.dynamic_index_in_dim(gathered, table[HELPER + place[3]], 0, False)
        return exchange(back, "z"), other

    tiles, other = lax.cond(table[GOOD] == 1, from_near, from_any, mine, back)
    second_panel, second_turned = call(
        second_panels,
        (two, sds((2, 128, HID), BF16)),
        [pltpu.VMEM((16, 192, 128), BF16), pltpu.SemaphoreType.DMA],
        specs=[SMEM, SMEM, ANY, VMEM],
        flops=300_000_000,
    )(table, place, seconds, right)
    chosen = call(
        select,
        sds((16, ROWS, RANK), BF16),
        [pltpu.VMEM((ROWS, RANK), BF16)],
        specs=[SMEM, SMEM, VMEM, VMEM, VMEM],
    )(table, place, mine, other, tiles)
    near = exchange(chosen, XY)
    near, turned, low, left, second_panel, second_turned = barrier(
        (near, turned, low, left, second_panel, second_turned)
    )
    far = lax.ppermute(near, "c", SWAP)
    right_out = call(
        finish_right, sds((EXPERTS, 2, BLOCK, RANK), F32), [pltpu.VMEM((EXPERTS, 200, RANK), F32)],
        specs=[SMEM, VMEM, VMEM], flops=1_000_000
    )(place, near, far)
    state_out, left_out = call(
        finish_state,
        (sds((4, 128, HID), BF16), sds((4, 128, RANK), F32)),
        [pltpu.VMEM((2 * RANK, RANK), F32), pltpu.VMEM((4, HID, RANK), F32)],
        specs=[SMEM, SMEM] + [VMEM] * 7,
        flops=1_200_000_000,
    )(table, place, turned, second_turned, near, far, low, second_panel, left)
    return (
        state_out.reshape(CAP, 2, 128, HID),
        left_out.reshape(CAP, 2, 128, RANK),
        right_out,
    )


def solution(mesh):
    fine = Mesh(mesh.devices.reshape(4, 4, 2, 16), ("x", "y", "c", "z"))
    return jax.shard_map(
        shards,
        mesh=fine,
        in_specs=(
            P(None, None, FSDP, "z"),
            P(None, None, FSDP, "z"),
            P(None, None, "z", None),
            P(),
        ),
        out_specs=(
            P("z", None, FSDP, None),
            P("z", None, FSDP, None),
            P(None, None, "z", None),
        ),
        check_vma=False,
    )
```

```python
import functools
import math

import jax
import jax.numpy as jnp
from jax import lax
from jax.experimental import pallas as pl
from jax.experimental.pallas import tpu as pltpu
from jax.sharding import Mesh
from jax.sharding import PartitionSpec as P

D = 4096
HID = 1536
CAP = 2
EXPERTS = 10
GROUPS = 16
BLOCK = 96
RANK = 128

ridge_term = 0.001
feedback = 0.1
epsilon = 1e-06

F32 = jnp.float32
BF16 = jnp.bfloat16
HIGHEST = lax.Precision.HIGHEST
XY = ("x", "y")
FSDP = ("x", "y", "c")
SWAP = [(0, 1), (1, 0)]
VMEM = pl.BlockSpec(memory_space=pltpu.VMEM)
SMEM = pl.BlockSpec(memory_space=pltpu.SMEM)
ANY = pl.BlockSpec(memory_space=pl.ANY)


def call(body, outs, scratch=(), flops=0, specs=None, n_in=0):
    return pl.pallas_call(
        body,
        out_shape=outs,
        in_specs=specs if specs is not None else [VMEM] * n_in,
        out_specs=jax.tree.map(lambda _: VMEM, outs),
        scratch_shapes=list(scratch),
        compiler_params=pltpu.CompilerParams(vmem_limit_bytes=16 * 1024 * 1024),
        cost_estimate=pl.CostEstimate(flops=flops, bytes_accessed=4_000_000, transcendentals=0),
    )


def dot(a, b, contract=((1,), (0,)), precision=None):
    return lax.dot_general(
        a, b, (contract, ((), ())), precision=precision, preferred_element_type=F32
    )


def iota(shape, dim):
    return lax.broadcasted_iota(jnp.int32, shape, dim)


COUNT, WORK, SECOND, HELPER, WHERE, FREE, SLOT, LIST, TABLE = 0, 17, 34, 51, 68, 80, 97, 114, 128
SECONDS = EXPERTS // 2
NONE = GROUPS


def fill_table(own, table):
    for g in range(GROUPS + 1):
        table[COUNT + g] = 0
        table[WORK + g] = EXPERTS
        table[SECOND + g] = EXPERTS
        table[HELPER + g] = 0
        table[SLOT + g] = 0
    for j in range(TABLE - LIST):
        table[LIST + j] = EXPERTS
    for e in range(EXPERTS):
        g = own[e]
        p = table[COUNT + g]
        table[COUNT + g] = p + 1
        table[WORK + jnp.where(p == 0, g, NONE)] = e
        table[SECOND + jnp.where(p == 0, NONE, g)] = e
    free = jnp.int32(0)
    for g in range(GROUPS):
        table[FREE + free] = g
        free = free + jnp.where(table[COUNT + g] == 0, 1, 0)
    used = jnp.int32(0)
    for e in range(EXPERTS):
        g = own[e]
        second = table[SECOND + g] == e
        h = table[FREE + used]
        table[WORK + jnp.where(second, h, NONE)] = e
        table[HELPER + jnp.where(second, g, NONE)] = h
        table[WHERE + e] = jnp.where(second, h, g)
        table[SLOT + jnp.where(second, g, NONE)] = used
        table[LIST + jnp.where(second, used, SECONDS)] = e
        used = used + jnp.where(second, 1, 0)


def slice_right(own, place, right, out, table, held):
    fill_table(own, table)
    f = place[0] * 8 + place[1] * 2 + place[2]
    pick = (iota((8, 192), 1) == iota((8, 192), 0) + 8 * f).astype(BF16)
    for e in range(EXPERTS):
        held[e] = dot(pick, right[e].reshape(192, RANK))
    held[EXPERTS] = jnp.zeros((8, RANK), F32)

    def group(g, _):
        pair = jnp.concatenate([held[table[WORK + g]], held[table[SECOND + g]]], axis=0)
        out[g] = pair.astype(BF16)
        return 0

    lax.fori_loop(0, GROUPS, group, 0)


def place_state(table, momentum, gradient, first, other):
    def put(out, i, e):
        @pl.when(e < EXPERTS)
        def _():
            total = momentum[e].astype(F32) + gradient[e].astype(F32)
            out[i] = total.astype(BF16).reshape(192, 128)

        @pl.when(e >= EXPERTS)
        def _():
            out[i] = jnp.zeros((192, 128), BF16)

    def slot(g, _):
        put(first, g, table[WORK + g])
        return 0

    lax.fori_loop(0, GROUPS, slot, 0)
    for j in range(SECONDS):
        put(other, j, table[LIST + j])


def offset(i):
    return jnp.where(i == 1, 3, jnp.where(i == 2, 1, jnp.where(i == 3, 2, 0)))


def join_matrix(place, core, relative, chips):
    col = iota((384, 16 * chips), 1)
    chip = col >> 4
    if relative:
        x = (place[0] + offset(chip & 3)) & 3
        y = (place[1] + offset(chip >> 2)) & 3
        chip = x * 4 + y
    f = chip * 2 + core
    target = ((col >> 3) & 1) * 192 + 8 * f + (col & 7)
    return ((iota((384, 16 * chips), 0) == target) & (f < 24)).astype(BF16)


def join_right(place, near, far, out, matrix):
    c = place[2]
    matrix[:, :256] = join_matrix(place, c, True, 16)
    matrix[:, 256:] = join_matrix(place, 1 - c, True, 16)

    def block(z, _):
        a = near[:, z].reshape(256, RANK)
        b = far[:, z].reshape(256, RANK)
        both = jnp.concatenate([a, b], axis=0)
        out[z] = dot(matrix[...], both).astype(BF16)
        return 0

    lax.fori_loop(0, GROUPS, block, 0, unroll=4)


def split3(value):
    high = value.astype(BF16)
    rest = value - high.astype(F32)
    middle = rest.astype(BF16)
    low = (rest - middle.astype(F32)).astype(BF16)
    return high, middle, low


def panel_of(block_of, right, kind, slot):
    def block(z, total):
        b = right[z, pl.ds(slot * 192 + kind * BLOCK, BLOCK), :]
        return total + dot(block_of(z), b, ((0,), (0,)))

    return lax.fori_loop(0, GROUPS, block, jnp.zeros((128, RANK), F32), unroll=4)


PACKED = 80


def pack(gram):
    middle = jnp.concatenate([gram[96:, 96:], gram[32:64, 32:]], axis=1)
    last = jnp.concatenate([gram[80:96, 64:], gram[64:80, 64:]], axis=1)
    return jnp.concatenate([gram[:32], middle, last], axis=0)


def unpack(packed):
    middle, last = packed[32:64], packed[64:]
    other = jnp.concatenate([last[:, 64:], last[:, :64]], axis=1)
    corner = jnp.concatenate([middle[:, 32:], middle[:, :32]], axis=1)
    return jnp.concatenate([packed[:32], middle, last, other, corner], axis=0)


def panels(place, state, right, panel, keep, send):
    grams = []
    for k in range(2):
        rows = slice(k * BLOCK, (k + 1) * BLOCK)
        value = panel_of(lambda z: state[z, rows, :], right, k, 0)
        panel[k] = value
        grams.append(pack(dot(value, value, ((0,), (0,)), HIGHEST)))
    mine = place[2] == 0
    keep[...] = jnp.where(mine, grams[0], grams[1])
    send[...] = jnp.where(mine, grams[1], grams[0])


def unit():
    return (iota((128, 128), 0) == iota((128, 128), 1)).astype(BF16)


def second_panels(table, place, states, right, panel, turned, state, arrived):
    copy = pltpu.make_async_copy(states.at[:, table[SLOT + place[3]]], state, arrived)
    copy.start()
    some = table[SECOND + place[3]] < EXPERTS
    eye = jnp.where(some, unit(), jnp.zeros((128, 128), BF16))
    copy.wait()
    for k in range(2):
        rows = slice(k * BLOCK, (k + 1) * BLOCK)
        panel[k] = panel_of(lambda z: state[z, rows, :], right, k, 1)
        whole = state[:, rows, :].reshape(HID, 128)
        turned[k] = dot(eye, whole, ((1,), (1,))).astype(BF16)


def tile_of(x, y, core, q):
    return 8 * (x - jnp.where(x > q, 1, 0)) + 2 * y + core


def place_of(x, z):
    q = z & 3
    return 3 * (z >> 2) + q - jnp.where(q > x, 1, 0)


def row_kinds(place):
    m = iota((96, RANK), 0) >> 3
    v = m - 3 * ((m * 11) >> 5)
    q = v + jnp.where(v >= place[0], 1, 0)
    return jnp.where(tile_of(place[0], place[1], place[2], q) >= 12, 1, 0)


def weigh(place, state, panel, keep, send, rows):
    weights = [jnp.concatenate(split3(panel[k]), axis=1) for k in range(2)]

    def block(g, _):
        for q in range(4):
            z = 4 * g + q
            for k in range(2):
                value = dot(state[z, k * BLOCK : (k + 1) * BLOCK, :], weights[k])
                total = value[:, :128] + (value[:, 128:256] + value[:, 256:])
                rows[q, k * BLOCK : (k + 1) * BLOCK, :] = total
            for x in range(4):
                if x == q:
                    continue
                m = 3 * g + q - int(q > x)
                for y in range(4):
                    first = 64 * (x - int(x > q)) + 16 * y
                    near = pl.multiple_of(first + 8 * place[2], 8)
                    far = pl.multiple_of(first + 8 - 8 * place[2], 8)
                    keep[4 * x + y, m] = rows[q, pl.ds(near, 8), :]
                    send[4 * x + y, m] = rows[q, pl.ds(far, 8), :]
        return 0

    lax.fori_loop(0, 4, block, 0)


def eliminate(sets, k):
    row = iota((8, 256), 0)
    n = len(sets[0])
    for g in range(n):
        first = k + 8 * g
        columns = [
            [
                [jnp.broadcast_to(s[t][:, first + j : first + j + 1], (8, 256)) for t in range(g, n)]
                for j in range(8)
            ]
            for s in sets
        ]
        scales = [jnp.zeros((8, 256), F32) for _ in sets]
        for i in range(8):
            inverses = [
                lax.rsqrt(jnp.broadcast_to(c[i][0][i : i + 1, :], (8, 256))) for c in columns
            ]
            for m, (s, c) in enumerate(zip(sets, columns)):
                scales[m] = jnp.where(row == i, inverses[m], scales[m])
                square = inverses[m] * inverses[m]
                factors = [part * square for part in c[i]]
                factors[0] = jnp.where(row > i, factors[0], 0.0)
                for j in range(i + 1, 8):
                    line = jnp.broadcast_to(c[j][0][i : i + 1, :], (8, 256))
                    c[j] = [part - f * line for part, f in zip(c[j], factors)]
                line = jnp.broadcast_to(s[g][i : i + 1, :], (8, 256))
                for t in range(g, n):
                    s[t] = s[t] - factors[t - g] * line
        for m, s in enumerate(sets):
            s[g] = s[g] * scales[m]


def invert(place, near, far, out, work, *, size):
    n = RANK
    eye = (iota((n, n), 0) == iota((n, n), 1)).astype(F32)
    mine = place[2] == 0
    first, other = unpack(near[...]), unpack(far[...])
    work[0, :, :n] = jnp.where(mine, first, other) + ridge_term * eye
    work[1, :, :n] = jnp.where(mine, other, first) + ridge_term * eye
    for m in range(2):
        work[m, :, n:] = eye
    lane = iota((size, n), 1)
    for k in range(0, n, size):
        sets = [[work[m, k + 8 * t : k + 8 * t + 8, :] for t in range(size // 8)] for m in range(2)]
        eliminate(sets, k)
        for m in range(2):
            b = jnp.concatenate(sets[m], axis=0)
            out[m, k : k + size, :] = b[:, n:]
            if k + size < n:
                left = jnp.where(lane >= k + size, b[:, :n], 0.0)
                change = dot(left, b, ((0,), (0,)), HIGHEST)
                work[m, k + size :, :] -= change[k + size :, :]


def scale_factor(place, inverse, parts, out):
    f = place[0] * 8 + place[1] * 2 + place[2]
    total = parts[0]
    for i in range(1, 16):
        total = total + parts[i]
    both = [dot(total, inverse[k], ((1,), (1,)), HIGHEST) for k in range(2)]
    out[:96] = jnp.where(row_kinds(place) == 0, both[0], both[1]).astype(BF16)
    half = jnp.where(f >= 16, 1, 0)
    start = pl.multiple_of(8 * f - 128 * half, 8)
    rows = inverse[half, pl.ds(start, 8), :]
    high = rows.astype(BF16).astype(F32)
    out[96:] = jnp.concatenate([high, rows - high], axis=0).astype(BF16)


def orthonormal(table, place, panel, inverse, left, low):
    owned = table[COUNT + place[3]] > 0
    for k in range(2):
        ortho = dot(panel[k], inverse[k], ((1,), (1,)), HIGHEST)
        ortho = jnp.where(owned, ortho, 0.0)
        left[k] = ortho * math.sqrt(D)
        low[k] = (ortho * (-feedback)).astype(BF16)


def turn(table, place, state, out):
    owned = table[COUNT + place[3]] > 0
    eye = jnp.where(owned, unit(), jnp.zeros((128, 128), BF16))
    for k in range(2):
        rows = state[:, k * BLOCK : (k + 1) * BLOCK, :].reshape(HID, 128)
        out[k] = dot(eye, rows, ((1,), (1,))).astype(BF16)


SECOND_ROWS, RIGHT_ROWS, SUM_ROWS, ROWS = 96, 208, 288, 320


def select(table, place, mine, tiles, out, packed):
    z = place[3]
    packed[:SECOND_ROWS, :] = mine[:96, :]
    packed[SECOND_ROWS:RIGHT_ROWS, :] = tiles[table[HELPER + z]]
    m = place_of(place[0], z)
    start = pl.multiple_of((m >> 1) * 16, 16)
    upper = (m & 1) == 1
    kinds = row_kinds(place)
    sums = []
    for e in range(0, EXPERTS, 2):
        pair = []
        for i in range(2):
            p = table[WHERE + e + i]
            value = tiles[p, pl.ds(start, 16), :].astype(F32)
            pair.append(jnp.where(upper, value[8:], value[:8]))
            whole = tiles[p, :96, :].astype(F32)
            square = whole * whole
            for k in range(2):
                sums.append(jnp.sum(jnp.where(kinds == k, square, 0.0), axis=0, keepdims=True))
        first = RIGHT_ROWS + e * 8
        packed[first : first + 16, :] = jnp.concatenate(pair, axis=0).astype(BF16)
    sums.append(jnp.zeros((ROWS - SUM_ROWS - 2 * EXPERTS, RANK), F32))
    packed[SUM_ROWS:, :] = jnp.concatenate(sums, axis=0).astype(BF16)
    value = packed[...]
    for i in range(16):
        out[i] = value


def finish_right(place, near, far, out, blocks):
    q = place[3] & 3
    parts = near[:, SUM_ROWS:, :].astype(F32) + far[:, SUM_ROWS:, :].astype(F32)
    scale = lax.rsqrt(jnp.sum(parts, axis=0) * (1.0 / HID) + epsilon)
    for part, core in ((near, place[2]), (far, 1 - place[2])):
        for chip in range(16):
            x, y = chip // 4, chip % 4
            t = jnp.where(q == x, 24, tile_of(x, y, core, q))
            row = pl.ds(pl.multiple_of(8 * t, 8), 8)
            for e in range(0, EXPERTS, 2):
                first = RIGHT_ROWS + e * 8
                value = part[chip, first : first + 16, :].astype(F32)
                blocks[e, row, :] = value[:8]
                blocks[e + 1, row, :] = value[8:]
    for e in range(EXPERTS):
        for k in range(2):
            rows = slice(k * BLOCK, (k + 1) * BLOCK)
            out[e, k] = blocks[e, rows, :] * scale[2 * e + k : 2 * e + k + 1, :]


def finish_state(
    table, place, turned, second, near, far, low, panel, left, out, left_out, inverse, factor
):
    for part, core in ((near, place[2]), (far, 1 - place[2])):
        for chip in range(16):
            x, y = chip // 4, chip % 4
            value = part[chip, SECOND_ROWS + 96 : SECOND_ROWS + 112, :].astype(F32)
            row = pl.multiple_of(16 * chip + 8 * core, 8)
            inverse[pl.ds(row, 8), :] = value[:8] + value[8:]
            for s in range(2):
                for g in range(6):
                    first = s * SECOND_ROWS + 16 * g
                    value = part[chip, first : first + 16, :].astype(F32)
                    for i in range(2):
                        m = 2 * g + i
                        v = m % 3
                        q = v + int(v >= x)
                        t = 8 * (x - int(x > q)) + 2 * y
                        base = (4 * (m // 3) + q) * BLOCK + 8 * (t % 12)
                        row = pl.ds(pl.multiple_of(base + 8 * core, 8), 8)
                        factor[2 * s + t // 12, row, :] = value[8 * i : 8 * i + 8]
    some = table[SECOND + place[3]] < EXPERTS
    lows = [low[0], low[1]]
    for k in range(2):
        ortho = dot(panel[k], inverse[k * RANK : (k + 1) * RANK, :], ((1,), (1,)), HIGHEST)
        ortho = jnp.where(some, ortho, 0.0)
        left_out[k] = left[k]
        left_out[2 + k] = ortho * math.sqrt(D)
        lows.append((ortho * (-feedback)).astype(BF16))
    for s, state in enumerate((turned, second)):
        for k in range(2):
            i = 2 * s + k
            change = dot(lows[i], factor[i].astype(BF16), ((1,), (1,)))
            out[i] = (state[k].astype(F32) + change).astype(BF16)


def ring(shift):
    return [(i, (i + shift) % 4) for i in range(4)]


SHIFTS = (3, 1, 2)


def gather_slices(x):
    for axis in ("x", "y"):
        x = jnp.stack([x] + [lax.ppermute(x, axis, ring((4 - d) % 4)) for d in SHIFTS])
    x = x.reshape((16,) + x.shape[2:])
    return x, lax.ppermute(x, "c", SWAP)


def exchange(x, axis):
    return lax.all_to_all(x, axis, split_axis=0, concat_axis=0, tiled=True)


def shards(momentum, gradient, right_in, owners):
    sds = jax.ShapeDtypeStruct
    barrier = lax.optimization_barrier
    place = jnp.stack([lax.axis_index(a) for a in ("x", "y", "c", "z")]).astype(jnp.int32)
    slices, table = pl.pallas_call(
        slice_right,
        out_shape=(sds((16, 16, RANK), BF16), sds((TABLE,), jnp.int32)),
        in_specs=[SMEM, SMEM, VMEM],
        out_specs=(VMEM, SMEM),
        scratch_shapes=[pltpu.VMEM((EXPERTS + 1, 8, RANK), F32)],
    )(owners, place, right_in)
    slices = exchange(slices, "z")
    sent, late = call(
        place_state,
        (sds((16, 192, 128), BF16), sds((SECONDS, 192, 128), BF16)),
        specs=[SMEM, VMEM, VMEM],
    )(table, jnp.swapaxes(momentum, 2, 3), jnp.swapaxes(gradient, 2, 3))
    sent, slices = barrier((sent, slices))
    state = exchange(sent, "z")
    near, far = gather_slices(slices)
    right = call(
        join_right,
        sds((16, 384, RANK), BF16),
        [pltpu.VMEM((384, 512), BF16)],
        flops=800_000_000,
        specs=[SMEM, VMEM, VMEM],
    )(place, near, far)
    square = sds((PACKED, RANK), F32)
    two = sds((2, 128, RANK), F32)
    panel, keep, send = call(
        panels, (two, square, square), specs=[SMEM, VMEM, VMEM], flops=300_000_000
    )(place, state, right)
    late, send = barrier((late, send))
    seconds = lax.all_gather(late, "z")
    gram = keep + lax.ppermute(send, "c", SWAP)
    half = sds((16, 12, 8, RANK), F32)
    keep, send = call(
        weigh, (half, half), [pltpu.VMEM((4, 192, RANK), F32)], specs=[SMEM, VMEM, VMEM], flops=400_000_000
    )(place, state, panel)
    parts = keep + lax.ppermute(send, "c", SWAP)
    gram = exchange(jnp.broadcast_to(gram[None], (16, PACKED, RANK)), XY)
    parts, gram = barrier((parts, gram))
    parts = exchange(parts.reshape(16, 96, RANK), XY)
    gram = jnp.sum(gram, axis=0)
    inverse = call(
        functools.partial(invert, size=32),
        sds((2, RANK, RANK), F32),
        [pltpu.VMEM((2, RANK, 2 * RANK), F32)],
        specs=[SMEM, VMEM, VMEM],
        flops=2_000_000_000,
    )(place, gram, lax.ppermute(gram, "c", SWAP))
    mine = call(scale_factor, sds((112, RANK), BF16), specs=[SMEM, VMEM, VMEM], flops=100_000_000)(
        place, inverse, parts
    )
    turned = call(turn, sds((2, 128, HID), BF16), specs=[SMEM, SMEM, VMEM], flops=100_000_000)(
        table, place, state
    )
    left, low = call(
        orthonormal, (two, sds((2, 128, RANK), BF16)), specs=[SMEM, SMEM, VMEM, VMEM], flops=100_000_000
    )(table, place, panel, inverse)
    tiles = lax.all_gather(mine, "z")
    second_panel, second_turned = call(
        second_panels,
        (two, sds((2, 128, HID), BF16)),
        [pltpu.VMEM((16, 192, 128), BF16), pltpu.SemaphoreType.DMA],
        specs=[SMEM, SMEM, ANY, VMEM],
        flops=300_000_000,
    )(table, place, seconds, right)
    chosen = call(
        select,
        sds((16, ROWS, RANK), BF16),
        [pltpu.VMEM((ROWS, RANK), BF16)],
        specs=[SMEM, SMEM, VMEM, VMEM],
    )(table, place, mine, tiles)
    near = exchange(chosen, XY)
    near, turned, low, left, second_panel, second_turned = barrier(
        (near, turned, low, left, second_panel, second_turned)
    )
    far = lax.ppermute(near, "c", SWAP)
    right_out = call(
        finish_right, sds((EXPERTS, 2, BLOCK, RANK), F32), [pltpu.VMEM((EXPERTS, 200, RANK), F32)],
        specs=[SMEM, VMEM, VMEM], flops=1_000_000
    )(place, near, far)
    state_out, left_out = call(
        finish_state,
        (sds((4, 128, HID), BF16), sds((4, 128, RANK), F32)),
        [pltpu.VMEM((2 * RANK, RANK), F32), pltpu.VMEM((4, HID, RANK), F32)],
        specs=[SMEM, SMEM] + [VMEM] * 7,
        flops=1_200_000_000,
    )(table, place, turned, second_turned, near, far, low, second_panel, left)
    return (
        state_out.reshape(CAP, 2, 128, HID),
        left_out.reshape(CAP, 2, 128, RANK),
        right_out,
    )


def solution(mesh):
    fine = Mesh(mesh.devices.reshape(4, 4, 2, 16), ("x", "y", "c", "z"))
    return jax.shard_map(
        shards,
        mesh=fine,
        in_specs=(
            P(None, None, FSDP, "z"),
            P(None, None, FSDP, "z"),
            P(None, None, "z", None),
            P(),
        ),
        out_specs=(
            P("z", None, FSDP, None),
            P("z", None, FSDP, None),
            P(None, None, "z", None),
        ),
        check_vma=False,
    )
```

```python
import functools
import math

import jax
import jax.numpy as jnp
from jax import lax
from jax.experimental import pallas as pl
from jax.experimental.pallas import tpu as pltpu
from jax.sharding import Mesh
from jax.sharding import PartitionSpec as P

D = 4096
HID = 1536
CAP = 2
EXPERTS = 10
GROUPS = 16
BLOCK = 96
RANK = 128

ridge_term = 0.001
feedback = 0.1
epsilon = 1e-06

F32 = jnp.float32
BF16 = jnp.bfloat16
HIGHEST = lax.Precision.HIGHEST
XY = ("x", "y")
FSDP = ("x", "y", "c")
SWAP = [(0, 1), (1, 0)]
VMEM = pl.BlockSpec(memory_space=pltpu.VMEM)
SMEM = pl.BlockSpec(memory_space=pltpu.SMEM)
ANY = pl.BlockSpec(memory_space=pl.ANY)


def call(body, outs, scratch=(), flops=0, specs=None, n_in=0):
    return pl.pallas_call(
        body,
        out_shape=outs,
        in_specs=specs if specs is not None else [VMEM] * n_in,
        out_specs=jax.tree.map(lambda _: VMEM, outs),
        scratch_shapes=list(scratch),
        compiler_params=pltpu.CompilerParams(vmem_limit_bytes=16 * 1024 * 1024),
        cost_estimate=pl.CostEstimate(flops=flops, bytes_accessed=4_000_000, transcendentals=0),
    )


def dot(a, b, contract=((1,), (0,)), precision=None):
    return lax.dot_general(
        a, b, (contract, ((), ())), precision=precision, preferred_element_type=F32
    )


def iota(shape, dim):
    return lax.broadcasted_iota(jnp.int32, shape, dim)


COUNT, WORK, SECOND, HELPER, WHERE, FREE, SLOT, LIST, TABLE = 0, 17, 34, 51, 68, 80, 97, 114, 128
SECONDS = EXPERTS // 2
NONE = GROUPS


def fill_table(own, table):
    for g in range(GROUPS + 1):
        table[COUNT + g] = 0
        table[WORK + g] = EXPERTS
        table[SECOND + g] = EXPERTS
        table[HELPER + g] = 0
        table[SLOT + g] = 0
    for j in range(TABLE - LIST):
        table[LIST + j] = EXPERTS
    for e in range(EXPERTS):
        g = own[e]
        p = table[COUNT + g]
        table[COUNT + g] = p + 1
        table[WORK + jnp.where(p == 0, g, NONE)] = e
        table[SECOND + jnp.where(p == 0, NONE, g)] = e
    free = jnp.int32(0)
    for g in range(GROUPS):
        table[FREE + free] = g
        free = free + jnp.where(table[COUNT + g] == 0, 1, 0)
    used = jnp.int32(0)
    for e in range(EXPERTS):
        g = own[e]
        second = table[SECOND + g] == e
        h = table[FREE + used]
        table[WORK + jnp.where(second, h, NONE)] = e
        table[HELPER + jnp.where(second, g, NONE)] = h
        table[WHERE + e] = jnp.where(second, h, g)
        table[SLOT + jnp.where(second, g, NONE)] = used
        table[LIST + jnp.where(second, used, SECONDS)] = e
        used = used + jnp.where(second, 1, 0)


def slice_right(own, place, right, out, table, held):
    fill_table(own, table)
    f = place[0] * 8 + place[1] * 2 + place[2]
    pick = (iota((8, 192), 1) == iota((8, 192), 0) + 8 * f).astype(BF16)
    for e in range(EXPERTS):
        held[e] = dot(pick, right[e].reshape(192, RANK))
    held[EXPERTS] = jnp.zeros((8, RANK), F32)

    def group(g, _):
        pair = jnp.concatenate([held[table[WORK + g]], held[table[SECOND + g]]], axis=0)
        out[g] = pair.astype(BF16)
        return 0

    lax.fori_loop(0, GROUPS, group, 0)


def place_state(table, momentum, gradient, first, other):
    def put(out, i, e):
        @pl.when(e < EXPERTS)
        def _():
            total = momentum[e].astype(F32) + gradient[e].astype(F32)
            out[i] = total.astype(BF16).reshape(192, 128)

        @pl.when(e >= EXPERTS)
        def _():
            out[i] = jnp.zeros((192, 128), BF16)

    def slot(g, _):
        put(first, g, table[WORK + g])
        return 0

    lax.fori_loop(0, GROUPS, slot, 0)
    for j in range(SECONDS):
        put(other, j, table[LIST + j])


def offset(i):
    return jnp.where(i == 1, 3, jnp.where(i == 2, 1, jnp.where(i == 3, 2, 0)))


def join_matrix(place, core, relative, chips):
    col = iota((384, 16 * chips), 1)
    chip = col >> 4
    if relative:
        x = (place[0] + offset(chip & 3)) & 3
        y = (place[1] + offset(chip >> 2)) & 3
        chip = x * 4 + y
    f = chip * 2 + core
    target = ((col >> 3) & 1) * 192 + 8 * f + (col & 7)
    return ((iota((384, 16 * chips), 0) == target) & (f < 24)).astype(BF16)


def join_right(place, near, far, out, matrix):
    c = place[2]
    matrix[:, :256] = join_matrix(place, c, True, 16)
    matrix[:, 256:] = join_matrix(place, 1 - c, True, 16)

    def block(z, _):
        a = near[:, z].reshape(256, RANK)
        b = far[:, z].reshape(256, RANK)
        both = jnp.concatenate([a, b], axis=0)
        out[z] = dot(matrix[...], both).astype(BF16)
        return 0

    lax.fori_loop(0, GROUPS, block, 0, unroll=4)


def split3(value):
    high = value.astype(BF16)
    rest = value - high.astype(F32)
    middle = rest.astype(BF16)
    low = (rest - middle.astype(F32)).astype(BF16)
    return high, middle, low


def panel_of(block_of, right, kind, slot):
    def block(z, total):
        b = right[z, pl.ds(slot * 192 + kind * BLOCK, BLOCK), :]
        return total + dot(block_of(z), b, ((0,), (0,)))

    return lax.fori_loop(0, GROUPS, block, jnp.zeros((128, RANK), F32), unroll=4)


PACKED = 96


def pack(gram):
    last = jnp.concatenate([gram[96:, 64:], gram[64:96, 64:]], axis=1)
    return jnp.concatenate([gram[:64], last], axis=0)


def unpack(packed):
    other = jnp.concatenate([packed[64:, 64:], packed[64:, :64]], axis=1)
    return jnp.concatenate([packed, other], axis=0)


def panels(place, state, right, panel, keep, send):
    grams = []
    for k in range(2):
        rows = slice(k * BLOCK, (k + 1) * BLOCK)
        value = panel_of(lambda z: state[z, rows, :], right, k, 0)
        panel[k] = value
        grams.append(pack(dot(value, value, ((0,), (0,)), HIGHEST)))
    mine = place[2] == 0
    keep[...] = jnp.where(mine, grams[0], grams[1])
    send[...] = jnp.where(mine, grams[1], grams[0])


def unit():
    return (iota((128, 128), 0) == iota((128, 128), 1)).astype(BF16)


def second_panels(table, place, states, right, panel, turned, state, arrived):
    copy = pltpu.make_async_copy(states.at[:, table[SLOT + place[3]]], state, arrived)
    copy.start()
    some = table[SECOND + place[3]] < EXPERTS
    eye = jnp.where(some, unit(), jnp.zeros((128, 128), BF16))
    copy.wait()
    for k in range(2):
        rows = slice(k * BLOCK, (k + 1) * BLOCK)
        panel[k] = panel_of(lambda z: state[z, rows, :], right, k, 1)
        whole = state[:, rows, :].reshape(HID, 128)
        turned[k] = dot(eye, whole, ((1,), (1,))).astype(BF16)


def tile_of(x, y, core, q):
    return 8 * (x - jnp.where(x > q, 1, 0)) + 2 * y + core


def place_of(x, z):
    q = z & 3
    return 3 * (z >> 2) + q - jnp.where(q > x, 1, 0)


def row_kinds(place):
    m = iota((96, RANK), 0) >> 3
    v = m - 3 * ((m * 11) >> 5)
    q = v + jnp.where(v >= place[0], 1, 0)
    return jnp.where(tile_of(place[0], place[1], place[2], q) >= 12, 1, 0)


def weigh(place, state, panel, keep, send, rows):
    weights = [jnp.concatenate(split3(panel[k]), axis=1) for k in range(2)]

    def block(g, _):
        for q in range(4):
            z = 4 * g + q
            for k in range(2):
                value = dot(state[z, k * BLOCK : (k + 1) * BLOCK, :], weights[k])
                total = value[:, :128] + (value[:, 128:256] + value[:, 256:])
                rows[q, k * BLOCK : (k + 1) * BLOCK, :] = total
            for x in range(4):
                if x == q:
                    continue
                m = 3 * g + q - int(q > x)
                for y in range(4):
                    first = 64 * (x - int(x > q)) + 16 * y
                    near = pl.multiple_of(first + 8 * place[2], 8)
                    far = pl.multiple_of(first + 8 - 8 * place[2], 8)
                    keep[4 * x + y, m] = rows[q, pl.ds(near, 8), :]
                    send[4 * x + y, m] = rows[q, pl.ds(far, 8), :]
        return 0

    lax.fori_loop(0, 4, block, 0)


def eliminate(sets, k):
    row = iota((8, 256), 0)
    n = len(sets[0])
    for g in range(n):
        first = k + 8 * g
        columns = [
            [
                [jnp.broadcast_to(s[t][:, first + j : first + j + 1], (8, 256)) for t in range(g, n)]
                for j in range(8)
            ]
            for s in sets
        ]
        scales = [jnp.zeros((8, 256), F32) for _ in sets]
        for i in range(8):
            inverses = [
                lax.rsqrt(jnp.broadcast_to(c[i][0][i : i + 1, :], (8, 256))) for c in columns
            ]
            for m, (s, c) in enumerate(zip(sets, columns)):
                scales[m] = jnp.where(row == i, inverses[m], scales[m])
                square = inverses[m] * inverses[m]
                factors = [part * square for part in c[i]]
                factors[0] = jnp.where(row > i, factors[0], 0.0)
                for j in range(i + 1, 8):
                    line = jnp.broadcast_to(c[j][0][i : i + 1, :], (8, 256))
                    c[j] = [part - f * line for part, f in zip(c[j], factors)]
                line = jnp.broadcast_to(s[g][i : i + 1, :], (8, 256))
                for t in range(g, n):
                    s[t] = s[t] - factors[t - g] * line
        for m, s in enumerate(sets):
            s[g] = s[g] * scales[m]


def invert(place, near, far, out, work, *, size):
    n = RANK
    eye = (iota((n, n), 0) == iota((n, n), 1)).astype(F32)
    mine = place[2] == 0
    first, other = unpack(near[...]), unpack(far[...])
    work[0, :, :n] = jnp.where(mine, first, other) + ridge_term * eye
    work[1, :, :n] = jnp.where(mine, other, first) + ridge_term * eye
    for m in range(2):
        work[m, :, n:] = eye
    lane = iota((size, n), 1)
    for k in range(0, n, size):
        sets = [[work[m, k + 8 * t : k + 8 * t + 8, :] for t in range(size // 8)] for m in range(2)]
        eliminate(sets, k)
        for m in range(2):
            b = jnp.concatenate(sets[m], axis=0)
            out[m, k : k + size, :] = b[:, n:]
            if k + size < n:
                left = jnp.where(lane >= k + size, b[:, :n], 0.0)
                change = dot(left, b, ((0,), (0,)), HIGHEST)
                work[m, k + size :, :] -= change[k + size :, :]


def scale_factor(place, inverse, parts, out):
    f = place[0] * 8 + place[1] * 2 + place[2]
    total = parts[0]
    for i in range(1, 16):
        total = total + parts[i]
    both = [dot(total, inverse[k], ((1,), (1,)), HIGHEST) for k in range(2)]
    out[:96] = jnp.where(row_kinds(place) == 0, both[0], both[1]).astype(BF16)
    half = jnp.where(f >= 16, 1, 0)
    start = pl.multiple_of(8 * f - 128 * half, 8)
    rows = inverse[half, pl.ds(start, 8), :]
    high = rows.astype(BF16).astype(F32)
    out[96:] = jnp.concatenate([high, rows - high], axis=0).astype(BF16)


def orthonormal(table, place, panel, inverse, left, low):
    owned = table[COUNT + place[3]] > 0
    for k in range(2):
        ortho = dot(panel[k], inverse[k], ((1,), (1,)), HIGHEST)
        ortho = jnp.where(owned, ortho, 0.0)
        left[k] = ortho * math.sqrt(D)
        low[k] = (ortho * (-feedback)).astype(BF16)


def turn(table, place, state, out):
    owned = table[COUNT + place[3]] > 0
    eye = jnp.where(owned, unit(), jnp.zeros((128, 128), BF16))
    for k in range(2):
        rows = state[:, k * BLOCK : (k + 1) * BLOCK, :].reshape(HID, 128)
        out[k] = dot(eye, rows, ((1,), (1,))).astype(BF16)


SECOND_ROWS, RIGHT_ROWS, SUM_ROWS, ROWS = 96, 208, 288, 320


def select(table, place, mine, tiles, out, packed):
    z = place[3]
    packed[:SECOND_ROWS, :] = mine[:96, :]
    packed[SECOND_ROWS:RIGHT_ROWS, :] = tiles[table[HELPER + z]]
    m = place_of(place[0], z)
    start = pl.multiple_of((m >> 1) * 16, 16)
    upper = (m & 1) == 1
    kinds = row_kinds(place)
    sums = []
    for e in range(0, EXPERTS, 2):
        pair = []
        for i in range(2):
            p = table[WHERE + e + i]
            value = tiles[p, pl.ds(start, 16), :].astype(F32)
            pair.append(jnp.where(upper, value[8:], value[:8]))
            whole = tiles[p, :96, :].astype(F32)
            square = whole * whole
            for k in range(2):
                sums.append(jnp.sum(jnp.where(kinds == k, square, 0.0), axis=0, keepdims=True))
        first = RIGHT_ROWS + e * 8
        packed[first : first + 16, :] = jnp.concatenate(pair, axis=0).astype(BF16)
    sums.append(jnp.zeros((ROWS - SUM_ROWS - 2 * EXPERTS, RANK), F32))
    packed[SUM_ROWS:, :] = jnp.concatenate(sums, axis=0).astype(BF16)
    value = packed[...]
    for i in range(16):
        out[i] = value


def finish_right(place, near, far, out, blocks):
    q = place[3] & 3
    parts = near[:, SUM_ROWS:, :].astype(F32) + far[:, SUM_ROWS:, :].astype(F32)
    scale = lax.rsqrt(jnp.sum(parts, axis=0) * (1.0 / HID) + epsilon)
    for part, core in ((near, place[2]), (far, 1 - place[2])):
        for chip in range(16):
            x, y = chip // 4, chip % 4
            t = jnp.where(q == x, 24, tile_of(x, y, core, q))
            row = pl.ds(pl.multiple_of(8 * t, 8), 8)
            for e in range(0, EXPERTS, 2):
                first = RIGHT_ROWS + e * 8
                value = part[chip, first : first + 16, :].astype(F32)
                blocks[e, row, :] = value[:8]
                blocks[e + 1, row, :] = value[8:]
    for e in range(EXPERTS):
        for k in range(2):
            rows = slice(k * BLOCK, (k + 1) * BLOCK)
            out[e, k] = blocks[e, rows, :] * scale[2 * e + k : 2 * e + k + 1, :]


def finish_state(
    table, place, turned, second, near, far, low, panel, left, out, left_out, inverse, factor
):
    for part, core in ((near, place[2]), (far, 1 - place[2])):
        for chip in range(16):
            x, y = chip // 4, chip % 4
            value = part[chip, SECOND_ROWS + 96 : SECOND_ROWS + 112, :].astype(F32)
            row = pl.multiple_of(16 * chip + 8 * core, 8)
            inverse[pl.ds(row, 8), :] = value[:8] + value[8:]
            for s in range(2):
                for g in range(6):
                    first = s * SECOND_ROWS + 16 * g
                    value = part[chip, first : first + 16, :].astype(F32)
                    for i in range(2):
                        m = 2 * g + i
                        v = m % 3
                        q = v + int(v >= x)
                        t = 8 * (x - int(x > q)) + 2 * y
                        base = (4 * (m // 3) + q) * BLOCK + 8 * (t % 12)
                        row = pl.ds(pl.multiple_of(base + 8 * core, 8), 8)
                        factor[2 * s + t // 12, row, :] = value[8 * i : 8 * i + 8]
    some = table[SECOND + place[3]] < EXPERTS
    lows = [low[0], low[1]]
    for k in range(2):
        ortho = dot(panel[k], inverse[k * RANK : (k + 1) * RANK, :], ((1,), (1,)), HIGHEST)
        ortho = jnp.where(some, ortho, 0.0)
        left_out[k] = left[k]
        left_out[2 + k] = ortho * math.sqrt(D)
        lows.append((ortho * (-feedback)).astype(BF16))
    for s, state in enumerate((turned, second)):
        for k in range(2):
            i = 2 * s + k
            change = dot(lows[i], factor[i].astype(BF16), ((1,), (1,)))
            out[i] = (state[k].astype(F32) + change).astype(BF16)


def ring(shift):
    return [(i, (i + shift) % 4) for i in range(4)]


SHIFTS = (3, 1, 2)


def gather_slices(x):
    for axis in ("x", "y"):
        x = jnp.stack([x] + [lax.ppermute(x, axis, ring((4 - d) % 4)) for d in SHIFTS])
    x = x.reshape((16,) + x.shape[2:])
    return x, lax.ppermute(x, "c", SWAP)


def exchange(x, axis):
    return lax.all_to_all(x, axis, split_axis=0, concat_axis=0, tiled=True)


def shards(momentum, gradient, right_in, owners):
    sds = jax.ShapeDtypeStruct
    barrier = lax.optimization_barrier
    place = jnp.stack([lax.axis_index(a) for a in ("x", "y", "c", "z")]).astype(jnp.int32)
    slices, table = pl.pallas_call(
        slice_right,
        out_shape=(sds((16, 16, RANK), BF16), sds((TABLE,), jnp.int32)),
        in_specs=[SMEM, SMEM, VMEM],
        out_specs=(VMEM, SMEM),
        scratch_shapes=[pltpu.VMEM((EXPERTS + 1, 8, RANK), F32)],
    )(owners, place, right_in)
    slices = exchange(slices, "z")
    sent, late = call(
        place_state,
        (sds((16, 192, 128), BF16), sds((SECONDS, 192, 128), BF16)),
        specs=[SMEM, VMEM, VMEM],
    )(table, jnp.swapaxes(momentum, 2, 3), jnp.swapaxes(gradient, 2, 3))
    sent, slices = barrier((sent, slices))
    state = exchange(sent, "z")
    near, far = gather_slices(slices)
    right = call(
        join_right,
        sds((16, 384, RANK), BF16),
        [pltpu.VMEM((384, 512), BF16)],
        flops=800_000_000,
        specs=[SMEM, VMEM, VMEM],
    )(place, near, far)
    square = sds((PACKED, RANK), F32)
    two = sds((2, 128, RANK), F32)
    panel, keep, send = call(
        panels, (two, square, square), specs=[SMEM, VMEM, VMEM], flops=300_000_000
    )(place, state, right)
    late, send = barrier((late, send))
    seconds = lax.all_gather(late, "z")
    gram = keep + lax.ppermute(send, "c", SWAP)
    half = sds((16, 12, 8, RANK), F32)
    keep, send = call(
        weigh, (half, half), [pltpu.VMEM((4, 192, RANK), F32)], specs=[SMEM, VMEM, VMEM], flops=400_000_000
    )(place, state, panel)
    parts = keep + lax.ppermute(send, "c", SWAP)
    gram = exchange(jnp.broadcast_to(gram[None], (16, PACKED, RANK)), XY)
    parts, gram = barrier((parts, gram))
    parts = exchange(parts.reshape(16, 96, RANK), XY)
    gram = jnp.sum(gram, axis=0)
    inverse = call(
        functools.partial(invert, size=32),
        sds((2, RANK, RANK), F32),
        [pltpu.VMEM((2, RANK, 2 * RANK), F32)],
        specs=[SMEM, VMEM, VMEM],
        flops=2_000_000_000,
    )(place, gram, lax.ppermute(gram, "c", SWAP))
    mine = call(scale_factor, sds((112, RANK), BF16), specs=[SMEM, VMEM, VMEM], flops=100_000_000)(
        place, inverse, parts
    )
    turned = call(turn, sds((2, 128, HID), BF16), specs=[SMEM, SMEM, VMEM], flops=100_000_000)(
        table, place, state
    )
    left, low = call(
        orthonormal, (two, sds((2, 128, RANK), BF16)), specs=[SMEM, SMEM, VMEM, VMEM], flops=100_000_000
    )(table, place, panel, inverse)
    tiles = lax.all_gather(mine, "z")
    second_panel, second_turned = call(
        second_panels,
        (two, sds((2, 128, HID), BF16)),
        [pltpu.VMEM((16, 192, 128), BF16), pltpu.SemaphoreType.DMA],
        specs=[SMEM, SMEM, ANY, VMEM],
        flops=300_000_000,
    )(table, place, seconds, right)
    chosen = call(
        select,
        sds((16, ROWS, RANK), BF16),
        [pltpu.VMEM((ROWS, RANK), BF16)],
        specs=[SMEM, SMEM, VMEM, VMEM],
    )(table, place, mine, tiles)
    near = exchange(chosen, XY)
    near, turned, low, left, second_panel, second_turned = barrier(
        (near, turned, low, left, second_panel, second_turned)
    )
    far = lax.ppermute(near, "c", SWAP)
    right_out = call(
        finish_right, sds((EXPERTS, 2, BLOCK, RANK), F32), [pltpu.VMEM((EXPERTS, 200, RANK), F32)],
        specs=[SMEM, VMEM, VMEM], flops=1_000_000
    )(place, near, far)
    state_out, left_out = call(
        finish_state,
        (sds((4, 128, HID), BF16), sds((4, 128, RANK), F32)),
        [pltpu.VMEM((2 * RANK, RANK), F32), pltpu.VMEM((4, HID, RANK), F32)],
        specs=[SMEM, SMEM] + [VMEM] * 7,
        flops=1_200_000_000,
    )(table, place, turned, second_turned, near, far, low, second_panel, left)
    return (
        state_out.reshape(CAP, 2, 128, HID),
        left_out.reshape(CAP, 2, 128, RANK),
        right_out,
    )


def solution(mesh):
    fine = Mesh(mesh.devices.reshape(4, 4, 2, 16), ("x", "y", "c", "z"))
    return jax.shard_map(
        shards,
        mesh=fine,
        in_specs=(
            P(None, None, FSDP, "z"),
            P(None, None, FSDP, "z"),
            P(None, None, "z", None),
            P(),
        ),
        out_specs=(
            P("z", None, FSDP, None),
            P("z", None, FSDP, None),
            P(None, None, "z", None),
        ),
        check_vma=False,
    )
```

```python
import functools
import math

import jax
import jax.numpy as jnp
from jax import lax
from jax.experimental import pallas as pl
from jax.experimental.pallas import tpu as pltpu
from jax.sharding import Mesh
from jax.sharding import PartitionSpec as P

D = 4096
HID = 1536
CAP = 2
EXPERTS = 10
GROUPS = 16
BLOCK = 96
RANK = 128

ridge_term = 0.001
feedback = 0.1
epsilon = 1e-06

F32 = jnp.float32
BF16 = jnp.bfloat16
HIGHEST = lax.Precision.HIGHEST
XY = ("x", "y")
FSDP = ("x", "y", "c")
SWAP = [(0, 1), (1, 0)]
VMEM = pl.BlockSpec(memory_space=pltpu.VMEM)
SMEM = pl.BlockSpec(memory_space=pltpu.SMEM)
ANY = pl.BlockSpec(memory_space=pl.ANY)


def call(body, outs, scratch=(), flops=0, specs=None, n_in=0):
    return pl.pallas_call(
        body,
        out_shape=outs,
        in_specs=specs if specs is not None else [VMEM] * n_in,
        out_specs=jax.tree.map(lambda _: VMEM, outs),
        scratch_shapes=list(scratch),
        compiler_params=pltpu.CompilerParams(vmem_limit_bytes=16 * 1024 * 1024),
        cost_estimate=pl.CostEstimate(flops=flops, bytes_accessed=4_000_000, transcendentals=0),
    )


def dot(a, b, contract=((1,), (0,)), precision=None):
    return lax.dot_general(
        a, b, (contract, ((), ())), precision=precision, preferred_element_type=F32
    )


def iota(shape, dim):
    return lax.broadcasted_iota(jnp.int32, shape, dim)


COUNT, WORK, SECOND, HELPER, WHERE, FREE, SLOT, LIST, TABLE = 0, 17, 34, 51, 68, 80, 97, 114, 128
SECONDS = EXPERTS // 2
NONE = GROUPS


def fill_table(own, table):
    for g in range(GROUPS + 1):
        table[COUNT + g] = 0
        table[WORK + g] = EXPERTS
        table[SECOND + g] = EXPERTS
        table[HELPER + g] = 0
        table[SLOT + g] = 0
    for j in range(TABLE - LIST):
        table[LIST + j] = EXPERTS
    for e in range(EXPERTS):
        g = own[e]
        p = table[COUNT + g]
        table[COUNT + g] = p + 1
        table[WORK + jnp.where(p == 0, g, NONE)] = e
        table[SECOND + jnp.where(p == 0, NONE, g)] = e
    free = jnp.int32(0)
    for g in range(GROUPS):
        table[FREE + free] = g
        free = free + jnp.where(table[COUNT + g] == 0, 1, 0)
    used = jnp.int32(0)
    for e in range(EXPERTS):
        g = own[e]
        second = table[SECOND + g] == e
        h = table[FREE + used]
        table[WORK + jnp.where(second, h, NONE)] = e
        table[HELPER + jnp.where(second, g, NONE)] = h
        table[WHERE + e] = jnp.where(second, h, g)
        table[SLOT + jnp.where(second, g, NONE)] = used
        table[LIST + jnp.where(second, used, SECONDS)] = e
        used = used + jnp.where(second, 1, 0)


def slice_right(own, place, right, out, table, held):
    fill_table(own, table)
    f = place[0] * 8 + place[1] * 2 + place[2]
    pick = (iota((8, 192), 1) == iota((8, 192), 0) + 8 * f).astype(BF16)
    for e in range(EXPERTS):
        held[e] = dot(pick, right[e].reshape(192, RANK))
    held[EXPERTS] = jnp.zeros((8, RANK), F32)

    def group(g, _):
        pair = jnp.concatenate([held[table[WORK + g]], held[table[SECOND + g]]], axis=0)
        out[g] = pair.astype(BF16)
        return 0

    lax.fori_loop(0, GROUPS, group, 0)


def place_state(table, momentum, gradient, first, other):
    def put(out, i, e):
        @pl.when(e < EXPERTS)
        def _():
            total = momentum[e].astype(F32) + gradient[e].astype(F32)
            out[i] = total.astype(BF16).reshape(192, 128)

        @pl.when(e >= EXPERTS)
        def _():
            out[i] = jnp.zeros((192, 128), BF16)

    def slot(g, _):
        put(first, g, table[WORK + g])
        return 0

    lax.fori_loop(0, GROUPS, slot, 0)
    for j in range(SECONDS):
        put(other, j, table[LIST + j])


def offset(i):
    return jnp.where(i == 1, 3, jnp.where(i == 2, 1, jnp.where(i == 3, 2, 0)))


def join_matrix(place, core, relative, chips):
    col = iota((384, 16 * chips), 1)
    chip = col >> 4
    if relative:
        x = (place[0] + offset(chip & 3)) & 3
        y = (place[1] + offset(chip >> 2)) & 3
        chip = x * 4 + y
    f = chip * 2 + core
    target = ((col >> 3) & 1) * 192 + 8 * f + (col & 7)
    return ((iota((384, 16 * chips), 0) == target) & (f < 24)).astype(BF16)


def join_right(place, near, far, out, matrix):
    c = place[2]
    matrix[:, :256] = join_matrix(place, c, True, 16)
    matrix[:, 256:] = join_matrix(place, 1 - c, True, 16)

    def block(z, _):
        a = near[:, z].reshape(256, RANK)
        b = far[:, z].reshape(256, RANK)
        both = jnp.concatenate([a, b], axis=0)
        out[z] = dot(matrix[...], both).astype(BF16)
        return 0

    lax.fori_loop(0, GROUPS, block, 0, unroll=4)


def split3(value):
    high = value.astype(BF16)
    rest = value - high.astype(F32)
    middle = rest.astype(BF16)
    low = (rest - middle.astype(F32)).astype(BF16)
    return high, middle, low


def panel_of(block_of, right, kind, slot):
    def block(z, total):
        b = right[z, pl.ds(slot * 192 + kind * BLOCK, BLOCK), :]
        return total + dot(block_of(z), b, ((0,), (0,)))

    return lax.fori_loop(0, GROUPS, block, jnp.zeros((128, RANK), F32), unroll=4)


def panels(place, state, right, panel, keep, send):
    grams = []
    for k in range(2):
        rows = slice(k * BLOCK, (k + 1) * BLOCK)
        value = panel_of(lambda z: state[z, rows, :], right, k, 0)
        panel[k] = value
        grams.append(dot(value, value, ((0,), (0,)), HIGHEST))
    mine = place[2] == 0
    keep[...] = jnp.where(mine, grams[0], grams[1])
    send[...] = jnp.where(mine, grams[1], grams[0])


def unit():
    return (iota((128, 128), 0) == iota((128, 128), 1)).astype(BF16)


def second_panels(table, place, states, right, panel, turned, state, arrived):
    copy = pltpu.make_async_copy(states.at[:, table[SLOT + place[3]]], state, arrived)
    copy.start()
    some = table[SECOND + place[3]] < EXPERTS
    eye = jnp.where(some, unit(), jnp.zeros((128, 128), BF16))
    copy.wait()
    for k in range(2):
        rows = slice(k * BLOCK, (k + 1) * BLOCK)
        panel[k] = panel_of(lambda z: state[z, rows, :], right, k, 1)
        whole = state[:, rows, :].reshape(HID, 128)
        turned[k] = dot(eye, whole, ((1,), (1,))).astype(BF16)


def tile_of(x, y, core, q):
    return 8 * (x - jnp.where(x > q, 1, 0)) + 2 * y + core


def place_of(x, z):
    q = z & 3
    return 3 * (z >> 2) + q - jnp.where(q > x, 1, 0)


def row_kinds(place):
    m = iota((96, RANK), 0) >> 3
    v = m - 3 * ((m * 11) >> 5)
    q = v + jnp.where(v >= place[0], 1, 0)
    return jnp.where(tile_of(place[0], place[1], place[2], q) >= 12, 1, 0)


def weigh(place, state, panel, keep, send, rows):
    weights = [jnp.concatenate(split3(panel[k]), axis=1) for k in range(2)]

    def block(g, _):
        for q in range(4):
            z = 4 * g + q
            for k in range(2):
                value = dot(state[z, k * BLOCK : (k + 1) * BLOCK, :], weights[k])
                total = value[:, :128] + (value[:, 128:256] + value[:, 256:])
                rows[q, k * BLOCK : (k + 1) * BLOCK, :] = total
            for x in range(4):
                if x == q:
                    continue
                m = 3 * g + q - int(q > x)
                for y in range(4):
                    first = 64 * (x - int(x > q)) + 16 * y
                    near = pl.multiple_of(first + 8 * place[2], 8)
                    far = pl.multiple_of(first + 8 - 8 * place[2], 8)
                    keep[4 * x + y, m] = rows[q, pl.ds(near, 8), :]
                    send[4 * x + y, m] = rows[q, pl.ds(far, 8), :]
        return 0

    lax.fori_loop(0, 4, block, 0)


def eliminate(sets, k):
    row = iota((8, 256), 0)
    n = len(sets[0])
    for g in range(n):
        first = k + 8 * g
        columns = [
            [
                [jnp.broadcast_to(s[t][:, first + j : first + j + 1], (8, 256)) for t in range(g, n)]
                for j in range(8)
            ]
            for s in sets
        ]
        scales = [jnp.zeros((8, 256), F32) for _ in sets]
        for i in range(8):
            inverses = [
                lax.rsqrt(jnp.broadcast_to(c[i][0][i : i + 1, :], (8, 256))) for c in columns
            ]
            for m, (s, c) in enumerate(zip(sets, columns)):
                scales[m] = jnp.where(row == i, inverses[m], scales[m])
                square = inverses[m] * inverses[m]
                factors = [part * square for part in c[i]]
                factors[0] = jnp.where(row > i, factors[0], 0.0)
                for j in range(i + 1, 8):
                    line = jnp.broadcast_to(c[j][0][i : i + 1, :], (8, 256))
                    c[j] = [part - f * line for part, f in zip(c[j], factors)]
                line = jnp.broadcast_to(s[g][i : i + 1, :], (8, 256))
                for t in range(g, n):
                    s[t] = s[t] - factors[t - g] * line
        for m, s in enumerate(sets):
            s[g] = s[g] * scales[m]


def invert(place, near, far, out, work, *, size):
    n = RANK
    eye = (iota((n, n), 0) == iota((n, n), 1)).astype(F32)
    mine = place[2] == 0
    first, other = near[...], far[...]
    work[0, :, :n] = jnp.where(mine, first, other) + ridge_term * eye
    work[1, :, :n] = jnp.where(mine, other, first) + ridge_term * eye
    for m in range(2):
        work[m, :, n:] = eye
    lane = iota((size, n), 1)
    for k in range(0, n, size):
        sets = [[work[m, k + 8 * t : k + 8 * t + 8, :] for t in range(size // 8)] for m in range(2)]
        eliminate(sets, k)
        for m in range(2):
            b = jnp.concatenate(sets[m], axis=0)
            out[m, k : k + size, :] = b[:, n:]
            if k + size < n:
                left = jnp.where(lane >= k + size, b[:, :n], 0.0)
                change = dot(left, b, ((0,), (0,)), HIGHEST)
                work[m, k + size :, :] -= change[k + size :, :]


def scale_factor(place, inverse, parts, out):
    f = place[0] * 8 + place[1] * 2 + place[2]
    total = parts[0]
    for i in range(1, 16):
        total = total + parts[i]
    both = [dot(total, inverse[k], ((1,), (1,)), HIGHEST) for k in range(2)]
    out[:96] = jnp.where(row_kinds(place) == 0, both[0], both[1]).astype(BF16)
    half = jnp.where(f >= 16, 1, 0)
    start = pl.multiple_of(8 * f - 128 * half, 8)
    rows = inverse[half, pl.ds(start, 8), :]
    high = rows.astype(BF16).astype(F32)
    out[96:] = jnp.concatenate([high, rows - high], axis=0).astype(BF16)


def orthonormal(table, place, panel, inverse, left, low):
    owned = table[COUNT + place[3]] > 0
    for k in range(2):
        ortho = dot(panel[k], inverse[k], ((1,), (1,)), HIGHEST)
        ortho = jnp.where(owned, ortho, 0.0)
        left[k] = ortho * math.sqrt(D)
        low[k] = (ortho * (-feedback)).astype(BF16)


def turn(table, place, state, out):
    owned = table[COUNT + place[3]] > 0
    eye = jnp.where(owned, unit(), jnp.zeros((128, 128), BF16))
    for k in range(2):
        rows = state[:, k * BLOCK : (k + 1) * BLOCK, :].reshape(HID, 128)
        out[k] = dot(eye, rows, ((1,), (1,))).astype(BF16)


SECOND_ROWS, RIGHT_ROWS, SUM_ROWS, ROWS = 96, 208, 288, 320


def select(table, place, mine, tiles, out, packed):
    z = place[3]
    packed[:SECOND_ROWS, :] = mine[:96, :]
    packed[SECOND_ROWS:RIGHT_ROWS, :] = tiles[table[HELPER + z]]
    m = place_of(place[0], z)
    start = pl.multiple_of((m >> 1) * 16, 16)
    upper = (m & 1) == 1
    kinds = row_kinds(place)
    sums = []
    for e in range(0, EXPERTS, 2):
        pair = []
        for i in range(2):
            p = table[WHERE + e + i]
            value = tiles[p, pl.ds(start, 16), :].astype(F32)
            pair.append(jnp.where(upper, value[8:], value[:8]))
            whole = tiles[p, :96, :].astype(F32)
            square = whole * whole
            for k in range(2):
                sums.append(jnp.sum(jnp.where(kinds == k, square, 0.0), axis=0, keepdims=True))
        first = RIGHT_ROWS + e * 8
        packed[first : first + 16, :] = jnp.concatenate(pair, axis=0).astype(BF16)
    sums.append(jnp.zeros((ROWS - SUM_ROWS - 2 * EXPERTS, RANK), F32))
    packed[SUM_ROWS:, :] = jnp.concatenate(sums, axis=0).astype(BF16)
    value = packed[...]
    for i in range(16):
        out[i] = value


def finish_right(place, near, far, out, blocks):
    q = place[3] & 3
    parts = near[:, SUM_ROWS:, :].astype(F32) + far[:, SUM_ROWS:, :].astype(F32)
    scale = lax.rsqrt(jnp.sum(parts, axis=0) * (1.0 / HID) + epsilon)
    for part, core in ((near, place[2]), (far, 1 - place[2])):
        for chip in range(16):
            x, y = chip // 4, chip % 4
            t = jnp.where(q == x, 24, tile_of(x, y, core, q))
            row = pl.ds(pl.multiple_of(8 * t, 8), 8)
            for e in range(0, EXPERTS, 2):
                first = RIGHT_ROWS + e * 8
                value = part[chip, first : first + 16, :].astype(F32)
                blocks[e, row, :] = value[:8]
                blocks[e + 1, row, :] = value[8:]
    for e in range(EXPERTS):
        for k in range(2):
            rows = slice(k * BLOCK, (k + 1) * BLOCK)
            out[e, k] = blocks[e, rows, :] * scale[2 * e + k : 2 * e + k + 1, :]


def finish(
    table, place, turned, second, near, far, low, panel, left,
    out, left_out, right_out, inverse, factor, blocks,
):
    finish_right(place, near, far, right_out, blocks)
    for part, core in ((near, place[2]), (far, 1 - place[2])):
        for chip in range(16):
            x, y = chip // 4, chip % 4
            value = part[chip, SECOND_ROWS + 96 : SECOND_ROWS + 112, :].astype(F32)
            row = pl.multiple_of(16 * chip + 8 * core, 8)
            inverse[pl.ds(row, 8), :] = value[:8] + value[8:]
            for s in range(2):
                for g in range(6):
                    first = s * SECOND_ROWS + 16 * g
                    value = part[chip, first : first + 16, :].astype(F32)
                    for i in range(2):
                        m = 2 * g + i
                        v = m % 3
                        q = v + int(v >= x)
                        t = 8 * (x - int(x > q)) + 2 * y
                        base = (4 * (m // 3) + q) * BLOCK + 8 * (t % 12)
                        row = pl.ds(pl.multiple_of(base + 8 * core, 8), 8)
                        factor[2 * s + t // 12, row, :] = value[8 * i : 8 * i + 8]
    some = table[SECOND + place[3]] < EXPERTS
    lows = [low[0], low[1]]
    for k in range(2):
        ortho = dot(panel[k], inverse[k * RANK : (k + 1) * RANK, :], ((1,), (1,)), HIGHEST)
        ortho = jnp.where(some, ortho, 0.0)
        left_out[k] = left[k]
        left_out[2 + k] = ortho * math.sqrt(D)
        lows.append((ortho * (-feedback)).astype(BF16))
    for s, state in enumerate((turned, second)):
        for k in range(2):
            i = 2 * s + k
            change = dot(lows[i], factor[i].astype(BF16), ((1,), (1,)))
            out[i] = (state[k].astype(F32) + change).astype(BF16)


def ring(shift):
    return [(i, (i + shift) % 4) for i in range(4)]


SHIFTS = (3, 1, 2)


def gather_slices(x):
    for axis in ("x", "y"):
        x = jnp.stack([x] + [lax.ppermute(x, axis, ring((4 - d) % 4)) for d in SHIFTS])
    x = x.reshape((16,) + x.shape[2:])
    return x, lax.ppermute(x, "c", SWAP)


def exchange(x, axis):
    return lax.all_to_all(x, axis, split_axis=0, concat_axis=0, tiled=True)


def shards(momentum, gradient, right_in, owners):
    sds = jax.ShapeDtypeStruct
    barrier = lax.optimization_barrier
    place = jnp.stack([lax.axis_index(a) for a in ("x", "y", "c", "z")]).astype(jnp.int32)
    slices, table = pl.pallas_call(
        slice_right,
        out_shape=(sds((16, 16, RANK), BF16), sds((TABLE,), jnp.int32)),
        in_specs=[SMEM, SMEM, VMEM],
        out_specs=(VMEM, SMEM),
        scratch_shapes=[pltpu.VMEM((EXPERTS + 1, 8, RANK), F32)],
    )(owners, place, right_in)
    slices = exchange(slices, "z")
    sent, late = call(
        place_state,
        (sds((16, 192, 128), BF16), sds((SECONDS, 192, 128), BF16)),
        specs=[SMEM, VMEM, VMEM],
    )(table, jnp.swapaxes(momentum, 2, 3), jnp.swapaxes(gradient, 2, 3))
    sent, slices = barrier((sent, slices))
    state = exchange(sent, "z")
    near, far = gather_slices(slices)
    right = call(
        join_right,
        sds((16, 384, RANK), BF16),
        [pltpu.VMEM((384, 512), BF16)],
        flops=800_000_000,
        specs=[SMEM, VMEM, VMEM],
    )(place, near, far)
    square = sds((RANK, RANK), F32)
    two = sds((2, 128, RANK), F32)
    panel, keep, send = call(
        panels, (two, square, square), specs=[SMEM, VMEM, VMEM], flops=300_000_000
    )(place, state, right)
    late, send = barrier((late, send))
    seconds = lax.all_gather(late, "z")
    gram = keep + lax.ppermute(send, "c", SWAP)
    half = sds((16, 12, 8, RANK), F32)
    keep, send = call(
        weigh, (half, half), [pltpu.VMEM((4, 192, RANK), F32)], specs=[SMEM, VMEM, VMEM], flops=400_000_000
    )(place, state, panel)
    parts = keep + lax.ppermute(send, "c", SWAP)
    gram = exchange(jnp.broadcast_to(gram[None], (16, RANK, RANK)), XY)
    parts, gram = barrier((parts, gram))
    parts = exchange(parts.reshape(16, 96, RANK), XY)
    gram = jnp.sum(gram, axis=0)
    inverse = call(
        functools.partial(invert, size=32),
        sds((2, RANK, RANK), F32),
        [pltpu.VMEM((2, RANK, 2 * RANK), F32)],
        specs=[SMEM, VMEM, VMEM],
        flops=2_000_000_000,
    )(place, gram, lax.ppermute(gram, "c", SWAP))
    mine = call(scale_factor, sds((112, RANK), BF16), specs=[SMEM, VMEM, VMEM], flops=100_000_000)(
        place, inverse, parts
    )
    turned = call(turn, sds((2, 128, HID), BF16), specs=[SMEM, SMEM, VMEM], flops=100_000_000)(
        table, place, state
    )
    left, low = call(
        orthonormal, (two, sds((2, 128, RANK), BF16)), specs=[SMEM, SMEM, VMEM, VMEM], flops=100_000_000
    )(table, place, panel, inverse)
    tiles = lax.all_gather(mine, "z")
    second_panel, second_turned = call(
        second_panels,
        (two, sds((2, 128, HID), BF16)),
        [pltpu.VMEM((16, 192, 128), BF16), pltpu.SemaphoreType.DMA],
        specs=[SMEM, SMEM, ANY, VMEM],
        flops=300_000_000,
    )(table, place, seconds, right)
    chosen = call(
        select,
        sds((16, ROWS, RANK), BF16),
        [pltpu.VMEM((ROWS, RANK), BF16)],
        specs=[SMEM, SMEM, VMEM, VMEM],
    )(table, place, mine, tiles)
    near = exchange(chosen, XY)
    near, turned, low, left, second_panel, second_turned = barrier(
        (near, turned, low, left, second_panel, second_turned)
    )
    far = lax.ppermute(near, "c", SWAP)
    state_out, left_out, right_out = call(
        finish,
        (
            sds((4, 128, HID), BF16),
            sds((4, 128, RANK), F32),
            sds((EXPERTS, 2, BLOCK, RANK), F32),
        ),
        [
            pltpu.VMEM((2 * RANK, RANK), F32),
            pltpu.VMEM((4, HID, RANK), F32),
            pltpu.VMEM((EXPERTS, 200, RANK), F32),
        ],
        specs=[SMEM, SMEM] + [VMEM] * 7,
        flops=1_200_000_000,
    )(table, place, turned, second_turned, near, far, low, second_panel, left)
    return (
        state_out.reshape(CAP, 2, 128, HID),
        left_out.reshape(CAP, 2, 128, RANK),
        right_out,
    )


def solution(mesh):
    fine = Mesh(mesh.devices.reshape(4, 4, 2, 16), ("x", "y", "c", "z"))
    return jax.shard_map(
        shards,
        mesh=fine,
        in_specs=(
            P(None, None, FSDP, "z"),
            P(None, None, FSDP, "z"),
            P(None, None, "z", None),
            P(),
        ),
        out_specs=(
            P("z", None, FSDP, None),
            P("z", None, FSDP, None),
            P(None, None, "z", None),
        ),
        check_vma=False,
    )
```

```python
import functools
import math

import jax
import jax.numpy as jnp
from jax import lax
from jax.experimental import pallas as pl
from jax.experimental.pallas import tpu as pltpu
from jax.sharding import Mesh
from jax.sharding import PartitionSpec as P

D = 4096
HID = 1536
CAP = 2
EXPERTS = 10
GROUPS = 16
BLOCK = 96
RANK = 128

ridge_term = 0.001
feedback = 0.1
epsilon = 1e-06

F32 = jnp.float32
BF16 = jnp.bfloat16
HIGHEST = lax.Precision.HIGHEST
XY = ("x", "y")
FSDP = ("x", "y", "c")
SWAP = [(0, 1), (1, 0)]
VMEM = pl.BlockSpec(memory_space=pltpu.VMEM)
SMEM = pl.BlockSpec(memory_space=pltpu.SMEM)
ANY = pl.BlockSpec(memory_space=pl.ANY)


def call(body, outs, scratch=(), flops=0, specs=None, n_in=0):
    return pl.pallas_call(
        body,
        out_shape=outs,
        in_specs=specs if specs is not None else [VMEM] * n_in,
        out_specs=jax.tree.map(lambda _: VMEM, outs),
        scratch_shapes=list(scratch),
        compiler_params=pltpu.CompilerParams(vmem_limit_bytes=16 * 1024 * 1024),
        cost_estimate=pl.CostEstimate(flops=flops, bytes_accessed=4_000_000, transcendentals=0),
    )


def dot(a, b, contract=((1,), (0,)), precision=None):
    return lax.dot_general(
        a, b, (contract, ((), ())), precision=precision, preferred_element_type=F32
    )


def iota(shape, dim):
    return lax.broadcasted_iota(jnp.int32, shape, dim)


COUNT, WORK, SECOND, HELPER, WHERE, FREE, SLOT, LIST, TABLE = 0, 17, 34, 51, 68, 80, 97, 114, 128
SECONDS = EXPERTS // 2
NONE = GROUPS


def fill_table(own, table):
    for g in range(GROUPS + 1):
        table[COUNT + g] = 0
        table[WORK + g] = EXPERTS
        table[SECOND + g] = EXPERTS
        table[HELPER + g] = 0
        table[SLOT + g] = 0
    for j in range(TABLE - LIST):
        table[LIST + j] = EXPERTS
    for e in range(EXPERTS):
        g = own[e]
        p = table[COUNT + g]
        table[COUNT + g] = p + 1
        table[WORK + jnp.where(p == 0, g, NONE)] = e
        table[SECOND + jnp.where(p == 0, NONE, g)] = e
    free = jnp.int32(0)
    for g in range(GROUPS):
        table[FREE + free] = g
        free = free + jnp.where(table[COUNT + g] == 0, 1, 0)
    used = jnp.int32(0)
    for e in range(EXPERTS):
        g = own[e]
        second = table[SECOND + g] == e
        h = table[FREE + used]
        table[WORK + jnp.where(second, h, NONE)] = e
        table[HELPER + jnp.where(second, g, NONE)] = h
        table[WHERE + e] = jnp.where(second, h, g)
        table[SLOT + jnp.where(second, g, NONE)] = used
        table[LIST + jnp.where(second, used, SECONDS)] = e
        used = used + jnp.where(second, 1, 0)


def slice_right(own, place, right, out, table, held):
    fill_table(own, table)
    f = place[0] * 8 + place[1] * 2 + place[2]
    pick = (iota((8, 192), 1) == iota((8, 192), 0) + 8 * f).astype(BF16)
    for e in range(EXPERTS):
        held[e] = dot(pick, right[e].reshape(192, RANK))
    held[EXPERTS] = jnp.zeros((8, RANK), F32)

    def group(g, _):
        pair = jnp.concatenate([held[table[WORK + g]], held[table[SECOND + g]]], axis=0)
        out[g] = pair.astype(BF16)
        return 0

    lax.fori_loop(0, GROUPS, group, 0)


def place_state(table, momentum, gradient, first, other):
    def put(out, i, e):
        @pl.when(e < EXPERTS)
        def _():
            total = momentum[e].astype(F32) + gradient[e].astype(F32)
            out[i] = total.astype(BF16).reshape(192, 128)

        @pl.when(e >= EXPERTS)
        def _():
            out[i] = jnp.zeros((192, 128), BF16)

    def slot(g, _):
        put(first, g, table[WORK + g])
        return 0

    lax.fori_loop(0, GROUPS, slot, 0)
    for j in range(SECONDS):
        put(other, j, table[LIST + j])


def offset(i):
    return jnp.where(i == 1, 3, jnp.where(i == 2, 1, jnp.where(i == 3, 2, 0)))


def join_matrix(place, core, relative, chips):
    col = iota((384, 16 * chips), 1)
    chip = col >> 4
    if relative:
        x = (place[0] + offset(chip & 3)) & 3
        y = (place[1] + offset(chip >> 2)) & 3
        chip = x * 4 + y
    f = chip * 2 + core
    target = ((col >> 3) & 1) * 192 + 8 * f + (col & 7)
    return ((iota((384, 16 * chips), 0) == target) & (f < 24)).astype(BF16)


def join_right(place, near, far, out, matrix):
    c = place[2]
    matrix[:, :256] = join_matrix(place, c, True, 16)
    matrix[:, 256:] = join_matrix(place, 1 - c, True, 16)

    def block(z, _):
        a = near[:, z].reshape(256, RANK)
        b = far[:, z].reshape(256, RANK)
        both = jnp.concatenate([a, b], axis=0)
        out[z] = dot(matrix[...], both).astype(BF16)
        return 0

    lax.fori_loop(0, GROUPS, block, 0, unroll=4)


def split3(value):
    high = value.astype(BF16)
    rest = value - high.astype(F32)
    middle = rest.astype(BF16)
    low = (rest - middle.astype(F32)).astype(BF16)
    return high, middle, low


def panel_of(block_of, right, kind, slot):
    def block(z, total):
        b = right[z, pl.ds(slot * 192 + kind * BLOCK, BLOCK), :]
        return total + dot(block_of(z), b, ((0,), (0,)))

    return lax.fori_loop(0, GROUPS, block, jnp.zeros((128, RANK), F32), unroll=4)


PACKED = 80


def pack(gram):
    middle = jnp.concatenate([gram[96:, 96:], gram[32:64, 32:]], axis=1)
    last = jnp.concatenate([gram[80:96, 64:], gram[64:80, 64:]], axis=1)
    return jnp.concatenate([gram[:32], middle, last], axis=0)


def unpack(packed):
    middle, last = packed[32:64], packed[64:]
    other = jnp.concatenate([last[:, 64:], last[:, :64]], axis=1)
    corner = jnp.concatenate([middle[:, 32:], middle[:, :32]], axis=1)
    return jnp.concatenate([packed[:32], middle, last, other, corner], axis=0)


def panels(place, state, right, panel, keep, send):
    grams = []
    for k in range(2):
        rows = slice(k * BLOCK, (k + 1) * BLOCK)
        value = panel_of(lambda z: state[z, rows, :], right, k, 0)
        panel[k] = value
        grams.append(pack(dot(value, value, ((0,), (0,)), HIGHEST)))
    mine = place[2] == 0
    keep[...] = jnp.where(mine, grams[0], grams[1])
    send[...] = jnp.where(mine, grams[1], grams[0])


def unit():
    return (iota((128, 128), 0) == iota((128, 128), 1)).astype(BF16)


def second_panels(table, place, states, right, panel, turned, state, arrived):
    copy = pltpu.make_async_copy(states.at[:, table[SLOT + place[3]]], state, arrived)
    copy.start()
    some = table[SECOND + place[3]] < EXPERTS
    eye = jnp.where(some, unit(), jnp.zeros((128, 128), BF16))
    copy.wait()
    for k in range(2):
        rows = slice(k * BLOCK, (k + 1) * BLOCK)
        panel[k] = panel_of(lambda z: state[z, rows, :], right, k, 1)
        whole = state[:, rows, :].reshape(HID, 128)
        turned[k] = dot(eye, whole, ((1,), (1,))).astype(BF16)


def tile_of(x, y, core, q):
    return 8 * (x - jnp.where(x > q, 1, 0)) + 2 * y + core


def place_of(x, z):
    q = z & 3
    return 3 * (z >> 2) + q - jnp.where(q > x, 1, 0)


def row_kinds(place):
    m = iota((96, RANK), 0) >> 3
    v = m - 3 * ((m * 11) >> 5)
    q = v + jnp.where(v >= place[0], 1, 0)
    return jnp.where(tile_of(place[0], place[1], place[2], q) >= 12, 1, 0)


def weigh(place, state, panel, _, keep, send, rows):
    weights = [jnp.concatenate(split3(panel[k]), axis=1) for k in range(2)]

    def block(g, _):
        for q in range(4):
            z = 4 * g + q
            for k in range(2):
                value = dot(state[z, k * BLOCK : (k + 1) * BLOCK, :], weights[k])
                total = value[:, :128] + (value[:, 128:256] + value[:, 256:])
                rows[q, k * BLOCK : (k + 1) * BLOCK, :] = total
            for x in range(4):
                if x == q:
                    continue
                m = 3 * g + q - int(q > x)
                for y in range(4):
                    first = 64 * (x - int(x > q)) + 16 * y
                    near = pl.multiple_of(first + 8 * place[2], 8)
                    far = pl.multiple_of(first + 8 - 8 * place[2], 8)
                    keep[4 * x + y, m] = rows[q, pl.ds(near, 8), :]
                    send[4 * x + y, m] = rows[q, pl.ds(far, 8), :]
        return 0

    lax.fori_loop(0, 4, block, 0)


def eliminate(sets, k):
    row = iota((8, 256), 0)
    n = len(sets[0])
    for g in range(n):
        first = k + 8 * g
        columns = [
            [
                [jnp.broadcast_to(s[t][:, first + j : first + j + 1], (8, 256)) for t in range(g, n)]
                for j in range(8)
            ]
            for s in sets
        ]
        scales = [jnp.zeros((8, 256), F32) for _ in sets]
        for i in range(8):
            inverses = [
                lax.rsqrt(jnp.broadcast_to(c[i][0][i : i + 1, :], (8, 256))) for c in columns
            ]
            for m, (s, c) in enumerate(zip(sets, columns)):
                scales[m] = jnp.where(row == i, inverses[m], scales[m])
                square = inverses[m] * inverses[m]
                factors = [part * square for part in c[i]]
                factors[0] = jnp.where(row > i, factors[0], 0.0)
                for j in range(i + 1, 8):
                    line = jnp.broadcast_to(c[j][0][i : i + 1, :], (8, 256))
                    c[j] = [part - f * line for part, f in zip(c[j], factors)]
                line = jnp.broadcast_to(s[g][i : i + 1, :], (8, 256))
                for t in range(g, n):
                    s[t] = s[t] - factors[t - g] * line
        for m, s in enumerate(sets):
            s[g] = s[g] * scales[m]


def invert(place, near, far, out, work, *, size):
    n = RANK
    eye = (iota((n, n), 0) == iota((n, n), 1)).astype(F32)
    mine = place[2] == 0
    first, other = unpack(near[...]), unpack(far[...])
    work[0, :, :n] = jnp.where(mine, first, other) + ridge_term * eye
    work[1, :, :n] = jnp.where(mine, other, first) + ridge_term * eye
    for m in range(2):
        work[m, :, n:] = eye
    lane = iota((size, n), 1)
    for k in range(0, n, size):
        sets = [[work[m, k + 8 * t : k + 8 * t + 8, :] for t in range(size // 8)] for m in range(2)]
        eliminate(sets, k)
        for m in range(2):
            b = jnp.concatenate(sets[m], axis=0)
            out[m, k : k + size, :] = b[:, n:]
            if k + size < n:
                left = jnp.where(lane >= k + size, b[:, :n], 0.0)
                change = dot(left, b, ((0,), (0,)), HIGHEST)
                work[m, k + size :, :] -= change[k + size :, :]


def scale_factor(place, inverse, parts, out):
    f = place[0] * 8 + place[1] * 2 + place[2]
    total = parts[0]
    for i in range(1, 16):
        total = total + parts[i]
    both = [dot(total, inverse[k], ((1,), (1,)), HIGHEST) for k in range(2)]
    out[:96] = jnp.where(row_kinds(place) == 0, both[0], both[1]).astype(BF16)
    half = jnp.where(f >= 16, 1, 0)
    start = pl.multiple_of(8 * f - 128 * half, 8)
    rows = inverse[half, pl.ds(start, 8), :]
    high = rows.astype(BF16).astype(F32)
    out[96:] = jnp.concatenate([high, rows - high], axis=0).astype(BF16)


def orthonormal(table, place, panel, inverse, left, low):
    owned = table[COUNT + place[3]] > 0
    for k in range(2):
        ortho = dot(panel[k], inverse[k], ((1,), (1,)), HIGHEST)
        ortho = jnp.where(owned, ortho, 0.0)
        left[k] = ortho * math.sqrt(D)
        low[k] = (ortho * (-feedback)).astype(BF16)


def turn(table, place, state, out):
    owned = table[COUNT + place[3]] > 0
    eye = jnp.where(owned, unit(), jnp.zeros((128, 128), BF16))
    for k in range(2):
        rows = state[:, k * BLOCK : (k + 1) * BLOCK, :].reshape(HID, 128)
        out[k] = dot(eye, rows, ((1,), (1,))).astype(BF16)


SECOND_ROWS, RIGHT_ROWS, SUM_ROWS, ROWS = 96, 208, 288, 320


def select(table, place, mine, tiles, out, packed):
    z = place[3]
    packed[:SECOND_ROWS, :] = mine[:96, :]
    packed[SECOND_ROWS:RIGHT_ROWS, :] = tiles[table[HELPER + z]]
    m = place_of(place[0], z)
    start = pl.multiple_of((m >> 1) * 16, 16)
    upper = (m & 1) == 1
    kinds = row_kinds(place)
    sums = []
    for e in range(0, EXPERTS, 2):
        pair = []
        for i in range(2):
            p = table[WHERE + e + i]
            value = tiles[p, pl.ds(start, 16), :].astype(F32)
            pair.append(jnp.where(upper, value[8:], value[:8]))
            whole = tiles[p, :96, :].astype(F32)
            square = whole * whole
            for k in range(2):
                sums.append(jnp.sum(jnp.where(kinds == k, square, 0.0), axis=0, keepdims=True))
        first = RIGHT_ROWS + e * 8
        packed[first : first + 16, :] = jnp.concatenate(pair, axis=0).astype(BF16)
    sums.append(jnp.zeros((ROWS - SUM_ROWS - 2 * EXPERTS, RANK), F32))
    packed[SUM_ROWS:, :] = jnp.concatenate(sums, axis=0).astype(BF16)
    value = packed[...]
    for i in range(16):
        out[i] = value


def finish_right(place, near, far, out, blocks):
    q = place[3] & 3
    parts = near[:, SUM_ROWS:, :].astype(F32) + far[:, SUM_ROWS:, :].astype(F32)
    scale = lax.rsqrt(jnp.sum(parts, axis=0) * (1.0 / HID) + epsilon)
    for part, core in ((near, place[2]), (far, 1 - place[2])):
        for chip in range(16):
            x, y = chip // 4, chip % 4
            t = jnp.where(q == x, 24, tile_of(x, y, core, q))
            row = pl.ds(pl.multiple_of(8 * t, 8), 8)
            for e in range(0, EXPERTS, 2):
                first = RIGHT_ROWS + e * 8
                value = part[chip, first : first + 16, :].astype(F32)
                blocks[e, row, :] = value[:8]
                blocks[e + 1, row, :] = value[8:]
    for e in range(EXPERTS):
        for k in range(2):
            rows = slice(k * BLOCK, (k + 1) * BLOCK)
            out[e, k] = blocks[e, rows, :] * scale[2 * e + k : 2 * e + k + 1, :]


def finish(
    table, place, turned, second, near, far, low, panel, left,
    out, left_out, right_out, inverse, factor, blocks,
):
    finish_right(place, near, far, right_out, blocks)
    for part, core in ((near, place[2]), (far, 1 - place[2])):
        for chip in range(16):
            x, y = chip // 4, chip % 4
            value = part[chip, SECOND_ROWS + 96 : SECOND_ROWS + 112, :].astype(F32)
            row = pl.multiple_of(16 * chip + 8 * core, 8)
            inverse[pl.ds(row, 8), :] = value[:8] + value[8:]
            for s in range(2):
                for g in range(6):
                    first = s * SECOND_ROWS + 16 * g
                    value = part[chip, first : first + 16, :].astype(F32)
                    for i in range(2):
                        m = 2 * g + i
                        v = m % 3
                        q = v + int(v >= x)
                        t = 8 * (x - int(x > q)) + 2 * y
                        base = (4 * (m // 3) + q) * BLOCK + 8 * (t % 12)
                        row = pl.ds(pl.multiple_of(base + 8 * core, 8), 8)
                        factor[2 * s + t // 12, row, :] = value[8 * i : 8 * i + 8]
    some = table[SECOND + place[3]] < EXPERTS
    lows = [low[0], low[1]]
    for k in range(2):
        ortho = dot(panel[k], inverse[k * RANK : (k + 1) * RANK, :], ((1,), (1,)), HIGHEST)
        ortho = jnp.where(some, ortho, 0.0)
        left_out[k] = left[k]
        left_out[2 + k] = ortho * math.sqrt(D)
        lows.append((ortho * (-feedback)).astype(BF16))
    for s, state in enumerate((turned, second)):
        for k in range(2):
            i = 2 * s + k
            change = dot(lows[i], factor[i].astype(BF16), ((1,), (1,)))
            out[i] = (state[k].astype(F32) + change).astype(BF16)


def ring(shift):
    return [(i, (i + shift) % 4) for i in range(4)]


SHIFTS = (3, 1, 2)


def gather_slices(x):
    for axis in ("x", "y"):
        x = jnp.stack([x] + [lax.ppermute(x, axis, ring((4 - d) % 4)) for d in SHIFTS])
    x = x.reshape((16,) + x.shape[2:])
    return x, lax.ppermute(x, "c", SWAP)


def exchange(x, axis):
    return lax.all_to_all(x, axis, split_axis=0, concat_axis=0, tiled=True)


def shards(momentum, gradient, right_in, owners):
    sds = jax.ShapeDtypeStruct
    barrier = lax.optimization_barrier
    place = jnp.stack([lax.axis_index(a) for a in ("x", "y", "c", "z")]).astype(jnp.int32)
    slices, table = pl.pallas_call(
        slice_right,
        out_shape=(sds((16, 16, RANK), BF16), sds((TABLE,), jnp.int32)),
        in_specs=[SMEM, SMEM, VMEM],
        out_specs=(VMEM, SMEM),
        scratch_shapes=[pltpu.VMEM((EXPERTS + 1, 8, RANK), F32)],
    )(owners, place, right_in)
    slices = exchange(slices, "z")
    sent, late = call(
        place_state,
        (sds((16, 192, 128), BF16), sds((SECONDS, 192, 128), BF16)),
        specs=[SMEM, VMEM, VMEM],
    )(table, jnp.swapaxes(momentum, 2, 3), jnp.swapaxes(gradient, 2, 3))
    sent, slices = barrier((sent, slices))
    state = exchange(sent, "z")
    near, far = gather_slices(slices)
    right = call(
        join_right,
        sds((16, 384, RANK), BF16),
        [pltpu.VMEM((384, 512), BF16)],
        flops=800_000_000,
        specs=[SMEM, VMEM, VMEM],
    )(place, near, far)
    square = sds((PACKED, RANK), F32)
    two = sds((2, 128, RANK), F32)
    panel, keep, send = call(
        panels, (two, square, square), specs=[SMEM, VMEM, VMEM], flops=300_000_000
    )(place, state, right)
    late, send = barrier((late, send))
    seconds = lax.all_gather(late, "z")
    gram = keep + lax.ppermute(send, "c", SWAP)
    half = sds((16, 12, 8, RANK), F32)
    keep, send = call(
        weigh, (half, half), [pltpu.VMEM((4, 192, RANK), F32)], specs=[SMEM, VMEM, VMEM, ANY], flops=400_000_000
    )(place, state, panel, gram)
    parts = keep + lax.ppermute(send, "c", SWAP)
    gram = exchange(jnp.broadcast_to(gram[None], (16, PACKED, RANK)), XY)
    parts, gram = barrier((parts, gram))
    parts = exchange(parts.reshape(16, 96, RANK), XY)
    gram = jnp.sum(gram, axis=0)
    inverse = call(
        functools.partial(invert, size=32),
        sds((2, RANK, RANK), F32),
        [pltpu.VMEM((2, RANK, 2 * RANK), F32)],
        specs=[SMEM, VMEM, VMEM],
        flops=2_000_000_000,
    )(place, gram, lax.ppermute(gram, "c", SWAP))
    mine = call(scale_factor, sds((112, RANK), BF16), specs=[SMEM, VMEM, VMEM], flops=100_000_000)(
        place, inverse, parts
    )
    turned = call(turn, sds((2, 128, HID), BF16), specs=[SMEM, SMEM, VMEM], flops=100_000_000)(
        table, place, state
    )
    left, low = call(
        orthonormal, (two, sds((2, 128, RANK), BF16)), specs=[SMEM, SMEM, VMEM, VMEM], flops=100_000_000
    )(table, place, panel, inverse)
    tiles = lax.all_gather(mine, "z")
    second_panel, second_turned = call(
        second_panels,
        (two, sds((2, 128, HID), BF16)),
        [pltpu.VMEM((16, 192, 128), BF16), pltpu.SemaphoreType.DMA],
        specs=[SMEM, SMEM, ANY, VMEM],
        flops=300_000_000,
    )(table, place, seconds, right)
    chosen = call(
        select,
        sds((16, ROWS, RANK), BF16),
        [pltpu.VMEM((ROWS, RANK), BF16)],
        specs=[SMEM, SMEM, VMEM, VMEM],
    )(table, place, mine, tiles)
    near = exchange(chosen, XY)
    near, turned, low, left, second_panel, second_turned = barrier(
        (near, turned, low, left, second_panel, second_turned)
    )
    far = lax.ppermute(near, "c", SWAP)
    state_out, left_out, right_out = call(
        finish,
        (
            sds((4, 128, HID), BF16),
            sds((4, 128, RANK), F32),
            sds((EXPERTS, 2, BLOCK, RANK), F32),
        ),
        [
            pltpu.VMEM((2 * RANK, RANK), F32),
            pltpu.VMEM((4, HID, RANK), F32),
            pltpu.VMEM((EXPERTS, 200, RANK), F32),
        ],
        specs=[SMEM, SMEM] + [VMEM] * 7,
        flops=1_200_000_000,
    )(table, place, turned, second_turned, near, far, low, second_panel, left)
    return (
        state_out.reshape(CAP, 2, 128, HID),
        left_out.reshape(CAP, 2, 128, RANK),
        right_out,
    )


def solution(mesh):
    fine = Mesh(mesh.devices.reshape(4, 4, 2, 16), ("x", "y", "c", "z"))
    return jax.shard_map(
        shards,
        mesh=fine,
        in_specs=(
            P(None, None, FSDP, "z"),
            P(None, None, FSDP, "z"),
            P(None, None, "z", None),
            P(),
        ),
        out_specs=(
            P("z", None, FSDP, None),
            P("z", None, FSDP, None),
            P(None, None, "z", None),
        ),
        check_vma=False,
    )
```
